32 devices in a mesh: pack: 8 (over z, y), row: 4 (over x, core).
Axes of the slice: x: 2, y: 2, z: 4, core: 2. Of those that a mesh axis runs over, the one named last changes fastest.
Arguments:
- tokens: float32 [16384, 256], P(('pack', 'row')), may hold values from -6 to 6
- cotangent: float32 [16384, 256], P(('pack', 'row')), may hold values from -6 to 6
- segment_ids: int32 [16384], P(('pack', 'row')), may hold values from 0 to 5, as said below
- padding: int32 [16384], P(('pack', 'row')), may hold values from 0 to 1, as said below
- master: float32 [10240, 128], P('pack')
- moment_first: float32 [10240, 128], P('pack')
- moment_second: float32 [10240, 128], P('pack'), as said below
- stat_left: float32 [10240, 128], P('pack'), as said below
- stat_right: float32 [10240, 128], P('pack'), as said below
- basis_left: float32 [10240, 128], P('pack'), as said below
- basis_right: float32 [10240, 128], P('pack'), as said below
- vec_params: float32 [4096], replicated
- vec_first: float32 [4096], replicated, may hold values from -40 to 40
- vec_second: float32 [4096], replicated, may hold values from 212.992 to 868.352
Outputs:
- layer_out: float32 [16384, 256], P(('pack', 'row'))
- input_grad: float32 [16384, 256], P(('pack', 'row'))
- first_new: float32 [10240, 128], P('pack')
- second_new: float32 [10240, 128], P('pack')
- master_new: float32 [10240, 128], P('pack')
- master_copy: bfloat16 [10240, 128], P('pack')
- left_new: float32 [10240, 128], P('pack')
- right_new: float32 [10240, 128], P('pack')
- basis_left_new: float32 [10240, 128], P('pack')
- basis_right_new: float32 [10240, 128], P('pack')
- vec_new: float32 [4096], replicated
- vec_first_new: float32 [4096], replicated
- vec_second_new: float32 [4096], replicated
The draws below stay inside these ranges and needn't reach their ends.
Inputs may be any that keep to these rules, and one draw needn't show every extreme that they name: `segment_ids`: within each pack of 2048 tokens the ids start at 0 and never fall. The first token of every image is not padding. `basis_left`: each block of 128 rows is an orthogonal matrix. `basis_right`: each block of 128 rows is an orthogonal matrix. `stat_left`: each block of 128 rows is symmetric positive definite. `stat_right`: each block of 128 rows is symmetric positive definite. `moment_second`: Positive.
All inputs are finite; a program needn't handle non-finite values.
Results may differ from the reference program's by a relative error of at most 0.009.
The reference program's roundings to bfloat16 on the way count: a program that leaves them out, or rounds other values in their place, can miss the bound.
Values may be sent and summed in bfloat16 or wider, within the bound.
A program may use at most 256 MiB of HBM per device.

```python
import math
import jax
import jax.numpy as jnp
from jax import lax

D = 256
HEADS = 8
FF = 2048
BLK = 128
IMAGES = 6
IMG_W = 32
STEP = 10
TOK_DEV = 512
PACK_LEN = 2048
PACKS = 8
TOKENS = 16384
BLOCKS = 80
VECS = 4096


def image_starts(key):
    key_cut, key_spot = jax.random.split(key)
    big_len = PACK_LEN // 2 + TOK_DEV
    rest_len = PACK_LEN - big_len
    ranks = jax.vmap(lambda subkey: jax.random.permutation(subkey, rest_len - 1))(jax.random.split(key_cut, PACKS))
    small = jnp.concatenate([jnp.ones((PACKS, 1), jnp.int32), (ranks < IMAGES - 2).astype(jnp.int32)], axis=1)
    spot = jax.random.randint(key_spot, (PACKS, 1), 0, IMAGES)
    counted = jnp.cumsum(small, axis=1)
    offset = jnp.sum((counted <= spot).astype(jnp.int32), axis=1, keepdims=True)
    index = jnp.arange(PACK_LEN, dtype=jnp.int32)[None, :]
    before = jnp.take_along_axis(small, jnp.broadcast_to(jnp.clip(index, 0, rest_len - 1), (PACKS, PACK_LEN)), axis=1)
    after = jnp.take_along_axis(small, jnp.broadcast_to(jnp.clip(index - big_len, 0, rest_len - 1), (PACKS, PACK_LEN)), axis=1)
    inside = (index == offset).astype(jnp.int32)
    return jnp.where(index < offset, before, jnp.where(index < offset + big_len, inside, after)).astype(jnp.int32)


def grad_factor(rows):
    blocks_of = jnp.arange(rows) // BLK
    square = (D // BLK) ** 2
    factor = jnp.where(blocks_of < 2 * square, 0.6, jnp.where(blocks_of < 3 * square, 0.4, jnp.where(blocks_of < 4 * square, 0.1, 0.4)))
    return factor * math.sqrt(TOKENS)


def statistic(key):
    key_noise, key_diag = jax.random.split(key)
    noise = jax.random.uniform(key_noise, (BLOCKS, BLK, BLK), jnp.float32, -1.0, 1.0)
    symmetric = 0.5 * (noise + jnp.swapaxes(noise, 1, 2))
    diagonal = jnp.exp(jax.random.uniform(key_diag, (BLOCKS, BLK, 1), jnp.float32, 0.0, math.log(4.0)))
    eye_mask = jnp.arange(BLK)[:, None] == jnp.arange(BLK)[None, :]
    matrix = jnp.where(eye_mask[None], diagonal, 0.093 * symmetric)
    factor = grad_factor(BLOCKS * BLK).reshape(BLOCKS, BLK)[:, 0]
    scales = 0.0526 * BLK * factor * factor
    return (matrix * scales[:, None, None]).reshape(BLOCKS * BLK, BLK)


def orthogonal(key):
    key_rows, key_cols, key_order = jax.random.split(key, 3)
    signs_row = (2 * jax.random.randint(key_rows, (BLOCKS, BLK, 1), 0, 2) - 1).astype(jnp.float32)
    signs_col = (2 * jax.random.randint(key_cols, (BLOCKS, 1, BLK), 0, 2) - 1).astype(jnp.float32)
    order = jax.vmap(lambda subkey: jax.random.permutation(subkey, BLK))(jax.random.split(key_order, BLOCKS))[:, None, :]
    row_index = jnp.arange(BLK).astype(jnp.float32)[None, :, None]
    weight_of = jnp.where(order == 0, math.sqrt(1.0 / BLK), math.sqrt(2.0 / BLK))
    matrix = signs_row * signs_col * weight_of * jnp.cos(math.pi * (row_index + 0.5) * order.astype(jnp.float32) / BLK)
    return matrix.reshape(BLOCKS * BLK, BLK)


def draw_segment_ids(key, part):
    flags = image_starts(key)
    return (jnp.cumsum(flags, axis=1) - 1).reshape(TOKENS).astype(jnp.int32)


def draw_padding(key, part):
    flags = image_starts(key)
    key = jax.random.fold_in(key, 5)
    holes = jax.random.randint(key, (PACKS, PACK_LEN), 0, 8) == 0
    return (holes & (flags == 0)).astype(jnp.int32).reshape(TOKENS)


def draw_master(key, part):
    key = jax.random.fold_in(key, 3)
    rows = BLOCKS * BLK
    blocks_of = jnp.arange(rows) // BLK
    square = (D // BLK) ** 2
    wide_blocks = D // BLK * (FF // BLK)
    scales = jnp.where(blocks_of < 3 * square, D ** (-0.5), jnp.where(blocks_of < 4 * square, max(D // 64, 1) ** (-0.5), jnp.where(blocks_of < 4 * square + wide_blocks, D ** (-0.5), FF ** (-0.5))))
    return jax.random.normal(key, (rows, BLK), jnp.float32) * scales[:, None]


def draw_moment_first(key, part):
    key = jax.random.fold_in(key, 7)
    rows = BLOCKS * BLK
    return jax.random.normal(key, (rows, BLK), jnp.float32) * (0.111 * grad_factor(rows))[:, None]


def draw_moment_second(key, part):
    key = jax.random.fold_in(key, 9)
    rows = BLOCKS * BLK
    factor = grad_factor(rows)
    spread = jnp.exp(jax.random.uniform(key, (rows, BLK), jnp.float32, 0.0, math.log(4.0)))
    return spread * (0.0526 * factor * factor)[:, None]


def draw_stat_left(key, part):
    key = jax.random.fold_in(key, 11)
    return statistic(key)


def draw_stat_right(key, part):
    key = jax.random.fold_in(key, 13)
    return statistic(key)


def draw_basis_left(key, part):
    key = jax.random.fold_in(key, 15)
    return orthogonal(key)


def draw_basis_right(key, part):
    key = jax.random.fold_in(key, 17)
    return orthogonal(key)


def draw_vec_params(key, part):
    key = jax.random.fold_in(key, 19)
    key_gain, key_bias = jax.random.split(key)
    spots = jnp.arange(VECS)
    gain_mask = (spots >= 3 * D) & (spots < 4 * D) | (spots >= 6 * D + FF) & (spots < 7 * D + FF)
    gains = 1.0 + jax.random.uniform(key_gain, (VECS,), jnp.float32, -0.3, 0.3)
    biases = 0.3 * jax.random.normal(key_bias, (VECS,), jnp.float32)
    return jnp.where(gain_mask, gains, biases)


def levels(rng, shape, cuts, low, high):
    factor_of = 1.0
    for axis_at, blocks in cuts:
        heights = jax.random.uniform(jax.random.fold_in(jax.random.fold_in(rng, 6), axis_at), (blocks,), jnp.float32, low / len(cuts), high / len(cuts))
        factor_of = factor_of * jnp.repeat(jnp.exp(heights), shape[axis_at] // blocks).reshape((-1,) + (1,) * (len(shape) - 1 - axis_at))
    return factor_of


def gaussian(rng, extent, scale, reach, cuts=(), kind=jnp.bfloat16):
    factor_of = levels(rng, extent, cuts, -0.22, 0.18) if cuts else 1.0
    entries = jax.random.normal(rng, extent, jnp.float32) * scale * factor_of
    return jnp.minimum(jnp.maximum(entries, -reach), reach).astype(kind)


def setup_inputs(seed: int = 0) -> dict:
    key_list = jax.random.split(jax.random.key(seed), 15)
    return {
        "tokens": gaussian(key_list[0], (TOKENS, D), 1.0, 6.0, ((0, 32),), jnp.float32),
        "cotangent": gaussian(key_list[1], (TOKENS, D), 1.0, 6.0, ((0, 32),), jnp.float32),
        "segment_ids": draw_segment_ids(jax.random.fold_in(key_list[14], 71), 0),
        "padding": draw_padding(jax.random.fold_in(key_list[14], 71), 0),
        "master": draw_master(jax.random.fold_in(key_list[14], 71), 0),
        "moment_first": draw_moment_first(jax.random.fold_in(key_list[14], 71), 0),
        "moment_second": draw_moment_second(jax.random.fold_in(key_list[14], 71), 0),
        "stat_left": draw_stat_left(jax.random.fold_in(key_list[14], 71), 0),
        "stat_right": draw_stat_right(jax.random.fold_in(key_list[14], 71), 0),
        "basis_left": draw_basis_left(jax.random.fold_in(key_list[14], 71), 0),
        "basis_right": draw_basis_right(jax.random.fold_in(key_list[14], 71), 0),
        "vec_params": draw_vec_params(jax.random.fold_in(key_list[14], 71), 0),
        "vec_first": gaussian(key_list[12], (VECS,), (0.055 * TOKENS ** 0.5), 40.0, (), jnp.float32),
        "vec_second": jnp.clip(jnp.exp(jax.random.uniform(key_list[13], (VECS,), jnp.float32, math.log(212.992), math.log(868.352))), 212.992, 868.352),
    }


MASKED_SCORE = -1e+30
BETA_ONE = 0.9
BETA_TWO = 0.95
LEARN_RATE = 0.25
WEIGHT_DECAY = 0.01
EPSILON = 1e-08
NORM_EPSILON = 1e-05
TOP_PRECISION = lax.Precision.HIGHEST

@jax.custom_vjp
def low(v):
    return lax.optimization_barrier(v.astype(jnp.bfloat16)).astype(jnp.float32)

@jax.custom_vjp
def low_back(v):
    return v

def low_keep(v):
    return (low(v), None)

def low_pass(kept, grad):
    return (grad,)

def back_keep(v):
    return (v, None)

def back_low(kept, grad):
    return (low(grad),)
low.defvjp(low_keep, low_pass)
low_back.defvjp(back_keep, back_low)

def matmul(left, right):
    return jnp.matmul(left, right, precision=TOP_PRECISION)

def einsum_high(form, left, right):
    return jnp.einsum(form, left, right, precision=TOP_PRECISION)

def layer_norm(hidden, gain, offset):
    center = hidden - lax.optimization_barrier(jnp.mean(hidden, axis=-1, keepdims=True))
    spread = lax.optimization_barrier(jnp.mean(center * center, axis=-1, keepdims=True))
    return center * lax.rsqrt(spread + NORM_EPSILON) * gain + offset

def sine_table(places, model_width):
    half_width = model_width // 2
    column = jnp.arange(half_width)
    period = 10000.0 ** ((2 * (column // 2)).astype(jnp.float32) / half_width)

    def embed_one(coordinate):
        angles = coordinate.astype(jnp.float32)[:, None] / period[None, :]
        return jnp.where(column[None, :] % 2 == 0, jnp.sin(angles), jnp.cos(angles))
    return jnp.concatenate([embed_one(places // IMG_W), embed_one(places % IMG_W)], axis=1)

def from_blocks(stack, row_count, col_count, block_size):
    shaped = stack.reshape(row_count // block_size, col_count // block_size, block_size, block_size)
    return shaped.transpose(0, 2, 1, 3).reshape(row_count, col_count)

def to_blocks(matrix, block_size):
    row_count, col_count = matrix.shape
    shaped = matrix.reshape(row_count // block_size, block_size, col_count // block_size, block_size)
    return shaped.transpose(0, 2, 1, 3).reshape(-1, block_size)

def split_weights(stack, model_width, hidden_width, block_size):
    square = model_width * model_width // block_size
    wide_rows = model_width * hidden_width // block_size
    bounds = [0, square, 2 * square, 3 * square, 4 * square, 4 * square + wide_rows, 4 * square + 2 * wide_rows]
    shapes = [(model_width, model_width)] * 4 + [(model_width, hidden_width), (hidden_width, model_width)]
    return [from_blocks(stack[bounds[number]:bounds[number + 1]], shapes[number][0], shapes[number][1], block_size) for number in range(6)]

def split_vectors(vector, model_width, hidden_width):
    lengths = [model_width] * 5 + [hidden_width] + [model_width] * 3
    pieces = []
    offset = 0
    for length in lengths:
        pieces.append(vector[offset:offset + length])
        offset = offset + length
    return pieces

def cholesky_basis(matrix):
    gram = einsum_high('nij,nik->njk', matrix, matrix)
    factor = jnp.linalg.cholesky(gram)
    solved = jax.vmap(lambda lower_part, block_rows: jax.scipy.linalg.solve_triangular(lower_part, block_rows.T, lower=True))(factor, matrix)
    return jnp.swapaxes(solved, 1, 2)

def soap_update(grad, first, second, left_stat, right_stat, left_basis, right_basis, weights, block_size):
    shape = (-1, block_size, block_size)
    grad, first, second = (grad.reshape(shape), first.reshape(shape), second.reshape(shape))
    left_stat, right_stat = (left_stat.reshape(shape), right_stat.reshape(shape))
    left_basis, right_basis, weights = (left_basis.reshape(shape), right_basis.reshape(shape), weights.reshape(shape))
    rotated = einsum_high('nji,njk->nik', left_basis, grad)
    rotated = einsum_high('nik,nkl->nil', rotated, right_basis)
    first_new = BETA_ONE * first + (1.0 - BETA_ONE) * rotated
    second_new = BETA_TWO * second + (1.0 - BETA_TWO) * rotated * rotated
    ratio = first_new / (1.0 - BETA_ONE ** STEP) / (jnp.sqrt(second_new / (1.0 - BETA_TWO ** STEP)) + EPSILON)
    stepped = einsum_high('nij,njk->nik', left_basis, ratio)
    stepped = einsum_high('nik,nlk->nil', stepped, right_basis)
    weights_new = weights - LEARN_RATE * (stepped + WEIGHT_DECAY * weights)
    left_new = BETA_TWO * left_stat + (1.0 - BETA_TWO) * einsum_high('nij,nkj->nik', grad, grad)
    right_new = BETA_TWO * right_stat + (1.0 - BETA_TWO) * einsum_high('nji,njk->nik', grad, grad)
    basis_left_new = cholesky_basis(einsum_high('nij,njk->nik', left_new, left_basis))
    basis_right_new = cholesky_basis(einsum_high('nij,njk->nik', right_new, right_basis))
    flat = lambda array_in: array_in.reshape(-1, block_size)
    return (flat(first_new), flat(second_new), flat(weights_new), flat(weights_new).astype(jnp.bfloat16), flat(left_new), flat(right_new), flat(basis_left_new), flat(basis_right_new))

def adam_vector(grad, vector, first, second):
    first_new = BETA_ONE * first + (1.0 - BETA_ONE) * grad
    second_new = BETA_TWO * second + (1.0 - BETA_TWO) * grad * grad
    ratio = first_new / (1.0 - BETA_ONE ** STEP) / (jnp.sqrt(second_new / (1.0 - BETA_TWO ** STEP)) + EPSILON)
    return (vector - LEARN_RATE * ratio, first_new, second_new)

def attention_heads(queries, key_rows, value_rows, allowed, score_scale):

    def one_head(inputs):
        head_query, head_key, head_value = inputs
        scores = low_back(matmul(head_query, head_key.T))
        scores = jnp.where(allowed, scores * score_scale, MASKED_SCORE)
        largest = lax.optimization_barrier(jnp.max(scores, axis=-1, keepdims=True))
        weights = jnp.exp(scores - largest)
        weights = weights / lax.optimization_barrier(jnp.sum(weights, axis=-1, keepdims=True))
        return matmul(low(weights), head_value)
    return lax.map(jax.checkpoint(one_head), (queries, key_rows, value_rows))

def forward(params, pack_tokens, positions, allowed):
    matrices, vectors = params
    w_query, w_key, w_value, w_out, w_one, w_two = [low(matrix) for matrix in matrices]
    bias_query, bias_value, bias_out, gain_one, shift_one, bias_hidden, bias_two, gain_two, shift_two = split_vectors(vectors, D, FF)
    with_place = low(pack_tokens + positions)
    plain_rows = low(pack_tokens)
    queries = low(low_back(matmul(with_place, w_query) + bias_query))
    key_rows = low(low_back(matmul(with_place, w_key)))
    value_rows = low(low_back(matmul(plain_rows, w_value) + bias_value))

    def by_head(matrix_rows):
        return matrix_rows.reshape(matrix_rows.shape[0], HEADS, D // HEADS).transpose(1, 0, 2)
    attended = attention_heads(by_head(queries), by_head(key_rows), by_head(value_rows), allowed, (D // HEADS) ** (-0.5))
    attended = low(low_back(attended.transpose(1, 0, 2).reshape(-1, D)))
    branch = low_back(matmul(attended, w_out) + bias_out)
    normed = layer_norm(pack_tokens + branch, gain_one, shift_one)
    hidden_pre = low_back(matmul(low(normed), w_one) + bias_hidden)
    activated = low(jax.nn.gelu(hidden_pre, approximate=True))
    second = low_back(matmul(activated, w_two) + bias_two)
    return layer_norm(normed + second, gain_two, shift_two)

def reference(tokens, cotangent, segment_ids, padding, master, moment_first, moment_second, stat_left, stat_right, basis_left, basis_right, vec_params, vec_first, vec_second):
    matrices = split_weights(master, D, FF, BLK)
    params = (matrices, vec_params)

    def pack_step(totals, inputs):
        pack_tokens, pack_cotangent, pack_ids, pack_padding = inputs
        starts = lax.optimization_barrier(jnp.sum(pack_ids[None, :] < pack_ids[:, None], axis=1)).astype(jnp.int32)
        places = jnp.arange(PACK_LEN, dtype=jnp.int32) - starts
        positions = sine_table(places, D)
        allowed = (pack_ids[:, None] == pack_ids[None, :]) & (pack_padding[None, :] == 0)
        result, pullback = jax.vjp(lambda values, pack_rows: forward(values, pack_rows, positions, allowed), params, pack_tokens)
        grads, token_grad = pullback(pack_cotangent)
        totals = jax.tree.map(jnp.add, totals, grads)
        return (totals, (result, token_grad))
    zeros = jax.tree.map(jnp.zeros_like, params)
    totals, (layer_out, input_grad) = lax.scan(pack_step, zeros, (tokens.reshape(PACKS, PACK_LEN, D), cotangent.reshape(PACKS, PACK_LEN, D), segment_ids.reshape(PACKS, PACK_LEN), padding.reshape(PACKS, PACK_LEN)))
    grad_blocks = jnp.concatenate([to_blocks(matrix, BLK) for matrix in totals[0]], axis=0)
    updated = soap_update(grad_blocks, moment_first, moment_second, stat_left, stat_right, basis_left, basis_right, master, BLK)
    vec_new, vec_first_new, vec_second_new = adam_vector(totals[1], vec_params, vec_first, vec_second)
    return (layer_out.reshape(TOKENS, D), input_grad.reshape(TOKENS, D), updated[0], updated[1], updated[2], updated[3], updated[4], updated[5], updated[6], updated[7], vec_new, vec_first_new, vec_second_new)
```

```python
import functools
import jax
import jax.numpy as jnp
from jax import lax
from jax.experimental import pallas as pl
from jax.experimental.pallas import tpu as pltpu
from jax.sharding import PartitionSpec as P

HEADS = 8
IMG_W = 32
MASKED_SCORE = -1e30
NORM_EPSILON = 1e-05
STEP = 10
BETA_ONE = 0.9
BETA_TWO = 0.95
LEARN_RATE = 0.25
WEIGHT_DECAY = 0.01
EPSILON = 1e-08
F32 = jnp.float32
BF16 = jnp.bfloat16
NN = (((1,), (0,)), ((), ()))
NT = (((1,), (1,)), ((), ()))
TN = (((0,), (0,)), ((), ()))


def dot(left, right, dims=NN):
    return lax.dot_general(left, right, dims, preferred_element_type=F32)


def split2(v):
    high = v.astype(BF16)
    return high, (v - high.astype(F32)).astype(BF16)


def split3(v):
    high = v.astype(BF16)
    rest = v - high.astype(F32)
    mid = rest.astype(BF16)
    return high, mid, (rest - mid.astype(F32)).astype(BF16)


def dot3(left, right, dims=NN):
    la, ra = dims[0][0][0], dims[0][1][0]
    lh, ll = split2(left)
    rh, rl = split2(right)
    return dot(jnp.concatenate([lh, ll, lh], la), jnp.concatenate([rh, rh, rl], ra), dims)


def dot6(left, right, dims=NN):
    la, ra = dims[0][0][0], dims[0][1][0]
    lh, lm, ll = split3(left)
    rh, rm, rl = split3(right)
    return dot(
        jnp.concatenate([lh, lh, lm, lm, lh, ll], la),
        jnp.concatenate([rh, rm, rh, rm, rl, rh], ra),
        dims,
    )


def eliminate(m_ref, qt_ref, count):
    sub = lax.broadcasted_iota(jnp.int32, (16, 128), 0)

    def panel(index, carry):
        base = pl.multiple_of(index * 16, 16)
        back = lax.rem(128 - base, 128)
        gram, rest = [], []
        for s in range(count):
            gram.append(pltpu.roll(m_ref[s, pl.ds(base, 16), :128], back, 1))
            rest.append(m_ref[s, pl.ds(base, 16), 128:])
        for j in range(16):
            for s in range(count):
                g, a = gram[s], rest[s]
                col = jnp.broadcast_to(g[:, j : j + 1], (16, 128))
                inv = lax.rsqrt(col[j : j + 1, :])
                row_g = g[j : j + 1, :] * inv
                row_a = a[j : j + 1, :] * inv
                factor = jnp.where(sub > j, col * inv, 0.0)
                gram[s] = jnp.where(sub == j, row_g, g - factor * row_g)
                rest[s] = jnp.where(sub == j, row_a, a - factor * row_a)
        for s in range(count):
            u = pltpu.roll(gram[s], base, 1)
            qt_ref[s, pl.ds(base, 16), :] = rest[s]
            uh, um, ul = split3(u)
            ah, am, al = split3(rest[s])
            wh, wm, wl = [jnp.concatenate(p, 1) for p in ((uh, ah), (um, am), (ul, al))]
            m_ref[s] -= dot(
                jnp.concatenate([uh, uh, um, um, uh, ul], 0),
                jnp.concatenate([wh, wm, wh, wm, wl, wh], 0),
                TN,
            )
        return carry

    lax.fori_loop(0, 8, panel, 0)


def soap_kernel(
    blocks, slots,
    grad_ref, first_ref, second_ref, left_ref, right_ref, lbasis_ref, rbasis_ref, master_ref,
    first_out, second_out, master_out, copy_out, left_out, right_out, basis_out,
    m_ref, qt_ref,
):
    me = lax.axis_index("row")
    for s in range(slots):
        t = jnp.minimum(me * slots + s, 2 * blocks - 1)
        is_right = t >= blocks
        rows = pl.ds(pl.multiple_of(jnp.where(is_right, t - blocks, t) * 128, 128), 128)
        g = grad_ref[rows, :].astype(F32)
        g = jnp.where(is_right, g.T, g).astype(BF16)
        stat = jnp.where(is_right, right_ref[rows, :], left_ref[rows, :])
        basis = jnp.where(is_right, rbasis_ref[rows, :], lbasis_ref[rows, :])
        new = BETA_TWO * stat + (1.0 - BETA_TWO) * dot(g, g, NT)
        a = dot6(new, basis)
        at = a.T
        m_ref[s, :, :128] = dot6(at, a)
        m_ref[s, :, 128:] = at
    eliminate(m_ref, qt_ref, slots)
    for s in range(slots):
        basis_out[s * 128 : (s + 1) * 128, :] = qt_ref[s].T

    def block_step(index, carry):
        rows = pl.ds(pl.multiple_of(index * 128, 128), 128)
        g = grad_ref[rows, :]
        left_out[rows, :] = BETA_TWO * left_ref[rows, :] + (1.0 - BETA_TWO) * dot(g, g, NT)
        right_out[rows, :] = BETA_TWO * right_ref[rows, :] + (1.0 - BETA_TWO) * dot(g, g, TN)
        lb, rb = lbasis_ref[rows, :], rbasis_ref[rows, :]
        lh, ll = split2(lb)
        turned = dot(jnp.concatenate([lh, ll], 0), jnp.concatenate([g, g], 0), TN)
        rotated = dot3(turned, rb)
        first = BETA_ONE * first_ref[rows, :] + (1.0 - BETA_ONE) * rotated
        second = BETA_TWO * second_ref[rows, :] + (1.0 - BETA_TWO) * rotated * rotated
        first_out[rows, :] = first
        second_out[rows, :] = second
        ratio = first / (1.0 - BETA_ONE**STEP) / (jnp.sqrt(second / (1.0 - BETA_TWO**STEP)) + EPSILON)
        stepped = dot3(dot3(lb, ratio), rb, NT)
        weights = master_ref[rows, :]
        weights = weights - LEARN_RATE * (stepped + WEIGHT_DECAY * weights)
        master_out[rows, :] = weights
        copy_out[rows, :] = weights.astype(BF16)
        return carry

    lax.fori_loop(0, blocks, block_step, 0)


def soap_call(row_count, grad, first, second, left, right, lbasis, rbasis, master):
    rows = grad.shape[0]
    blocks = rows // 128
    slots = -(-2 * blocks // row_count)
    full = jax.ShapeDtypeStruct((rows, 128), F32)
    vm = pl.BlockSpec(memory_space=pltpu.VMEM)
    return pl.pallas_call(
        functools.partial(soap_kernel, blocks, slots),
        out_shape=(full, full, full, jax.ShapeDtypeStruct((rows, 128), BF16), full, full,
                   jax.ShapeDtypeStruct((slots * 128, 128), F32)),
        in_specs=[vm] * 8,
        out_specs=(vm,) * 7,
        scratch_shapes=[pltpu.VMEM((slots, 128, 256), F32), pltpu.VMEM((slots, 128, 128), F32)],
        compiler_params=pltpu.CompilerParams(vmem_limit_bytes=40 << 20),
        name="soap",
    )(grad, first, second, left, right, lbasis, rbasis, master)


def layer_norm(hidden, gain, offset):
    center = hidden - jnp.mean(hidden, axis=-1, keepdims=True)
    spread = jnp.mean(center * center, axis=-1, keepdims=True)
    return center * lax.rsqrt(spread + NORM_EPSILON) * gain + offset


def gelu_tanh(values):
    return jax.nn.gelu(values, approximate=True)


def sine_table(places, model_width):
    half_width = model_width // 2
    column = jnp.arange(half_width)
    period = 10000.0 ** ((2 * (column // 2)).astype(jnp.float32) / half_width)

    def embed_one(coordinate):
        angles = coordinate.astype(jnp.float32)[:, None] / period[None, :]
        return jnp.where(column[None, :] % 2 == 0, jnp.sin(angles), jnp.cos(angles))

    return jnp.concatenate([embed_one(places // IMG_W), embed_one(places % IMG_W)], axis=1)


def from_blocks(stack, row_count, col_count, block_size):
    shaped = stack.reshape(row_count // block_size, col_count // block_size, block_size, block_size)
    return shaped.transpose(0, 2, 1, 3).reshape(row_count, col_count)


def to_blocks(matrix, block_size):
    row_count, col_count = matrix.shape
    shaped = matrix.reshape(
        row_count // block_size, block_size, col_count // block_size, block_size
    )
    return shaped.transpose(0, 2, 1, 3).reshape(-1, block_size)


def split_weights(stack, model_width, hidden_width, block_size):
    square = model_width * model_width // block_size
    wide_rows = model_width * hidden_width // block_size
    bounds = [
        0,
        square,
        2 * square,
        3 * square,
        4 * square,
        4 * square + wide_rows,
        4 * square + 2 * wide_rows,
    ]
    shapes = [(model_width, model_width)] * 4 + [
        (model_width, hidden_width),
        (hidden_width, model_width),
    ]
    return [
        from_blocks(
            stack[bounds[number] : bounds[number + 1]],
            shapes[number][0],
            shapes[number][1],
            block_size,
        )
        for number in range(6)
    ]


def split_vectors(vector, model_width, hidden_width):
    lengths = [model_width] * 5 + [hidden_width] + [model_width] * 3
    pieces = []
    offset = 0
    for length in lengths:
        pieces.append(vector[offset : offset + length])
        offset = offset + length
    return pieces


def adam_vector(grad, vector, first, second):
    first_new = BETA_ONE * first + (1.0 - BETA_ONE) * grad
    second_new = BETA_TWO * second + (1.0 - BETA_TWO) * grad * grad
    ratio = (
        first_new
        / (1.0 - BETA_ONE**STEP)
        / (jnp.sqrt(second_new / (1.0 - BETA_TWO**STEP)) + EPSILON)
    )
    return (vector - LEARN_RATE * ratio, first_new, second_new)


def contract_rows(left, right):
    return jnp.einsum("ti,to->io", left, right, preferred_element_type=jnp.float32)


def project_back(grad, weight):
    return jnp.einsum("to,io->ti", grad, weight, preferred_element_type=jnp.float32)


def head_scores(queries, key_rows, allowed, columns, score_scale):
    scores = jnp.einsum(
        "qd,kd->qk", queries[:, columns], key_rows[:, columns], preferred_element_type=jnp.float32
    )
    return jnp.where(allowed, scores * score_scale, MASKED_SCORE)


def attend(queries, key_rows, value_rows, allowed, head_count, score_scale):
    head_width = queries.shape[1] // head_count
    pieces, totals = ([], [])
    for head_index in range(head_count):
        columns = slice(head_index * head_width, (head_index + 1) * head_width)
        scores = head_scores(queries, key_rows, allowed, columns, score_scale)
        largest = jnp.max(scores, axis=1, keepdims=True)
        weights = jnp.exp(scores - largest)
        summed = jnp.sum(weights, axis=1, keepdims=True)
        weights = (weights / summed).astype(jnp.bfloat16)
        pieces.append(jnp.dot(weights, value_rows[:, columns], preferred_element_type=jnp.float32))
        totals.append(largest + jnp.log(summed))
    return (jnp.concatenate(pieces, axis=1), totals)


def attend_back(queries, key_rows, value_rows, grad_out, allowed, totals, head_count, score_scale):
    head_width = queries.shape[1] // head_count
    query_parts, key_parts, value_parts, centers = ([], [], [], [])
    for head_index in range(head_count):
        columns = slice(head_index * head_width, (head_index + 1) * head_width)
        scores = head_scores(queries, key_rows, allowed, columns, score_scale)
        probs = jnp.exp(scores - totals[head_index])
        head_grad = grad_out[:, columns]
        along = jnp.einsum(
            "qd,kd->qk", head_grad, value_rows[:, columns], preferred_element_type=jnp.float32
        )
        center = jnp.sum(probs * along, axis=1, keepdims=True)
        centers.append(center)
        score_grad = (probs * (along - center) * score_scale).astype(jnp.bfloat16)
        query_parts.append(
            jnp.dot(score_grad, key_rows[:, columns], preferred_element_type=jnp.float32)
        )
        key_parts.append(
            jnp.einsum(
                "qk,qd->kd", score_grad, queries[:, columns], preferred_element_type=jnp.float32
            )
        )
        value_parts.append(
            jnp.einsum(
                "qk,qd->kd",
                probs.astype(jnp.bfloat16),
                head_grad,
                preferred_element_type=jnp.float32,
            )
        )
    query_grad = jnp.concatenate(query_parts, axis=1)
    return (
        query_grad,
        jnp.concatenate(key_parts, axis=1),
        jnp.concatenate(value_parts, axis=1),
        centers,
    )


def shards(
    tokens,
    cotangent,
    segment_ids,
    padding,
    master,
    moment_first,
    moment_second,
    stat_left,
    stat_right,
    basis_left,
    basis_right,
    vec_params,
    vec_first,
    vec_second,
):
    tok_rows, model_width = tokens.shape
    block_size = master.shape[1]
    owned_count = master.shape[0]
    hidden_width = vec_params.shape[0] - 8 * model_width
    score_scale = (model_width // HEADS) ** (-0.5)
    gathered = lax.all_gather(master.astype(jnp.bfloat16), "pack", axis=0, tiled=True)
    w_query, w_key, w_value, w_out, w_one, w_two = split_weights(
        gathered, model_width, hidden_width, block_size
    )
    (
        bias_query,
        bias_value,
        bias_out,
        gain_one,
        shift_one,
        bias_hidden,
        bias_two,
        gain_two,
        shift_two,
    ) = split_vectors(vec_params, model_width, hidden_width)
    code_rows = lax.all_gather(jnp.stack([segment_ids, padding]), "row", axis=1, tiled=True)
    key_ids = code_rows[0]
    key_padding = code_rows[1]
    starts = jnp.sum(key_ids[None, :] < segment_ids[:, None], axis=1)
    places = lax.axis_index("row") * tok_rows + jnp.arange(tok_rows, dtype=jnp.int32) - starts
    positions = sine_table(places, model_width)
    allowed = (segment_ids[:, None] == key_ids[None, :]) & (key_padding[None, :] == 0)
    with_place = (tokens + positions).astype(jnp.bfloat16)
    plain_rows = tokens.astype(jnp.bfloat16)
    queries = (
        jnp.dot(with_place, w_query, preferred_element_type=jnp.float32) + bias_query
    ).astype(jnp.bfloat16)
    key_rows = jnp.dot(with_place, w_key, preferred_element_type=jnp.float32).astype(jnp.bfloat16)
    value_rows = (
        jnp.dot(plain_rows, w_value, preferred_element_type=jnp.float32) + bias_value
    ).astype(jnp.bfloat16)
    key_all, value_all = (
        lax.all_gather(key_rows, "row", axis=0, tiled=True),
        lax.all_gather(value_rows, "row", axis=0, tiled=True),
    )
    attended, totals = attend(queries, key_all, value_all, allowed, HEADS, score_scale)
    attended = attended.astype(jnp.bfloat16)
    branch = jnp.dot(attended, w_out, preferred_element_type=jnp.float32) + bias_out
    normed, first_norm_back = jax.vjp(layer_norm, tokens + branch, gain_one, shift_one)
    normed_low = normed.astype(jnp.bfloat16)
    hidden_pre = jnp.dot(normed_low, w_one, preferred_element_type=jnp.float32) + bias_hidden
    activated, gelu_back = jax.vjp(gelu_tanh, hidden_pre)
    activated = activated.astype(jnp.bfloat16)
    second = jnp.dot(activated, w_two, preferred_element_type=jnp.float32) + bias_two
    layer_out, second_norm_back = jax.vjp(layer_norm, normed + second, gain_two, shift_two)
    sum_grad, grad_gain_two, grad_shift_two = second_norm_back(cotangent)
    second_grad = sum_grad.astype(jnp.bfloat16)
    grad_w_two = contract_rows(activated, second_grad)
    grad_bias_two = jnp.sum(second_grad.astype(jnp.float32), axis=0)
    (hidden_grad,) = gelu_back(project_back(second_grad, w_two))
    hidden_grad = hidden_grad.astype(jnp.bfloat16)
    grad_w_one = contract_rows(normed_low, hidden_grad)
    grad_bias_hidden = jnp.sum(hidden_grad.astype(jnp.float32), axis=0)
    normed_grad = sum_grad + project_back(hidden_grad, w_one)
    branch_grad, grad_gain_one, grad_shift_one = first_norm_back(normed_grad)
    branch_low = branch_grad.astype(jnp.bfloat16)
    grad_w_out = contract_rows(attended, branch_low)
    grad_bias_out = jnp.sum(branch_low.astype(jnp.float32), axis=0)
    attended_grad = project_back(branch_low, w_out).astype(jnp.bfloat16)
    query_grad, key_grad_all, value_grad_all, centers = attend_back(
        queries, key_all, value_all, attended_grad, allowed, totals, HEADS, score_scale
    )
    key_grad, value_grad = (
        lax.psum_scatter(key_grad_all, "row", scatter_dimension=0, tiled=True),
        lax.psum_scatter(value_grad_all, "row", scatter_dimension=0, tiled=True),
    )
    query_low = query_grad.astype(jnp.bfloat16)
    key_low = key_grad.astype(jnp.bfloat16)
    value_low = value_grad.astype(jnp.bfloat16)
    grad_w_query = contract_rows(with_place, query_low)
    grad_w_key = contract_rows(with_place, key_low)
    grad_w_value = contract_rows(plain_rows, value_low)
    grad_bias_query = jnp.sum(query_low.astype(jnp.float32), axis=0)
    grad_bias_value = jnp.sum(value_low.astype(jnp.float32), axis=0)
    input_grad = (
        branch_grad
        + project_back(query_low, w_query)
        + project_back(key_low, w_key)
        + project_back(value_low, w_value)
    )
    grad_stack = jnp.concatenate(
        [
            to_blocks(matrix, block_size)
            for matrix in (
                grad_w_query,
                grad_w_key,
                grad_w_value,
                grad_w_out,
                grad_w_one,
                grad_w_two,
            )
        ],
        axis=0,
    )
    grad_vector = jnp.concatenate(
        [
            grad_bias_query,
            grad_bias_value,
            grad_bias_out,
            grad_gain_one,
            grad_shift_one,
            grad_bias_hidden,
            grad_bias_two,
            grad_gain_two,
            grad_shift_two,
        ]
    )
    total_vector = lax.psum(grad_vector, ("pack", "row"))
    share = lax.psum_scatter(grad_stack, ("pack", "row"), scatter_dimension=0, tiled=True)
    owned = lax.all_gather(share.astype(BF16), "row", axis=0, tiled=True)
    updated = soap_call(
        lax.axis_size("row"), owned, moment_first, moment_second, stat_left, stat_right,
        basis_left, basis_right, master,
    )
    bases = lax.all_gather(updated[6], "row", axis=0, tiled=True)
    updated = updated[:6] + (bases[:owned_count], bases[owned_count : 2 * owned_count])
    vec_new, vec_first_new, vec_second_new = adam_vector(
        total_vector, vec_params, vec_first, vec_second
    )
    return (
        layer_out,
        input_grad,
        updated[0],
        updated[1],
        updated[2],
        updated[3],
        updated[4],
        updated[5],
        updated[6],
        updated[7],
        vec_new,
        vec_first_new,
        vec_second_new,
    )


def solution(mesh):
    placed = (
        P(("pack", "row"), None),
        P(("pack", "row"), None),
        P(("pack", "row")),
        P(("pack", "row")),
        P("pack", None),
        P("pack", None),
        P("pack", None),
        P("pack", None),
        P("pack", None),
        P("pack", None),
        P("pack", None),
        P(),
        P(),
        P(),
    )
    return jax.shard_map(
        shards,
        mesh=mesh,
        in_specs=placed,
        out_specs=(
            P(("pack", "row"), None),
            P(("pack", "row"), None),
            P("pack", None),
            P("pack", None),
            P("pack", None),
            P("pack", None),
            P("pack", None),
            P("pack", None),
            P("pack", None),
            P("pack", None),
            P(),
            P(),
            P(),
        ),
        check_vma=False,
    )
```

```python
import functools
import jax
import jax.numpy as jnp
from jax import lax
from jax.experimental import pallas as pl
from jax.experimental.pallas import tpu as pltpu
from jax.sharding import PartitionSpec as P

HEADS = 8
IMG_W = 32
MASKED_SCORE = -1e30
NORM_EPSILON = 1e-05
STEP = 10
BETA_ONE = 0.9
BETA_TWO = 0.95
LEARN_RATE = 0.25
WEIGHT_DECAY = 0.01
EPSILON = 1e-08
F32 = jnp.float32
BF16 = jnp.bfloat16
NN = (((1,), (0,)), ((), ()))
NT = (((1,), (1,)), ((), ()))
TN = (((0,), (0,)), ((), ()))
MESH = pl.DeviceIdType.MESH


class Place:
    def __init__(self, packs, rows):
        self.packs, self.rows = packs, rows
        self.nx = rows // 2
        self.ny = self.nx if packs % self.nx == 0 else 1
        self.nz = packs // self.ny
        self.size = {"c": 2, "x": self.nx, "y": self.ny, "z": self.nz}

    def locate(self):
        self.p = lax.axis_index("pack")
        self.r = lax.axis_index("row")
        self.at = {
            "c": lax.rem(self.r, 2),
            "x": lax.div(self.r, 2),
            "y": lax.rem(self.p, self.ny),
            "z": lax.div(self.p, self.ny),
        }
        return self

    def device(self, **moved):
        at = {**self.at, **moved}
        return {"pack": at["z"] * self.ny + at["y"], "row": at["x"] * 2 + at["c"]}

    def other(self, dim, step):
        return lax.rem(self.at[dim] + step, self.size[dim])

    def peers(self, dim):
        found = []
        for step in range(1, self.size[dim]):
            there = self.other(dim, step)
            found.append((there, self.device(**{dim: there})))
        return found

    def row_peers(self):
        return [
            {"pack": self.p, "row": lax.rem(self.r + step, self.rows)} for step in range(1, self.rows)
        ]


class Mail:
    def __init__(self, send_sem, recv_sem):
        self.send_sem, self.recv_sem, self.sent = send_sem, recv_sem, []

    def put(self, source, target, device):
        index = len(self.sent)
        copy = pltpu.make_async_remote_copy(
            src_ref=source, dst_ref=target,
            send_sem=self.send_sem.at[index], recv_sem=self.recv_sem.at[index],
            device_id=device, device_id_type=MESH,
        )
        copy.start()
        self.sent.append(copy)
        return copy

    def finish(self):
        for copy in self.sent:
            copy.wait_send()


def greet(devices):
    barrier = pltpu.get_barrier_semaphore()
    for device in devices:
        pl.semaphore_signal(barrier, inc=1, device_id=device, device_id_type=MESH)
    pl.semaphore_wait(barrier, len(devices))


def reduce_plan(packs, rows, total_rows):
    place = Place(packs, rows)
    share = total_rows // (packs * rows)
    chunks = 5 if share % 80 == 0 else 1
    return place, share, chunks, share // chunks


def reduce_scratch(packs, rows, total_rows):
    place, share, chunks, size = reduce_plan(packs, rows, total_rows)
    nx, ny, nz = place.nx, place.ny, place.nz
    half = nx * ny * nz
    first, second = max(nx, ny), max(nx, ny)
    copies = chunks * (1 + (nx - 1) + (ny - 1) + (nz - 1) + rows - 1) + 1 + nx - 1 + ny - 1 + nz - 1
    return [
        pltpu.VMEM((chunks, half, size, 128), BF16),
        pltpu.VMEM((chunks, half, size, 128), BF16),
        pltpu.VMEM((chunks, half, size, 128), BF16),
        pltpu.VMEM((chunks, half, size, 128), BF16),
        pltpu.VMEM((chunks, half // min(nx, ny), size, 128), F32),
        pltpu.VMEM((chunks, half // min(nx, ny), size, 128), BF16),
        pltpu.VMEM((chunks, half // min(nx, ny), size, 128), BF16),
        pltpu.VMEM((chunks, nz, size, 128), F32),
        pltpu.VMEM((chunks, nz, size, 128), BF16),
        pltpu.VMEM((chunks, nz, size, 128), BF16),
        pltpu.VMEM((2, 32, 128), F32),
        pltpu.VMEM((nx, 32, 128), F32),
        pltpu.VMEM((ny, 32, 128), F32),
        pltpu.VMEM((nz, 32, 128), F32),
        pltpu.SemaphoreType.DMA((copies,)),
        pltpu.SemaphoreType.DMA((copies,)),
    ]


def reduce_kernel(
    packs, rows, grad_ref, vec_ref, out_ref, vec_out,
    stage0, recv0, stage1, recv1, kept1, stage2, recv2, kept2, stage3, recv3,
    vec_c, vec_x, vec_y, vec_z, send_sem, recv_sem,
):
    place, share, chunks, size = reduce_plan(packs, rows, grad_ref.shape[0])
    place.locate()
    mail = Mail(send_sem, recv_sem)
    at, nz = place.at, place.nz
    greet(
        place.row_peers()
        + [device for dim in ("y", "z") for _, device in place.peers(dim)]
    )

    def grad_rows(chunk, x, c, y, z):
        row = (z * place.ny + y) * (rows * share) + (x * 2 + c) * share + chunk * size
        return grad_ref[pl.ds(pl.multiple_of(row, 16), size), :]

    def order(chunk):
        return ("x", "y") if chunk % 2 == 0 else ("y", "x")

    def spot(chunk, one, two, z):
        return {order(chunk)[0]: one, order(chunk)[1]: two, "z": z}

    partner = place.peers("c")[0]
    hops0 = []
    for chunk in range(chunks):
        n1, n2 = [place.size[d] for d in order(chunk)]
        for one in range(n1):
            for two in range(n2):
                for z in range(nz):
                    piece = grad_rows(chunk, c=partner[0], **spot(chunk, one, two, z))
                    stage0[chunk, (one * n2 + two) * nz + z] = piece.astype(BF16)
        hops0.append(mail.put(stage0.at[chunk], recv0.at[chunk], partner[1]))

    def vec_step(dim, buffer, value):
        buffer[at[dim]] = value
        return [mail.put(buffer.at[at[dim]], buffer.at[at[dim]], device) for _, device in place.peers(dim)]

    def vec_sum(hops, buffer):
        for hop in hops:
            hop.wait_recv()
        total = buffer[0]
        for index in range(1, buffer.shape[0]):
            total = total + buffer[index]
        return total

    vec_hops = vec_step("c", vec_c, vec_ref[...])

    hops1 = []
    for chunk in range(chunks):
        n1, n2 = [place.size[d] for d in order(chunk)]
        hops0[chunk].wait_recv()
        for two in range(n2):
            for z in range(nz):
                slot = (at[order(chunk)[0]] * n2 + two) * nz + z
                kept1[chunk, two * nz + z] = (
                    grad_rows(chunk, c=at["c"], **spot(chunk, at[order(chunk)[0]], two, z))
                    + recv0[chunk, slot].astype(F32)
                )
        hops = []
        for step, (there, device) in enumerate(place.peers(order(chunk)[0])):
            for two in range(n2):
                for z in range(nz):
                    slot = (there * n2 + two) * nz + z
                    stage1[chunk, step * n2 * nz + two * nz + z] = (
                        grad_rows(chunk, c=at["c"], **spot(chunk, there, two, z))
                        + recv0[chunk, slot].astype(F32)
                    ).astype(BF16)
            part = pl.ds(step * n2 * nz, n2 * nz)
            hops.append(mail.put(stage1.at[chunk, part], recv1.at[chunk, part], device))
        hops1.append(hops)
    vec_hops = vec_step("x", vec_x, vec_sum(vec_hops, vec_c))

    hops2 = []
    for chunk in range(chunks):
        n1, n2 = [place.size[d] for d in order(chunk)]
        for hop in hops1[chunk]:
            hop.wait_recv()

        def summed(two, z):
            total = kept1[chunk, two * nz + z]
            for step in range(n1 - 1):
                total = total + recv1[chunk, step * n2 * nz + two * nz + z].astype(F32)
            return total

        hops = []
        for step, (there, device) in enumerate(place.peers(order(chunk)[1])):
            for z in range(nz):
                stage2[chunk, step * nz + z] = summed(there, z).astype(BF16)
            part = pl.ds(step * nz, nz)
            hops.append(mail.put(stage2.at[chunk, part], recv2.at[chunk, part], device))
        for z in range(nz):
            kept2[chunk, z] = summed(at[order(chunk)[1]], z)
        hops2.append(hops)
    vec_hops = vec_step("y", vec_y, vec_sum(vec_hops, vec_x))

    hops3 = []
    for chunk in range(chunks):
        n2 = place.size[order(chunk)[1]]
        for hop in hops2[chunk]:
            hop.wait_recv()

        def summed(z):
            total = kept2[chunk, z]
            for step in range(n2 - 1):
                total = total + recv2[chunk, step * nz + z].astype(F32)
            return total

        hops = []
        for step, (there, device) in enumerate(place.peers("z")):
            stage3[chunk, step] = summed(there).astype(BF16)
            hops.append(mail.put(stage3.at[chunk, step], recv3.at[chunk, step], device))
        kept2[chunk, at["z"]] = summed(at["z"])
        hops3.append(hops)
    vec_hops = vec_step("z", vec_z, vec_sum(vec_hops, vec_y))

    hops4 = []
    for chunk in range(chunks):
        total = kept2[chunk, at["z"]]
        for step, hop in enumerate(hops3[chunk]):
            hop.wait_recv()
            total = total + recv3[chunk, step].astype(F32)
        mine = pl.ds(pl.multiple_of(place.r * share + chunk * size, 16), size)
        out_ref[mine, :] = total.astype(BF16)
        for device in place.row_peers():
            hops4.append(mail.put(out_ref.at[mine], out_ref.at[mine], device))
    vec_out[...] = vec_sum(vec_hops, vec_z)
    for hop in hops4:
        hop.wait_recv()
    mail.finish()


def reduce_call(packs, rows, grad, vec):
    total_rows = grad.shape[0]
    vm = pl.BlockSpec(memory_space=pltpu.VMEM)
    out, vec_out = pl.pallas_call(
        functools.partial(reduce_kernel, packs, rows),
        out_shape=(
            jax.ShapeDtypeStruct((total_rows // packs, 128), BF16),
            jax.ShapeDtypeStruct((32, 128), F32),
        ),
        in_specs=[vm, vm],
        out_specs=(vm, vm),
        scratch_shapes=reduce_scratch(packs, rows, total_rows),
        compiler_params=pltpu.CompilerParams(
            collective_id=1, has_side_effects=True, vmem_limit_bytes=48 << 20
        ),
        name="reduce",
    )(grad, vec.reshape(32, 128))
    return out, vec_out.reshape(-1)


def dot(left, right, dims=NN):
    return lax.dot_general(left, right, dims, preferred_element_type=F32)


def split2(v):
    high = v.astype(BF16)
    return high, (v - high.astype(F32)).astype(BF16)


def split3(v):
    high = v.astype(BF16)
    rest = v - high.astype(F32)
    mid = rest.astype(BF16)
    return high, mid, (rest - mid.astype(F32)).astype(BF16)


def dot3(left, right, dims=NN):
    la, ra = dims[0][0][0], dims[0][1][0]
    lh, ll = split2(left)
    rh, rl = split2(right)
    return dot(jnp.concatenate([lh, ll, lh], la), jnp.concatenate([rh, rh, rl], ra), dims)


def dot6(left, right, dims=NN):
    la, ra = dims[0][0][0], dims[0][1][0]
    lh, lm, ll = split3(left)
    rh, rm, rl = split3(right)
    return dot(
        jnp.concatenate([lh, lh, lm, lm, lh, ll], la),
        jnp.concatenate([rh, rm, rh, rm, rl, rh], ra),
        dims,
    )


def eliminate(m_ref, qt_ref, count):
    sub = lax.broadcasted_iota(jnp.int32, (16, 128), 0)

    def panel(index, carry):
        base = pl.multiple_of(index * 16, 16)
        back = lax.rem(128 - base, 128)
        gram, rest = [], []
        for s in range(count):
            gram.append(pltpu.roll(m_ref[s, pl.ds(base, 16), :128], back, 1))
            rest.append(m_ref[s, pl.ds(base, 16), 128:])
        for j in range(16):
            for s in range(count):
                g, a = gram[s], rest[s]
                col = jnp.broadcast_to(g[:, j : j + 1], (16, 128))
                inv = lax.rsqrt(col[j : j + 1, :])
                row_g = g[j : j + 1, :] * inv
                row_a = a[j : j + 1, :] * inv
                factor = jnp.where(sub > j, col * inv, 0.0)
                gram[s] = jnp.where(sub == j, row_g, g - factor * row_g)
                rest[s] = jnp.where(sub == j, row_a, a - factor * row_a)
        for s in range(count):
            u = pltpu.roll(gram[s], base, 1)
            qt_ref[s, pl.ds(base, 16), :] = rest[s]
            uh, um, ul = split3(u)
            ah, am, al = split3(rest[s])
            wh, wm, wl = [jnp.concatenate(p, 1) for p in ((uh, ah), (um, am), (ul, al))]
            m_ref[s] -= dot(
                jnp.concatenate([uh, uh, um, um, uh, ul], 0),
                jnp.concatenate([wh, wm, wh, wm, wl, wh], 0),
                TN,
            )
        return carry

    lax.fori_loop(0, 8, panel, 0)


def soap_kernel(
    packs, row_count, blocks, slots,
    grad_ref, first_ref, second_ref, left_ref, right_ref, lbasis_ref, rbasis_ref, master_ref,
    first_out, second_out, master_out, copy_out, left_out, right_out, lbasis_out, rbasis_out,
    m_ref, qt_ref, q_ref, send_sem, recv_sem,
):
    place = Place(packs, row_count).locate()
    mail = Mail(send_sem, recv_sem)
    partner = place.peers("c")[0]
    across = place.peers("x")
    greet([partner[1]] + [device for _, device in across])
    me = place.r
    for s in range(slots):
        t = jnp.minimum(me * slots + s, 2 * blocks - 1)
        is_right = t >= blocks
        rows = pl.ds(pl.multiple_of(jnp.where(is_right, t - blocks, t) * 128, 128), 128)
        g = grad_ref[rows, :].astype(F32)
        g = jnp.where(is_right, g.T, g).astype(BF16)
        stat = jnp.where(is_right, right_ref[rows, :], left_ref[rows, :])
        basis = jnp.where(is_right, rbasis_ref[rows, :], lbasis_ref[rows, :])
        new = BETA_TWO * stat + (1.0 - BETA_TWO) * dot(g, g, NT)
        a = dot6(new, basis)
        at = a.T
        m_ref[s, :, :128] = dot6(at, a)
        m_ref[s, :, 128:] = at
    eliminate(m_ref, qt_ref, slots)

    def spot(row, s):
        return q_ref.at[pl.ds(pl.multiple_of((row * slots + s) * 128, 128), 128), :]

    hops_c, hops_x, hops_f = [], [], []
    for s in range(slots):
        q_ref[pl.ds(pl.multiple_of((me * slots + s) * 128, 128), 128), :] = qt_ref[s].T
        hops_x.append([mail.put(spot(me, s), spot(me, s), device) for _, device in across])
        hops_c.append(mail.put(spot(me, s), spot(me, s), partner[1]))

    def block_step(index, carry):
        rows = pl.ds(pl.multiple_of(index * 128, 128), 128)
        g = grad_ref[rows, :]
        left_out[rows, :] = BETA_TWO * left_ref[rows, :] + (1.0 - BETA_TWO) * dot(g, g, NT)
        right_out[rows, :] = BETA_TWO * right_ref[rows, :] + (1.0 - BETA_TWO) * dot(g, g, TN)
        lb, rb = lbasis_ref[rows, :], rbasis_ref[rows, :]
        lh, ll = split2(lb)
        turned = dot(jnp.concatenate([lh, ll], 0), jnp.concatenate([g, g], 0), TN)
        rotated = dot3(turned, rb)
        first = BETA_ONE * first_ref[rows, :] + (1.0 - BETA_ONE) * rotated
        second = BETA_TWO * second_ref[rows, :] + (1.0 - BETA_TWO) * rotated * rotated
        first_out[rows, :] = first
        second_out[rows, :] = second
        ratio = first / (1.0 - BETA_ONE**STEP) / (jnp.sqrt(second / (1.0 - BETA_TWO**STEP)) + EPSILON)
        stepped = dot3(dot3(lb, ratio), rb, NT)
        weights = master_ref[rows, :]
        weights = weights - LEARN_RATE * (stepped + WEIGHT_DECAY * weights)
        master_out[rows, :] = weights
        copy_out[rows, :] = weights.astype(BF16)
        return carry

    for s in range(slots):
        lax.fori_loop(blocks * s // slots, blocks * (s + 1) // slots, block_step, 0)
        for step, hop in enumerate(hops_x[s]):
            hop.wait_recv()
            source = lax.rem(place.at["x"] + place.nx - 1 - step, place.nx) * 2 + place.at["c"]
            hops_f.append(mail.put(spot(source, s), spot(source, s), partner[1]))
    for hop in hops_c + hops_f:
        hop.wait_recv()
    lbasis_out[...] = q_ref[: blocks * 128, :]
    rbasis_out[...] = q_ref[blocks * 128 : 2 * blocks * 128, :]
    mail.finish()


def soap_call(packs, row_count, grad, first, second, left, right, lbasis, rbasis, master):
    rows = grad.shape[0]
    blocks = rows // 128
    slots = -(-2 * blocks // row_count)
    full = jax.ShapeDtypeStruct((rows, 128), F32)
    vm = pl.BlockSpec(memory_space=pltpu.VMEM)
    copies = slots * row_count
    return pl.pallas_call(
        functools.partial(soap_kernel, packs, row_count, blocks, slots),
        out_shape=(full, full, full, jax.ShapeDtypeStruct((rows, 128), BF16), full, full, full, full),
        in_specs=[vm] * 8,
        out_specs=(vm,) * 8,
        scratch_shapes=[
            pltpu.VMEM((slots, 128, 256), F32),
            pltpu.VMEM((slots, 128, 128), F32),
            pltpu.VMEM((row_count * slots * 128, 128), F32),
            pltpu.SemaphoreType.DMA((copies,)),
            pltpu.SemaphoreType.DMA((copies,)),
        ],
        compiler_params=pltpu.CompilerParams(
            collective_id=2, has_side_effects=True, vmem_limit_bytes=40 << 20
        ),
        name="soap",
    )(grad, first, second, left, right, lbasis, rbasis, master)


def layer_norm(hidden, gain, offset):
    center = hidden - jnp.mean(hidden, axis=-1, keepdims=True)
    spread = jnp.mean(center * center, axis=-1, keepdims=True)
    return center * lax.rsqrt(spread + NORM_EPSILON) * gain + offset


def gelu_tanh(values):
    return jax.nn.gelu(values, approximate=True)


def sine_table(places, model_width):
    half_width = model_width // 2
    column = jnp.arange(half_width)
    period = 10000.0 ** ((2 * (column // 2)).astype(jnp.float32) / half_width)

    def embed_one(coordinate):
        angles = coordinate.astype(jnp.float32)[:, None] / period[None, :]
        return jnp.where(column[None, :] % 2 == 0, jnp.sin(angles), jnp.cos(angles))

    return jnp.concatenate([embed_one(places // IMG_W), embed_one(places % IMG_W)], axis=1)


def from_blocks(stack, row_count, col_count, block_size):
    shaped = stack.reshape(row_count // block_size, col_count // block_size, block_size, block_size)
    return shaped.transpose(0, 2, 1, 3).reshape(row_count, col_count)


def to_blocks(matrix, block_size):
    row_count, col_count = matrix.shape
    shaped = matrix.reshape(
        row_count // block_size, block_size, col_count // block_size, block_size
    )
    return shaped.transpose(0, 2, 1, 3).reshape(-1, block_size)


def split_weights(stack, model_width, hidden_width, block_size):
    square = model_width * model_width // block_size
    wide_rows = model_width * hidden_width // block_size
    bounds = [
        0,
        square,
        2 * square,
        3 * square,
        4 * square,
        4 * square + wide_rows,
        4 * square + 2 * wide_rows,
    ]
    shapes = [(model_width, model_width)] * 4 + [
        (model_width, hidden_width),
        (hidden_width, model_width),
    ]
    return [
        from_blocks(
            stack[bounds[number] : bounds[number + 1]],
            shapes[number][0],
            shapes[number][1],
            block_size,
        )
        for number in range(6)
    ]


def split_vectors(vector, model_width, hidden_width):
    lengths = [model_width] * 5 + [hidden_width] + [model_width] * 3
    pieces = []
    offset = 0
    for length in lengths:
        pieces.append(vector[offset : offset + length])
        offset = offset + length
    return pieces


def adam_vector(grad, vector, first, second):
    first_new = BETA_ONE * first + (1.0 - BETA_ONE) * grad
    second_new = BETA_TWO * second + (1.0 - BETA_TWO) * grad * grad
    ratio = (
        first_new
        / (1.0 - BETA_ONE**STEP)
        / (jnp.sqrt(second_new / (1.0 - BETA_TWO**STEP)) + EPSILON)
    )
    return (vector - LEARN_RATE * ratio, first_new, second_new)


def contract_rows(left, right):
    return jnp.einsum("ti,to->io", left, right, preferred_element_type=jnp.float32)


def project_back(grad, weight):
    return jnp.einsum("to,io->ti", grad, weight, preferred_element_type=jnp.float32)


def head_scores(queries, key_rows, allowed, columns, score_scale):
    scores = jnp.einsum(
        "qd,kd->qk", queries[:, columns], key_rows[:, columns], preferred_element_type=jnp.float32
    )
    return jnp.where(allowed, scores * score_scale, MASKED_SCORE)


def attend(queries, key_rows, value_rows, allowed, head_count, score_scale):
    head_width = queries.shape[1] // head_count
    pieces, totals = ([], [])
    for head_index in range(head_count):
        columns = slice(head_index * head_width, (head_index + 1) * head_width)
        scores = head_scores(queries, key_rows, allowed, columns, score_scale)
        largest = jnp.max(scores, axis=1, keepdims=True)
        weights = jnp.exp(scores - largest)
        summed = jnp.sum(weights, axis=1, keepdims=True)
        weights = (weights / summed).astype(jnp.bfloat16)
        pieces.append(jnp.dot(weights, value_rows[:, columns], preferred_element_type=jnp.float32))
        totals.append(largest + jnp.log(summed))
    return (jnp.concatenate(pieces, axis=1), totals)


def attend_back(queries, key_rows, value_rows, grad_out, allowed, totals, head_count, score_scale):
    head_width = queries.shape[1] // head_count
    query_parts, key_parts, value_parts, centers = ([], [], [], [])
    for head_index in range(head_count):
        columns = slice(head_index * head_width, (head_index + 1) * head_width)
        scores = head_scores(queries, key_rows, allowed, columns, score_scale)
        probs = jnp.exp(scores - totals[head_index])
        head_grad = grad_out[:, columns]
        along = jnp.einsum(
            "qd,kd->qk", head_grad, value_rows[:, columns], preferred_element_type=jnp.float32
        )
        center = jnp.sum(probs * along, axis=1, keepdims=True)
        centers.append(center)
        score_grad = (probs * (along - center) * score_scale).astype(jnp.bfloat16)
        query_parts.append(
            jnp.dot(score_grad, key_rows[:, columns], preferred_element_type=jnp.float32)
        )
        key_parts.append(
            jnp.einsum(
                "qk,qd->kd", score_grad, queries[:, columns], preferred_element_type=jnp.float32
            )
        )
        value_parts.append(
            jnp.einsum(
                "qk,qd->kd",
                probs.astype(jnp.bfloat16),
                head_grad,
                preferred_element_type=jnp.float32,
            )
        )
    query_grad = jnp.concatenate(query_parts, axis=1)
    return (
        query_grad,
        jnp.concatenate(key_parts, axis=1),
        jnp.concatenate(value_parts, axis=1),
        centers,
    )


def shards(
    tokens,
    cotangent,
    segment_ids,
    padding,
    master,
    moment_first,
    moment_second,
    stat_left,
    stat_right,
    basis_left,
    basis_right,
    vec_params,
    vec_first,
    vec_second,
):
    tok_rows, model_width = tokens.shape
    block_size = master.shape[1]
    owned_count = master.shape[0]
    hidden_width = vec_params.shape[0] - 8 * model_width
    score_scale = (model_width // HEADS) ** (-0.5)
    gathered = lax.all_gather(master.astype(jnp.bfloat16), "pack", axis=0, tiled=True)
    w_query, w_key, w_value, w_out, w_one, w_two = split_weights(
        gathered, model_width, hidden_width, block_size
    )
    (
        bias_query,
        bias_value,
        bias_out,
        gain_one,
        shift_one,
        bias_hidden,
        bias_two,
        gain_two,
        shift_two,
    ) = split_vectors(vec_params, model_width, hidden_width)
    code_rows = lax.all_gather(jnp.stack([segment_ids, padding]), "row", axis=1, tiled=True)
    key_ids = code_rows[0]
    key_padding = code_rows[1]
    starts = jnp.sum(key_ids[None, :] < segment_ids[:, None], axis=1)
    places = lax.axis_index("row") * tok_rows + jnp.arange(tok_rows, dtype=jnp.int32) - starts
    positions = sine_table(places, model_width)
    allowed = (segment_ids[:, None] == key_ids[None, :]) & (key_padding[None, :] == 0)
    with_place = (tokens + positions).astype(jnp.bfloat16)
    plain_rows = tokens.astype(jnp.bfloat16)
    queries = (
        jnp.dot(with_place, w_query, preferred_element_type=jnp.float32) + bias_query
    ).astype(jnp.bfloat16)
    key_rows = jnp.dot(with_place, w_key, preferred_element_type=jnp.float32).astype(jnp.bfloat16)
    value_rows = (
        jnp.dot(plain_rows, w_value, preferred_element_type=jnp.float32) + bias_value
    ).astype(jnp.bfloat16)
    key_all, value_all = (
        lax.all_gather(key_rows, "row", axis=0, tiled=True),
        lax.all_gather(value_rows, "row", axis=0, tiled=True),
    )
    attended, totals = attend(queries, key_all, value_all, allowed, HEADS, score_scale)
    attended = attended.astype(jnp.bfloat16)
    branch = jnp.dot(attended, w_out, preferred_element_type=jnp.float32) + bias_out
    normed, first_norm_back = jax.vjp(layer_norm, tokens + branch, gain_one, shift_one)
    normed_low = normed.astype(jnp.bfloat16)
    hidden_pre = jnp.dot(normed_low, w_one, preferred_element_type=jnp.float32) + bias_hidden
    activated, gelu_back = jax.vjp(gelu_tanh, hidden_pre)
    activated = activated.astype(jnp.bfloat16)
    second = jnp.dot(activated, w_two, preferred_element_type=jnp.float32) + bias_two
    layer_out, second_norm_back = jax.vjp(layer_norm, normed + second, gain_two, shift_two)
    sum_grad, grad_gain_two, grad_shift_two = second_norm_back(cotangent)
    second_grad = sum_grad.astype(jnp.bfloat16)
    grad_w_two = contract_rows(activated, second_grad)
    grad_bias_two = jnp.sum(second_grad.astype(jnp.float32), axis=0)
    (hidden_grad,) = gelu_back(project_back(second_grad, w_two))
    hidden_grad = hidden_grad.astype(jnp.bfloat16)
    grad_w_one = contract_rows(normed_low, hidden_grad)
    grad_bias_hidden = jnp.sum(hidden_grad.astype(jnp.float32), axis=0)
    normed_grad = sum_grad + project_back(hidden_grad, w_one)
    branch_grad, grad_gain_one, grad_shift_one = first_norm_back(normed_grad)
    branch_low = branch_grad.astype(jnp.bfloat16)
    grad_w_out = contract_rows(attended, branch_low)
    grad_bias_out = jnp.sum(branch_low.astype(jnp.float32), axis=0)
    attended_grad = project_back(branch_low, w_out).astype(jnp.bfloat16)
    query_grad, key_grad_all, value_grad_all, centers = attend_back(
        queries, key_all, value_all, attended_grad, allowed, totals, HEADS, score_scale
    )
    key_grad, value_grad = (
        lax.psum_scatter(key_grad_all, "row", scatter_dimension=0, tiled=True),
        lax.psum_scatter(value_grad_all, "row", scatter_dimension=0, tiled=True),
    )
    query_low = query_grad.astype(jnp.bfloat16)
    key_low = key_grad.astype(jnp.bfloat16)
    value_low = value_grad.astype(jnp.bfloat16)
    grad_w_query = contract_rows(with_place, query_low)
    grad_w_key = contract_rows(with_place, key_low)
    grad_w_value = contract_rows(plain_rows, value_low)
    grad_bias_query = jnp.sum(query_low.astype(jnp.float32), axis=0)
    grad_bias_value = jnp.sum(value_low.astype(jnp.float32), axis=0)
    input_grad = (
        branch_grad
        + project_back(query_low, w_query)
        + project_back(key_low, w_key)
        + project_back(value_low, w_value)
    )
    grad_stack = jnp.concatenate(
        [
            to_blocks(matrix, block_size)
            for matrix in (
                grad_w_query,
                grad_w_key,
                grad_w_value,
                grad_w_out,
                grad_w_one,
                grad_w_two,
            )
        ],
        axis=0,
    )
    grad_vector = jnp.concatenate(
        [
            grad_bias_query,
            grad_bias_value,
            grad_bias_out,
            grad_gain_one,
            grad_shift_one,
            grad_bias_hidden,
            grad_bias_two,
            grad_gain_two,
            grad_shift_two,
        ]
    )
    packs, row_count = lax.axis_size("pack"), lax.axis_size("row")
    owned, total_vector = reduce_call(packs, row_count, grad_stack, grad_vector)
    updated = soap_call(
        packs, row_count, owned, moment_first, moment_second, stat_left, stat_right,
        basis_left, basis_right, master,
    )
    vec_new, vec_first_new, vec_second_new = adam_vector(
        total_vector, vec_params, vec_first, vec_second
    )
    return (
        layer_out,
        input_grad,
        updated[0],
        updated[1],
        updated[2],
        updated[3],
        updated[4],
        updated[5],
        updated[6],
        updated[7],
        vec_new,
        vec_first_new,
        vec_second_new,
    )


def solution(mesh):
    placed = (
        P(("pack", "row"), None),
        P(("pack", "row"), None),
        P(("pack", "row")),
        P(("pack", "row")),
        P("pack", None),
        P("pack", None),
        P("pack", None),
        P("pack", None),
        P("pack", None),
        P("pack", None),
        P("pack", None),
        P(),
        P(),
        P(),
    )
    return jax.shard_map(
        shards,
        mesh=mesh,
        in_specs=placed,
        out_specs=(
            P(("pack", "row"), None),
            P(("pack", "row"), None),
            P("pack", None),
            P("pack", None),
            P("pack", None),
            P("pack", None),
            P("pack", None),
            P("pack", None),
            P("pack", None),
            P("pack", None),
            P(),
            P(),
            P(),
        ),
        check_vma=False,
    )
```

```python
import functools
import jax
import ml_dtypes
import numpy as np
import jax.numpy as jnp
from jax import lax
from jax.experimental import pallas as pl
from jax.experimental.pallas import tpu as pltpu
from jax.sharding import PartitionSpec as P

HEADS = 8
IMG_W = 32
MASKED_SCORE = -1e30
NORM_EPSILON = 1e-05
STEP = 10
BETA_ONE = 0.9
BETA_TWO = 0.95
LEARN_RATE = 0.25
WEIGHT_DECAY = 0.01
EPSILON = 1e-08
F32 = jnp.float32
BF16 = jnp.bfloat16
NN = (((1,), (0,)), ((), ()))
NT = (((1,), (1,)), ((), ()))
TN = (((0,), (0,)), ((), ()))
MESH = pl.DeviceIdType.MESH


class Place:
    def __init__(self, packs, rows):
        self.packs, self.rows = packs, rows
        self.nx = rows // 2
        self.ny = self.nx if packs % self.nx == 0 else 1
        self.nz = packs // self.ny
        self.size = {"c": 2, "x": self.nx, "y": self.ny, "z": self.nz}

    def locate(self):
        self.p = lax.axis_index("pack")
        self.r = lax.axis_index("row")
        self.at = {
            "c": lax.rem(self.r, 2),
            "x": lax.div(self.r, 2),
            "y": lax.rem(self.p, self.ny),
            "z": lax.div(self.p, self.ny),
        }
        return self

    def device(self, **moved):
        at = {**self.at, **moved}
        return {"pack": at["z"] * self.ny + at["y"], "row": at["x"] * 2 + at["c"]}

    def other(self, dim, step):
        return lax.rem(self.at[dim] + step, self.size[dim])

    def peers(self, dim):
        found = []
        for step in range(1, self.size[dim]):
            there = self.other(dim, step)
            found.append((there, self.device(**{dim: there})))
        return found

    def row_peers(self):
        return [
            {"pack": self.p, "row": lax.rem(self.r + step, self.rows)} for step in range(1, self.rows)
        ]


class Mail:
    def __init__(self, send_sem, recv_sem):
        self.send_sem, self.recv_sem, self.sent = send_sem, recv_sem, []

    def put(self, source, target, device):
        index = len(self.sent)
        copy = pltpu.make_async_remote_copy(
            src_ref=source, dst_ref=target,
            send_sem=self.send_sem.at[index], recv_sem=self.recv_sem.at[index],
            device_id=device, device_id_type=MESH,
        )
        copy.start()
        self.sent.append(copy)
        return copy

    def finish(self):
        for copy in self.sent:
            copy.wait_send()


def greet(devices):
    barrier = pltpu.get_barrier_semaphore()
    for device in devices:
        pl.semaphore_signal(barrier, inc=1, device_id=device, device_id_type=MESH)
    pl.semaphore_wait(barrier, len(devices))


def reduce_plan(packs, rows, total_rows):
    place = Place(packs, rows)
    share = total_rows // (packs * rows)
    chunks = 5 if share % 80 == 0 else 1
    return place, share, chunks, share // chunks


def reduce_scratch(packs, rows, total_rows):
    place, share, chunks, size = reduce_plan(packs, rows, total_rows)
    nx, ny, nz = place.nx, place.ny, place.nz
    half = nx * ny * nz
    first, second = max(nx, ny), max(nx, ny)
    copies = chunks * (1 + (nx - 1) + (ny - 1) + (nz - 1) + rows - 1) + 1 + nx - 1 + ny - 1 + nz - 1
    return [
        pltpu.VMEM((chunks, half, size, 128), BF16),
        pltpu.VMEM((chunks, half, size, 128), BF16),
        pltpu.VMEM((chunks, half, size, 128), BF16),
        pltpu.VMEM((chunks, half, size, 128), BF16),
        pltpu.VMEM((chunks, half // min(nx, ny), size, 128), F32),
        pltpu.VMEM((chunks, half // min(nx, ny), size, 128), BF16),
        pltpu.VMEM((chunks, half // min(nx, ny), size, 128), BF16),
        pltpu.VMEM((chunks, nz, size, 128), F32),
        pltpu.VMEM((chunks, nz, size, 128), BF16),
        pltpu.VMEM((chunks, nz, size, 128), BF16),
        pltpu.VMEM((2, 32, 128), F32),
        pltpu.VMEM((nx, 32, 128), F32),
        pltpu.VMEM((ny, 32, 128), F32),
        pltpu.VMEM((nz, 32, 128), F32),
        pltpu.SemaphoreType.DMA((copies,)),
        pltpu.SemaphoreType.DMA((copies,)),
    ]


def reduce_kernel(
    packs, rows, early_ref, late_ref, vec_ref, out_ref, vec_out,
    grad_ref, stage0, recv0, stage1, recv1, kept1, stage2, recv2, kept2, stage3, recv3,
    vec_c, vec_x, vec_y, vec_z, send_sem, recv_sem, load_sem,
):
    early = early_ref.shape[0]
    loads = [
        pltpu.make_async_copy(early_ref, grad_ref.at[:early], load_sem.at[0]),
        pltpu.make_async_copy(late_ref, grad_ref.at[early:], load_sem.at[1]),
    ]
    for load in loads:
        load.start()
    place, share, chunks, size = reduce_plan(packs, rows, grad_ref.shape[0])
    place.locate()
    mail = Mail(send_sem, recv_sem)
    at, nz = place.at, place.nz
    greet(
        place.row_peers()
        + [device for dim in ("y", "z") for _, device in place.peers(dim)]
    )
    for load in loads:
        load.wait()

    def grad_rows(chunk, x, c, y, z):
        row = (z * place.ny + y) * (rows * share) + (x * 2 + c) * share + chunk * size
        return grad_ref[pl.ds(pl.multiple_of(row, 16), size), :]

    def order(chunk):
        return ("x", "y") if chunk % 2 == 0 else ("y", "x")

    def spot(chunk, one, two, z):
        return {order(chunk)[0]: one, order(chunk)[1]: two, "z": z}

    partner = place.peers("c")[0]
    hops0 = []
    for chunk in range(chunks):
        n1, n2 = [place.size[d] for d in order(chunk)]
        for one in range(n1):
            for two in range(n2):
                for z in range(nz):
                    piece = grad_rows(chunk, c=partner[0], **spot(chunk, one, two, z))
                    stage0[chunk, (one * n2 + two) * nz + z] = piece.astype(BF16)
        hops0.append(mail.put(stage0.at[chunk], recv0.at[chunk], partner[1]))

    def vec_step(dim, buffer, value):
        buffer[at[dim]] = value
        return [mail.put(buffer.at[at[dim]], buffer.at[at[dim]], device) for _, device in place.peers(dim)]

    def vec_sum(hops, buffer):
        for hop in hops:
            hop.wait_recv()
        total = buffer[0]
        for index in range(1, buffer.shape[0]):
            total = total + buffer[index]
        return total

    vec_hops = vec_step("c", vec_c, vec_ref[...])

    hops1 = []
    for chunk in range(chunks):
        n1, n2 = [place.size[d] for d in order(chunk)]
        hops0[chunk].wait_recv()
        for two in range(n2):
            for z in range(nz):
                slot = (at[order(chunk)[0]] * n2 + two) * nz + z
                kept1[chunk, two * nz + z] = (
                    grad_rows(chunk, c=at["c"], **spot(chunk, at[order(chunk)[0]], two, z))
                    + recv0[chunk, slot].astype(F32)
                )
        hops = []
        for step, (there, device) in enumerate(place.peers(order(chunk)[0])):
            for two in range(n2):
                for z in range(nz):
                    slot = (there * n2 + two) * nz + z
                    stage1[chunk, step * n2 * nz + two * nz + z] = (
                        grad_rows(chunk, c=at["c"], **spot(chunk, there, two, z))
                        + recv0[chunk, slot].astype(F32)
                    ).astype(BF16)
            part = pl.ds(step * n2 * nz, n2 * nz)
            hops.append(mail.put(stage1.at[chunk, part], recv1.at[chunk, part], device))
        hops1.append(hops)
    vec_hops = vec_step("x", vec_x, vec_sum(vec_hops, vec_c))

    hops2 = []
    for chunk in range(chunks):
        n1, n2 = [place.size[d] for d in order(chunk)]
        for hop in hops1[chunk]:
            hop.wait_recv()

        def summed(two, z):
            total = kept1[chunk, two * nz + z]
            for step in range(n1 - 1):
                total = total + recv1[chunk, step * n2 * nz + two * nz + z].astype(F32)
            return total

        hops = []
        for step, (there, device) in enumerate(place.peers(order(chunk)[1])):
            for z in range(nz):
                stage2[chunk, step * nz + z] = summed(there, z).astype(BF16)
            part = pl.ds(step * nz, nz)
            hops.append(mail.put(stage2.at[chunk, part], recv2.at[chunk, part], device))
        for z in range(nz):
            kept2[chunk, z] = summed(at[order(chunk)[1]], z)
        hops2.append(hops)
    vec_hops = vec_step("y", vec_y, vec_sum(vec_hops, vec_x))

    hops3 = []
    for chunk in range(chunks):
        n2 = place.size[order(chunk)[1]]
        for hop in hops2[chunk]:
            hop.wait_recv()

        def summed(z):
            total = kept2[chunk, z]
            for step in range(n2 - 1):
                total = total + recv2[chunk, step * nz + z].astype(F32)
            return total

        hops = []
        for step, (there, device) in enumerate(place.peers("z")):
            stage3[chunk, step] = summed(there).astype(BF16)
            hops.append(mail.put(stage3.at[chunk, step], recv3.at[chunk, step], device))
        kept2[chunk, at["z"]] = summed(at["z"])
        hops3.append(hops)
    vec_hops = vec_step("z", vec_z, vec_sum(vec_hops, vec_y))

    hops4 = []
    for chunk in range(chunks):
        total = kept2[chunk, at["z"]]
        for step, hop in enumerate(hops3[chunk]):
            hop.wait_recv()
            total = total + recv3[chunk, step].astype(F32)
        mine = pl.ds(pl.multiple_of(place.r * share + chunk * size, 16), size)
        out_ref[mine, :] = total.astype(BF16)
        for device in place.row_peers():
            hops4.append(mail.put(out_ref.at[mine], out_ref.at[mine], device))
    vec_out[...] = vec_sum(vec_hops, vec_z)
    for hop in hops4:
        hop.wait_recv()
    mail.finish()


def reduce_call(packs, rows, early, late, vec):
    total_rows = early.shape[0] + late.shape[0]
    vm = pl.BlockSpec(memory_space=pltpu.VMEM)
    hbm = pl.BlockSpec(memory_space=pl.ANY)
    out, vec_out = pl.pallas_call(
        functools.partial(reduce_kernel, packs, rows),
        out_shape=(
            jax.ShapeDtypeStruct((total_rows // packs, 128), BF16),
            jax.ShapeDtypeStruct((32, 128), F32),
        ),
        in_specs=[hbm, hbm, vm],
        out_specs=(vm, vm),
        scratch_shapes=[pltpu.VMEM((total_rows, 128), F32)]
        + reduce_scratch(packs, rows, total_rows)
        + [pltpu.SemaphoreType.DMA((2,))],
        compiler_params=pltpu.CompilerParams(
            collective_id=1, has_side_effects=True, vmem_limit_bytes=48 << 20
        ),
        name="reduce",
    )(early, late, vec)
    return out, vec_out.reshape(-1)


def dot(left, right, dims=NN):
    return lax.dot_general(left, right, dims, preferred_element_type=F32)


def split2(v):
    high = v.astype(BF16)
    return high, (v - high.astype(F32)).astype(BF16)


def split3(v):
    high = v.astype(BF16)
    rest = v - high.astype(F32)
    mid = rest.astype(BF16)
    return high, mid, (rest - mid.astype(F32)).astype(BF16)


def dot3(left, right, dims=NN):
    la, ra = dims[0][0][0], dims[0][1][0]
    lh, ll = split2(left)
    rh, rl = split2(right)
    return dot(jnp.concatenate([lh, ll, lh], la), jnp.concatenate([rh, rh, rl], ra), dims)


def dot6(left, right, dims=NN):
    la, ra = dims[0][0][0], dims[0][1][0]
    lh, lm, ll = split3(left)
    rh, rm, rl = split3(right)
    return dot(
        jnp.concatenate([lh, lh, lm, lm, lh, ll], la),
        jnp.concatenate([rh, rm, rh, rm, rl, rh], ra),
        dims,
    )


def eliminate(m_ref, qt_ref, count):
    sub = lax.broadcasted_iota(jnp.int32, (16, 128), 0)

    def panel(index, carry):
        base = pl.multiple_of(index * 16, 16)
        back = lax.rem(128 - base, 128)
        gram, rest = [], []
        for s in range(count):
            gram.append(pltpu.roll(m_ref[s, pl.ds(base, 16), :128], back, 1))
            rest.append(m_ref[s, pl.ds(base, 16), 128:])
        for j in range(16):
            for s in range(count):
                g, a = gram[s], rest[s]
                col = jnp.broadcast_to(g[:, j : j + 1], (16, 128))
                inv = lax.rsqrt(col[j : j + 1, :])
                row_g = g[j : j + 1, :] * inv
                row_a = a[j : j + 1, :] * inv
                factor = jnp.where(sub > j, col * inv, 0.0)
                gram[s] = jnp.where(sub == j, row_g, g - factor * row_g)
                rest[s] = jnp.where(sub == j, row_a, a - factor * row_a)
        for s in range(count):
            u = pltpu.roll(gram[s], base, 1)
            qt_ref[s, pl.ds(base, 16), :] = rest[s]
            uh, um, ul = split3(u)
            ah, am, al = split3(rest[s])
            wh, wm, wl = [jnp.concatenate(p, 1) for p in ((uh, ah), (um, am), (ul, al))]
            m_ref[s] -= dot(
                jnp.concatenate([uh, uh, um, um, uh, ul], 0),
                jnp.concatenate([wh, wm, wh, wm, wl, wh], 0),
                TN,
            )
        return carry

    lax.fori_loop(0, 8, panel, 0)


def soap_kernel(
    packs, row_count, blocks, slots,
    grad_ref, first_ref, second_ref, left_ref, right_ref, lbasis_ref, rbasis_ref, master_ref,
    first_out, second_out, master_out, copy_out, left_out, right_out, lbasis_out, rbasis_out,
    m_ref, qt_ref, q_ref, send_sem, recv_sem,
):
    place = Place(packs, row_count).locate()
    mail = Mail(send_sem, recv_sem)
    partner = place.peers("c")[0]
    across = place.peers("x")
    greet([partner[1]] + [device for _, device in across])
    me = place.r
    for s in range(slots):
        t = jnp.minimum(me * slots + s, 2 * blocks - 1)
        is_right = t >= blocks
        rows = pl.ds(pl.multiple_of(jnp.where(is_right, t - blocks, t) * 128, 128), 128)
        g = grad_ref[rows, :].astype(F32)
        g = jnp.where(is_right, g.T, g).astype(BF16)
        stat = jnp.where(is_right, right_ref[rows, :], left_ref[rows, :])
        basis = jnp.where(is_right, rbasis_ref[rows, :], lbasis_ref[rows, :])
        new = BETA_TWO * stat + (1.0 - BETA_TWO) * dot(g, g, NT)
        a = dot6(new, basis)
        at = a.T
        m_ref[s, :, :128] = dot6(at, a)
        m_ref[s, :, 128:] = at
    eliminate(m_ref, qt_ref, slots)

    def spot(row, s):
        return q_ref.at[pl.ds(pl.multiple_of((row * slots + s) * 128, 128), 128), :]

    hops_c, hops_x, hops_f = [], [], []
    for s in range(slots):
        q_ref[pl.ds(pl.multiple_of((me * slots + s) * 128, 128), 128), :] = qt_ref[s].T
        hops_x.append([mail.put(spot(me, s), spot(me, s), device) for _, device in across])
        hops_c.append(mail.put(spot(me, s), spot(me, s), partner[1]))

    def block_step(index, carry):
        rows = pl.ds(pl.multiple_of(index * 128, 128), 128)
        g = grad_ref[rows, :]
        left_out[rows, :] = BETA_TWO * left_ref[rows, :] + (1.0 - BETA_TWO) * dot(g, g, NT)
        right_out[rows, :] = BETA_TWO * right_ref[rows, :] + (1.0 - BETA_TWO) * dot(g, g, TN)
        lb, rb = lbasis_ref[rows, :], rbasis_ref[rows, :]
        lh, ll = split2(lb)
        turned = dot(jnp.concatenate([lh, ll], 0), jnp.concatenate([g, g], 0), TN)
        rotated = dot3(turned, rb)
        first = BETA_ONE * first_ref[rows, :] + (1.0 - BETA_ONE) * rotated
        second = BETA_TWO * second_ref[rows, :] + (1.0 - BETA_TWO) * rotated * rotated
        first_out[rows, :] = first
        second_out[rows, :] = second
        ratio = first / (1.0 - BETA_ONE**STEP) / (jnp.sqrt(second / (1.0 - BETA_TWO**STEP)) + EPSILON)
        stepped = dot3(dot3(lb, ratio), rb, NT)
        weights = master_ref[rows, :]
        weights = weights - LEARN_RATE * (stepped + WEIGHT_DECAY * weights)
        master_out[rows, :] = weights
        copy_out[rows, :] = weights.astype(BF16)
        return carry

    for s in range(slots):
        lax.fori_loop(blocks * s // slots, blocks * (s + 1) // slots, block_step, 0)
        for step, hop in enumerate(hops_x[s]):
            hop.wait_recv()
            source = lax.rem(place.at["x"] + place.nx - 1 - step, place.nx) * 2 + place.at["c"]
            hops_f.append(mail.put(spot(source, s), spot(source, s), partner[1]))
    for hop in hops_c + hops_f:
        hop.wait_recv()
    lbasis_out[...] = q_ref[: blocks * 128, :]
    rbasis_out[...] = q_ref[blocks * 128 : 2 * blocks * 128, :]
    mail.finish()


def soap_call(packs, row_count, grad, first, second, left, right, lbasis, rbasis, master):
    rows = grad.shape[0]
    blocks = rows // 128
    slots = -(-2 * blocks // row_count)
    full = jax.ShapeDtypeStruct((rows, 128), F32)
    vm = pl.BlockSpec(memory_space=pltpu.VMEM)
    copies = slots * row_count
    return pl.pallas_call(
        functools.partial(soap_kernel, packs, row_count, blocks, slots),
        out_shape=(full, full, full, jax.ShapeDtypeStruct((rows, 128), BF16), full, full, full, full),
        in_specs=[vm] * 8,
        out_specs=(vm,) * 8,
        scratch_shapes=[
            pltpu.VMEM((slots, 128, 256), F32),
            pltpu.VMEM((slots, 128, 128), F32),
            pltpu.VMEM((row_count * slots * 128, 128), F32),
            pltpu.SemaphoreType.DMA((copies,)),
            pltpu.SemaphoreType.DMA((copies,)),
        ],
        compiler_params=pltpu.CompilerParams(
            collective_id=2, has_side_effects=True, vmem_limit_bytes=40 << 20
        ),
        name="soap",
    )(grad, first, second, left, right, lbasis, rbasis, master)


def flat_rows(ref, count):
    return jnp.concatenate([ref[i : i + 1, :] for i in range(count)], 1)


def blocks_of(ref, first, down, across, stride):
    lines = []
    for i in range(down):
        row = [ref[pl.ds((first + i * stride + j) * 128, 128), :] for j in range(across)]
        lines.append(row[0] if across == 1 else jnp.concatenate(row, 1))
    return lines[0] if down == 1 else jnp.concatenate(lines, 0)


def gather_kernel(
    packs, rows, tokens_ref, codes_ref, master_ref, tokens_out, codes_out, weights_out, send_sem, recv_sem
):
    place = Place(packs, rows).locate()
    mail = Mail(send_sem, recv_sem)
    at = place.at
    owned = master_ref.shape[0]
    half = owned // 2
    partner = place.peers("c")[0][1]
    greet(place.row_peers() + [device for dim in ("y", "z") for _, device in place.peers(dim)])
    hops_x = [mail.put(tokens_ref, tokens_out.at[place.r], device) for _, device in place.peers("x")]
    hops = [mail.put(codes_ref, codes_out.at[place.r], device) for device in place.row_peers()]
    hops.append(mail.put(tokens_ref, tokens_out.at[place.r], partner))
    own = pl.ds(pl.multiple_of(place.p * owned, 16), owned)
    weights_out[own, :] = master_ref[...].astype(BF16)

    def piece(z, y):
        start = (z * place.ny + y) * owned + at["c"] * half
        return weights_out.at[pl.ds(pl.multiple_of(start, 16), half), :]

    def source(dim, step):
        return lax.rem(at[dim] + place.size[dim] - 1 - step, place.size[dim])

    mine = piece(at["z"], at["y"])
    hops_z = [mail.put(mine, mine, device) for _, device in place.peers("z")]
    hops_y = [(at["z"], [mail.put(mine, mine, device) for _, device in place.peers("y")])]
    tokens_out[place.r] = tokens_ref[...]
    codes_out[place.r] = codes_ref[...]
    for step, hop in enumerate(hops_z):
        hop.wait_recv()
        z = source("z", step)
        part = piece(z, at["y"])
        hops_y.append((z, [mail.put(part, part, device) for _, device in place.peers("y")]))
        hops.append(mail.put(part, part, partner))
    for step, hop in enumerate(hops_x):
        hop.wait_recv()
        row = source("x", step) * 2 + at["c"]
        hops.append(mail.put(tokens_out.at[row], tokens_out.at[row], partner))
    for z, found in hops_y:
        for step, hop in enumerate(found):
            hop.wait_recv()
            part = piece(z, source("y", step))
            hops.append(mail.put(part, part, partner))
    for hop in hops:
        hop.wait_recv()
    mail.finish()


def gather_call(packs, rows, tokens, codes, master):
    vm = pl.BlockSpec(memory_space=pltpu.VMEM)
    place = Place(packs, rows)
    nx, ny, nz = place.nx, place.ny, place.nz
    copies = 2 * (nx - 1) + rows + 2 * (nz - 1) + 2 * nz * (ny - 1)
    return pl.pallas_call(
        functools.partial(gather_kernel, packs, rows),
        out_shape=(
            jax.ShapeDtypeStruct((rows,) + tokens.shape, F32),
            jax.ShapeDtypeStruct((rows,) + codes.shape, jnp.int32),
            jax.ShapeDtypeStruct((packs * master.shape[0], 128), BF16),
        ),
        in_specs=[vm] * 3,
        out_specs=(vm,) * 3,
        scratch_shapes=[pltpu.SemaphoreType.DMA((copies,)), pltpu.SemaphoreType.DMA((copies,))],
        compiler_params=pltpu.CompilerParams(collective_id=3, has_side_effects=True, vmem_limit_bytes=32 << 20),
        name="gather",
    )(tokens, codes, master)


TILE = 256
LOG2E = 1.4426950408889634


def sine_rows(pack_len, half):
    column = np.arange(half)
    period = np.float32(10000.0) ** ((2 * (column // 2)).astype(np.float32) / np.float32(half))
    high = pack_len // IMG_W
    angles = np.arange(max(high, IMG_W)).astype(np.float32)[:, None] / period[None, :].astype(np.float32)
    angles = angles.astype(np.float64)
    table = np.where(column[None, :] % 2 == 0, np.sin(angles), np.cos(angles)).astype(np.float32)
    both = np.zeros((high + IMG_W, 2 * half), np.float32)
    both[:high, :half] = table[:high]
    both[high:, half:] = table[:IMG_W]
    pieces, rest = [], both
    for _ in range(3):
        piece = rest.astype(ml_dtypes.bfloat16)
        pieces.append(piece)
        rest = rest - piece.astype(np.float32)
    return np.concatenate(pieces, 0)


def attend_kernel(
    packs, rows, tokens_ref, codes_ref, all_ref, vec_ref, table_ref,
    att_out, place_out, kf_out, qf_out, vf_out, kt_out, q_out, ot_out,
    vt_ref, post_ref, weights_ref, send_sem, recv_sem, load_sem,
):
    load = pltpu.make_async_copy(all_ref.at[: weights_ref.shape[0]], weights_ref, load_sem)
    load.start()
    place = Place(packs, rows).locate()
    me = place.r
    _, tok, width = tokens_ref.shape
    heads = HEADS // rows
    part = width // rows
    head = part // heads
    groups = tok // 128
    high = rows * tok // IMG_W
    greet(place.row_peers())

    ids, pad = codes_ref[:, :groups, :], codes_ref[:, groups:, :]
    index = (
        lax.broadcasted_iota(jnp.int32, ids.shape, 0) * tok
        + lax.broadcasted_iota(jnp.int32, ids.shape, 1) * 128
        + lax.broadcasted_iota(jnp.int32, ids.shape, 2)
    )
    starts = jnp.zeros(ids.shape, jnp.int32)
    for image in range(8):
        count = jnp.sum(jnp.where(ids == image, 1.0, 0.0)).astype(jnp.int32)
        starts = starts + jnp.where(ids > image, count, 0)
    places = index - starts
    down = lax.div(places, IMG_W)
    right = places - down * IMG_W

    def line(values, r):
        return jnp.concatenate([values[r, g : g + 1, :] for g in range(groups)], 1)

    load.wait()
    pick = (
        lax.broadcasted_iota(jnp.int32, (width, part), 0)
        == lax.broadcasted_iota(jnp.int32, (width, part), 1) + me * part
    )
    pick = jnp.where(pick, 1.0, 0.0).astype(BF16)
    square = (width // 128) ** 2
    wq, wk, wv = [
        dot(blocks_of(weights_ref, n * square, width // 128, width // 128, width // 128), pick).astype(BF16)
        for n in range(3)
    ]
    lines = width // 128

    def bias(first):
        row = jnp.concatenate([vec_ref[first + i : first + i + 1, :] for i in range(lines)], 1)
        row = jnp.broadcast_to(row, (8, width))
        return pltpu.roll(row, lax.rem(width - me * part, width), 1)[:1, :part]

    bias_q, bias_v = bias(0), bias(lines)
    scale = LOG2E * head**-0.5
    sub8 = lax.broadcasted_iota(jnp.int32, (8, tok), 0)
    for r in range(rows):
        span = slice(r * tok, (r + 1) * tok)
        sub = lax.broadcasted_iota(jnp.int32, (high, tok), 0)
        hot = jnp.concatenate(
            [
                jnp.where(sub == line(down, r), 1.0, 0.0),
                jnp.where(sub[:IMG_W] == line(right, r), 1.0, 0.0),
            ],
            0,
        ).astype(BF16)
        positions = dot(jnp.concatenate([hot] * 3, 0), table_ref[...], TN)
        rows_in = tokens_ref[r]
        placed = (rows_in + positions).astype(BF16)
        place_out[span, :] = placed
        q = (dot(placed, wq) + bias_q).astype(BF16)
        k = dot(placed, wk).astype(BF16)
        v = (dot(rows_in.astype(BF16), wv) + bias_v).astype(BF16)
        q_out[span, :] = q
        qt, kt, vt = q.astype(F32).T, k.astype(F32).T, v.astype(F32).T
        kt_out[:, span] = kt.astype(BF16)
        vt_ref[:, span] = vt.astype(BF16)
        scaled = qt * scale
        q_high = scaled.astype(BF16).astype(F32)
        q_low = scaled - q_high
        same = sub8 == line(ids, r)
        ones = jnp.ones((8, tok), F32)
        free = jnp.zeros((128 - 2 * head - 8, tok), F32)
        barred = jnp.where(same & (line(pad, r) == 0), 0.0, MASKED_SCORE)
        for h in range(heads):
            own = slice(h * head, (h + 1) * head)
            qf_out[h, :, span] = jnp.concatenate(
                [q_high[own], q_low[own], jnp.where(same, 1.0, 0.0), free], 0
            ).astype(BF16)
            kf = jnp.concatenate([kt[own], kt[own], barred, ones, free[8:]], 0)
            kf_out[h, span, :] = kf.T.astype(BF16)
            vf = jnp.concatenate([vt[own], vt[own], ones, free], 0)
            vf_out[h, span, :] = vf.T.astype(BF16)

    def post(step):
        return pltpu.make_async_remote_copy(
            src_ref=post_ref.at[step], dst_ref=att_out.at[me],
            send_sem=send_sem.at[step], recv_sem=recv_sem.at[step],
            device_id={"pack": place.p, "row": lax.rem(me + 1 + step, rows)}, device_id_type=MESH,
        )

    def tile_step(number, carry):
        step = lax.div(number, tok // TILE)
        inner = lax.rem(number, tok // TILE)
        dest = lax.rem(me + 1 + step, rows)
        span = pl.ds(pl.multiple_of(dest * tok + inner * TILE, TILE), TILE)
        pieces = []
        for h in range(heads):
            scores = dot(kf_out[h], qf_out[h, :, span])
            largest = jnp.max(scores, axis=0, keepdims=True)
            weights = jnp.exp2(scores - largest)
            total = jnp.sum(weights, axis=0, keepdims=True)
            piece = dot(vt_ref[h * head : (h + 1) * head, :], weights.astype(BF16))
            pieces.append(piece * (1.0 / total))
            lse = -(largest + jnp.log2(total))
            lh = lse.astype(BF16).astype(F32)
            lm = (lse - lh).astype(BF16).astype(F32)
            tail = qf_out[h, 2 * head : 2 * head + 16, span].astype(F32)
            tail = jnp.concatenate([tail[:8], lh, lm, lse - lh - lm, jnp.zeros((5, TILE), F32)], 0)
            qf_out[h, 2 * head : 2 * head + 16, span] = tail.astype(BF16)
        out = pieces[0] if heads == 1 else jnp.concatenate(pieces, 0)
        ot_out[:, span] = out
        post_ref[step, :, pl.ds(pl.multiple_of(inner * TILE, TILE), TILE)] = out.astype(BF16)

        @pl.when((inner == tok // TILE - 1) & (step < rows - 1))
        def _():
            post(step).start()

        return carry

    lax.fori_loop(0, rows * (tok // TILE), tile_step, 0)
    att_out[me] = post_ref[rows - 1]
    for step in range(rows - 1):
        post(step).wait_recv()
    for step in range(rows - 1):
        post(step).wait_send()


def attend_call(packs, rows, tokens_all, codes_all, weights, vec):
    vm = pl.BlockSpec(memory_space=pltpu.VMEM)
    _, tok, width = tokens_all.shape
    pack_len = rows * tok
    heads, part = HEADS // rows, width // rows
    table = jnp.asarray(sine_rows(pack_len, width // 2))
    used = 3 * width * width // 128
    return pl.pallas_call(
        functools.partial(attend_kernel, packs, rows),
        out_shape=(
            jax.ShapeDtypeStruct((rows, part, tok), BF16),
            jax.ShapeDtypeStruct((pack_len, width), BF16),
            jax.ShapeDtypeStruct((heads, pack_len, 128), BF16),
            jax.ShapeDtypeStruct((heads, 128, pack_len), BF16),
            jax.ShapeDtypeStruct((heads, pack_len, 128), BF16),
            jax.ShapeDtypeStruct((part, pack_len), BF16),
            jax.ShapeDtypeStruct((pack_len, part), BF16),
            jax.ShapeDtypeStruct((part, pack_len), F32),
        ),
        in_specs=[vm, vm, pl.BlockSpec(memory_space=pl.ANY), vm, vm],
        out_specs=(vm,) * 8,
        scratch_shapes=[
            pltpu.VMEM((part, pack_len), BF16),
            pltpu.VMEM((rows, part, tok), BF16),
            pltpu.VMEM((used, 128), BF16),
            pltpu.SemaphoreType.DMA((rows,)),
            pltpu.SemaphoreType.DMA((rows,)),
            pltpu.SemaphoreType.DMA,
        ],
        compiler_params=pltpu.CompilerParams(collective_id=4, has_side_effects=True, vmem_limit_bytes=56 << 20),
        name="attend",
    )(tokens_all, codes_all, weights, vec, table)


def norm_forward(hidden):
    center = hidden - jnp.mean(hidden, axis=-1, keepdims=True)
    scale = lax.rsqrt(jnp.mean(center * center, axis=-1, keepdims=True) + NORM_EPSILON)
    return center * scale, scale


def norm_backward(grad, gain, unit, scale):
    inner = grad * gain
    mean = jnp.mean(inner, axis=-1, keepdims=True)
    along = jnp.mean(inner * unit, axis=-1, keepdims=True)
    return scale * (inner - mean - unit * along)


def column_sum(values):
    return jnp.sum(values, axis=0, keepdims=True)


def middle_kernel(
    packs, rows, att_ref, tokens_ref, cot_ref, weights_ref, vec_ref,
    layer_out, branch_out, dot_out, grad_out, vec_out,
    act_ref, slope_ref, post_ref, send_sem, recv_sem,
):
    place = Place(packs, rows).locate()
    mail = Mail(send_sem, recv_sem)
    me = place.r
    tok, width = tokens_ref.shape
    part = width // rows
    lines = width // 128
    square = lines * lines
    hidden = vec_ref.shape[0] * 128 - 8 * width
    count = 4
    size = hidden // count
    wide = size // 128
    greet(place.row_peers())

    def vector(first):
        return jnp.concatenate([vec_ref[first + i : first + i + 1, :] for i in range(lines)], 1)

    def put_vector(first, value):
        for i in range(value.shape[1] // 128):
            vec_out[first + i : first + i + 1, :] = value[:, i * 128 : (i + 1) * 128]

    bias_out, gain_one, shift_one = vector(2 * lines), vector(3 * lines), vector(4 * lines)
    last = 5 * lines + hidden // 128
    bias_two, gain_two, shift_two = vector(last), vector(last + lines), vector(last + 2 * lines)

    def w_one(n):
        return blocks_of(weights_ref, 4 * square + n * wide, lines, wide, hidden // 128)

    def w_two(n):
        first = 4 * square + lines * hidden // 128
        return blocks_of(weights_ref, first + n * wide * lines, wide, lines, lines)

    def put_grad(first, stride, value):
        for i in range(value.shape[0] // 128):
            for j in range(value.shape[1] // 128):
                row = (first + i * stride + j) * 128
                grad_out[row : row + 128, :] = value[i * 128 : (i + 1) * 128, j * 128 : (j + 1) * 128]

    attended_t = jnp.concatenate([att_ref[r] for r in range(rows)], 0)
    w_out = blocks_of(weights_ref, 3 * square, lines, lines, lines)
    branch = dot(attended_t, w_out, TN) + bias_out
    unit_one, scale_one = norm_forward(tokens_ref[...] + branch)
    normed = unit_one * gain_one + shift_one
    normed_low = normed.astype(BF16)
    second = jnp.zeros((tok, width), F32)
    for n in range(count):
        first = 5 * lines + n * wide
        bias = jnp.concatenate([vec_ref[first + i : first + i + 1, :] for i in range(wide)], 1)
        pre = dot(normed_low, w_one(n)) + bias
        square_pre = pre * pre
        inner = 0.7978845608028654 * pre * (1.0 + 0.044715 * square_pre)
        curve = jnp.tanh(inner)
        half = 0.5 * (1.0 + curve)
        act = (pre * half).astype(BF16)
        slope_ref[n] = half + 0.5 * pre * (1.0 - curve * curve) * (
            0.7978845608028654 * (1.0 + 0.134145 * square_pre)
        )
        act_ref[n] = act
        second = second + dot(act, w_two(n))
    unit_two, scale_two = norm_forward(normed + (second + bias_two))
    layer_out[...] = unit_two * gain_two + shift_two
    cot = cot_ref[...]
    put_vector(last + lines, column_sum(cot * unit_two))
    put_vector(last + 2 * lines, column_sum(cot))
    sum_grad = norm_backward(cot, gain_two, unit_two, scale_two)
    second_grad = sum_grad.astype(BF16)
    put_vector(last, column_sum(second_grad.astype(F32)))
    normed_grad = sum_grad
    for n in range(count):
        two = w_two(n)
        hidden_grad = (dot(second_grad, two, NT) * slope_ref[n]).astype(BF16)
        put_vector(5 * lines + n * wide, column_sum(hidden_grad.astype(F32)))
        normed_grad = normed_grad + dot(hidden_grad, w_one(n), NT)
        first = lines * hidden // 128 + square + n * wide * lines
        put_grad(first, lines, dot(act_ref[n], second_grad, TN))
        put_grad(square + n * wide, hidden // 128, dot(normed_low, hidden_grad, TN))
    put_vector(3 * lines, column_sum(normed_grad * unit_one))
    put_vector(4 * lines, column_sum(normed_grad))
    branch_grad = norm_backward(normed_grad, gain_one, unit_one, scale_one)
    branch_out[...] = branch_grad
    branch_low = branch_grad.astype(BF16)
    grad_t = dot(w_out, branch_low, NT).astype(BF16)
    for r in range(rows):
        post_ref[r] = grad_t[r * part : (r + 1) * part, :]
    lanes = pl.ds(pl.multiple_of(me * tok, 128), tok)
    hops = [
        mail.put(post_ref.at[device["row"]], dot_out.at[:, lanes], device) for device in place.row_peers()
    ]
    dot_out[:, lanes] = post_ref[me]
    put_vector(2 * lines, column_sum(branch_low.astype(F32)))
    put_grad(0, lines, dot(attended_t, branch_low))
    vec_out[: 2 * lines, :] = jnp.zeros((2 * lines, 128), F32)
    for hop in hops:
        hop.wait_recv()
    mail.finish()


def middle_call(packs, rows, attended, tokens, cotangent, weights, vec):
    vm = pl.BlockSpec(memory_space=pltpu.VMEM)
    tok, width = tokens.shape
    hidden = vec.shape[0] * 128 - 8 * width
    part = width // rows
    return pl.pallas_call(
        functools.partial(middle_kernel, packs, rows),
        out_shape=(
            jax.ShapeDtypeStruct((tok, width), F32),
            jax.ShapeDtypeStruct((tok, width), F32),
            jax.ShapeDtypeStruct((part, rows * tok), BF16),
            jax.ShapeDtypeStruct(((width * width + 2 * width * hidden) // 128, 128), F32),
            jax.ShapeDtypeStruct(vec.shape, F32),
        ),
        in_specs=[vm] * 5,
        out_specs=(vm,) * 5,
        scratch_shapes=[
            pltpu.VMEM((4, tok, hidden // 4), BF16),
            pltpu.VMEM((4, tok, hidden // 4), F32),
            pltpu.VMEM((rows, part, tok), BF16),
            pltpu.SemaphoreType.DMA((rows,)),
            pltpu.SemaphoreType.DMA((rows,)),
        ],
        compiler_params=pltpu.CompilerParams(collective_id=5, has_side_effects=True, vmem_limit_bytes=56 << 20),
        name="middle",
    )(attended, tokens, cotangent, weights, vec)


def back_kernel(
    packs, rows, dot_ref, kf_ref, qf_ref, vf_ref, kt_ref, q_ref, ot_ref, place_ref, tokens_ref,
    branch_ref, all_ref, vec_ref,
    input_out, grad_out, vec_out,
    df_ref, mix_ref, both_ref, pair_ref, qt_ref, post_ref, got_ref, weights_ref, send_sem, recv_sem, load_sem,
):
    load = pltpu.make_async_copy(all_ref.at[: weights_ref.shape[0]], weights_ref, load_sem)
    load.start()
    place = Place(packs, rows).locate()
    mail = Mail(send_sem, recv_sem)
    me = place.r
    heads, pack_len, _ = kf_ref.shape
    tok, width = tokens_ref.shape
    part = width // rows
    head = part // heads
    lines = width // 128
    square = lines * lines
    scale = head**-0.5
    greet(place.row_peers())

    lane = lax.broadcasted_iota(jnp.int32, (tok, part), 1)
    for r in range(rows):
        span = slice(r * tok, (r + 1) * tok)
        grad_t = dot_ref[:, span].astype(F32)
        center = grad_t * ot_ref[:, span]
        grad_rows = grad_t.T
        queries = q_ref[span, :].astype(F32)
        scaled = grad_t * scale
        g_high = scaled.astype(BF16).astype(F32)
        g_low = scaled - g_high
        for h in range(heads):
            own = slice(h * head, (h + 1) * head)
            shift = -scale * column_sum(center[own])
            sh = shift.astype(BF16).astype(F32)
            sm = (shift - sh).astype(BF16).astype(F32)
            df_ref[h, :, span] = jnp.concatenate(
                [g_high[own], g_low[own], sh, sm, shift - sh - sm, jnp.zeros((128 - 2 * head - 3, tok), F32)], 0
            ).astype(BF16)
            mine = (lane >= h * head) & (lane < (h + 1) * head)
            none = jnp.zeros((tok, part), F32)
            pad = [jnp.zeros((tok, 128 - 2 * part), F32)] if part < 64 else []
            mix_ref[2 * h, span, :] = jnp.concatenate([jnp.where(mine, grad_rows, 0.0), none] + pad, 1).astype(BF16)
            mix_ref[2 * h + 1, span, :] = jnp.concatenate([none, jnp.where(mine, queries, 0.0)] + pad, 1).astype(BF16)
    pair_ref[...] = jnp.zeros_like(pair_ref)

    def tile_step(number, carry):
        span = pl.ds(pl.multiple_of(number * TILE, TILE), TILE)
        pieces, mix = [], []
        for h in range(heads):
            probs = jnp.exp2(dot(kf_ref[h], qf_ref[h, :, span]))
            along = dot(vf_ref[h], df_ref[h, :, span])
            both_ref[:, 2 * h * TILE : (2 * h + 1) * TILE] = probs.astype(BF16)
            score_grad = (probs * along).astype(BF16)
            both_ref[:, (2 * h + 1) * TILE : (2 * h + 2) * TILE] = score_grad
            pieces.append(dot(kt_ref[h * head : (h + 1) * head, :], score_grad))
            mix += [mix_ref[2 * h, span, :], mix_ref[2 * h + 1, span, :]]
        qt_ref[:, span] = pieces[0] if heads == 1 else jnp.concatenate(pieces, 0)
        pair_ref[...] += dot(both_ref[...], jnp.concatenate(mix, 0))
        return carry

    lax.fori_loop(0, pack_len // TILE, tile_step, 0)
    for r in range(rows):
        span = slice(r * tok, (r + 1) * tok)
        pair = pair_ref[span, :].T
        post_ref[r] = jnp.concatenate([qt_ref[:, span], pair[part : 2 * part], pair[:part]], 0).astype(BF16)
    hops = [mail.put(post_ref.at[device["row"]], got_ref.at[me], device) for device in place.row_peers()]
    got_ref[me] = post_ref[me]
    for hop in hops:
        hop.wait_recv()

    load.wait()
    total = branch_ref[...]
    own_rows = place_ref[pl.ds(pl.multiple_of(me * tok, 16), tok), :]
    plain = tokens_ref[...].astype(BF16)
    for n in range(3):
        grad_t = jnp.concatenate([got_ref[r, n * part : (n + 1) * part, :] for r in range(rows)], 0)
        weight = blocks_of(weights_ref, n * square, lines, lines, lines)
        total = total + dot(grad_t, weight, (((0,), (1,)), ((), ())))
        product = dot(grad_t, plain if n == 2 else own_rows)
        for i in range(lines):
            for j in range(lines):
                row = (n * square + i * lines + j) * 128
                block = product[j * 128 : (j + 1) * 128, i * 128 : (i + 1) * 128]
                grad_out[row : row + 128, :] = block.T
        if n != 1:
            sums = jnp.sum(grad_t.astype(F32).T, axis=0, keepdims=True)
            for i in range(lines):
                row = (n // 2) * lines + i
                vec_out[row : row + 1, :] = sums[:, i * 128 : (i + 1) * 128]
    input_out[...] = total
    vec_out[2 * lines :, :] = vec_ref[2 * lines :, :]
    mail.finish()


def back_call(packs, rows, grad_t, kf, qf, vf, kt, q, ot, placed, tokens, branch, weights, vec_grad):
    vm = pl.BlockSpec(memory_space=pltpu.VMEM)
    tok, width = tokens.shape
    pack_len = rows * tok
    heads, part = HEADS // rows, width // rows
    used = 3 * width * width // 128
    return pl.pallas_call(
        functools.partial(back_kernel, packs, rows),
        out_shape=(
            jax.ShapeDtypeStruct((tok, width), F32),
            jax.ShapeDtypeStruct((used, 128), F32),
            jax.ShapeDtypeStruct(vec_grad.shape, F32),
        ),
        in_specs=[vm] * 10 + [pl.BlockSpec(memory_space=pl.ANY), vm],
        out_specs=(vm,) * 3,
        scratch_shapes=[
            pltpu.VMEM((heads, 128, pack_len), BF16),
            pltpu.VMEM((2 * heads, pack_len, 128), BF16),
            pltpu.VMEM((pack_len, 2 * heads * TILE), BF16),
            pltpu.VMEM((pack_len, 128), F32),
            pltpu.VMEM((part, pack_len), F32),
            pltpu.VMEM((rows, 3 * part, tok), BF16),
            pltpu.VMEM((rows, 3 * part, tok), BF16),
            pltpu.VMEM((used, 128), BF16),
            pltpu.SemaphoreType.DMA((rows,)),
            pltpu.SemaphoreType.DMA((rows,)),
            pltpu.SemaphoreType.DMA,
        ],
        compiler_params=pltpu.CompilerParams(collective_id=6, has_side_effects=True, vmem_limit_bytes=56 << 20),
        name="back",
    )(grad_t, kf, qf, vf, kt, q, ot, placed, tokens, branch, weights, vec_grad)


def adam_vector(grad, vector, first, second):
    first_new = BETA_ONE * first + (1.0 - BETA_ONE) * grad
    second_new = BETA_TWO * second + (1.0 - BETA_TWO) * grad * grad
    ratio = (
        first_new
        / (1.0 - BETA_ONE**STEP)
        / (jnp.sqrt(second_new / (1.0 - BETA_TWO**STEP)) + EPSILON)
    )
    return (vector - LEARN_RATE * ratio, first_new, second_new)


def shards(
    tokens, cotangent, segment_ids, padding, master, moment_first, moment_second,
    stat_left, stat_right, basis_left, basis_right, vec_params, vec_first, vec_second,
):
    packs, rows = lax.axis_size("pack"), lax.axis_size("row")
    codes = jnp.concatenate([segment_ids.reshape(-1, 128), padding.reshape(-1, 128)], 0)
    vec = vec_params.reshape(-1, 128)
    tokens_all, codes_all, weights = gather_call(packs, rows, tokens, codes, master)
    attended, placed, kf, qf, vf, kt, q, ot = attend_call(packs, rows, tokens_all, codes_all, weights, vec)
    layer_out, branch, grad_t, grad_late, vec_grad = middle_call(
        packs, rows, attended, tokens, cotangent, weights, vec
    )
    input_grad, grad_early, vec_grad = back_call(
        packs, rows, grad_t, kf, qf, vf, kt, q, ot, placed, tokens, branch, weights, vec_grad
    )
    owned, total_vector = reduce_call(packs, rows, grad_early, grad_late, vec_grad)
    updated = soap_call(
        packs, rows, owned, moment_first, moment_second, stat_left, stat_right, basis_left, basis_right, master
    )
    return (layer_out, input_grad) + updated + adam_vector(total_vector, vec_params, vec_first, vec_second)


def solution(mesh):
    placed = (
        P(("pack", "row"), None),
        P(("pack", "row"), None),
        P(("pack", "row")),
        P(("pack", "row")),
        P("pack", None),
        P("pack", None),
        P("pack", None),
        P("pack", None),
        P("pack", None),
        P("pack", None),
        P("pack", None),
        P(),
        P(),
        P(),
    )
    return jax.shard_map(
        shards,
        mesh=mesh,
        in_specs=placed,
        out_specs=(
            P(("pack", "row"), None),
            P(("pack", "row"), None),
            P("pack", None),
            P("pack", None),
            P("pack", None),
            P("pack", None),
            P("pack", None),
            P("pack", None),
            P("pack", None),
            P("pack", None),
            P(),
            P(),
            P(),
        ),
        check_vma=False,
    )
```

```python
import functools
import types
import jax
import ml_dtypes
import numpy as np
import jax.numpy as jnp
from jax import lax
from jax.experimental import pallas as pl
from jax.experimental.pallas import tpu as pltpu
from jax.sharding import PartitionSpec as P

HEADS = 8
IMG_W = 32
MASKED_SCORE = -1e30
NORM_EPSILON = 1e-05
STEP = 10
BETA_ONE = 0.9
BETA_TWO = 0.95
LEARN_RATE = 0.25
WEIGHT_DECAY = 0.01
EPSILON = 1e-08
F32 = jnp.float32
BF16 = jnp.bfloat16
NN = (((1,), (0,)), ((), ()))
NT = (((1,), (1,)), ((), ()))
TN = (((0,), (0,)), ((), ()))
MESH = pl.DeviceIdType.MESH


class Place:
    def __init__(self, packs, rows):
        self.packs, self.rows = packs, rows
        self.nx = rows // 2
        self.ny = self.nx if packs % self.nx == 0 else 1
        self.nz = packs // self.ny
        self.size = {"c": 2, "x": self.nx, "y": self.ny, "z": self.nz}

    def locate(self):
        self.p = lax.axis_index("pack")
        self.r = lax.axis_index("row")
        self.at = {
            "c": lax.rem(self.r, 2),
            "x": lax.div(self.r, 2),
            "y": lax.rem(self.p, self.ny),
            "z": lax.div(self.p, self.ny),
        }
        return self

    def device(self, **moved):
        at = {**self.at, **moved}
        return {"pack": at["z"] * self.ny + at["y"], "row": at["x"] * 2 + at["c"]}

    def other(self, dim, step):
        return lax.rem(self.at[dim] + step, self.size[dim])

    def peers(self, dim):
        found = []
        for step in range(1, self.size[dim]):
            there = self.other(dim, step)
            found.append((there, self.device(**{dim: there})))
        return found

    def row_peers(self):
        return [
            {"pack": self.p, "row": lax.rem(self.r + step, self.rows)} for step in range(1, self.rows)
        ]


def dot(left, right, dims=NN):
    return lax.dot_general(left, right, dims, preferred_element_type=F32)


def split2(v):
    high = v.astype(BF16)
    return high, (v - high.astype(F32)).astype(BF16)


def split3(v):
    high = v.astype(BF16)
    rest = v - high.astype(F32)
    mid = rest.astype(BF16)
    return high, mid, (rest - mid.astype(F32)).astype(BF16)


def dot3(left, right, dims=NN):
    la, ra = dims[0][0][0], dims[0][1][0]
    lh, ll = split2(left)
    rh, rl = split2(right)
    return dot(jnp.concatenate([lh, ll, lh], la), jnp.concatenate([rh, rh, rl], ra), dims)


def dot6(left, right, dims=NN):
    la, ra = dims[0][0][0], dims[0][1][0]
    lh, lm, ll = split3(left)
    rh, rm, rl = split3(right)
    return dot(
        jnp.concatenate([lh, lh, lm, lm, lh, ll], la),
        jnp.concatenate([rh, rm, rh, rm, rl, rh], ra),
        dims,
    )


def eliminate(m_ref, qt_ref, count):
    sub = lax.broadcasted_iota(jnp.int32, (16, 128), 0)

    def panel(index, carry):
        base = pl.multiple_of(index * 16, 16)
        back = lax.rem(128 - base, 128)
        gram, rest = [], []
        for s in range(count):
            gram.append(pltpu.roll(m_ref[s, pl.ds(base, 16), :128], back, 1))
            rest.append(m_ref[s, pl.ds(base, 16), 128:])
        for j in range(16):
            for s in range(count):
                g, a = gram[s], rest[s]
                col = jnp.broadcast_to(g[:, j : j + 1], (16, 128))
                inv = lax.rsqrt(col[j : j + 1, :])
                row_g = g[j : j + 1, :] * inv
                row_a = a[j : j + 1, :] * inv
                factor = jnp.where(sub > j, col * inv, 0.0)
                gram[s] = jnp.where(sub == j, row_g, g - factor * row_g)
                rest[s] = jnp.where(sub == j, row_a, a - factor * row_a)
        for s in range(count):
            u = pltpu.roll(gram[s], base, 1)
            qt_ref[s, pl.ds(base, 16), :] = rest[s]
            uh, um, ul = split3(u)
            ah, am, al = split3(rest[s])
            wh, wm, wl = [jnp.concatenate(p, 1) for p in ((uh, ah), (um, am), (ul, al))]
            m_ref[s] -= dot(
                jnp.concatenate([uh, uh, um, um, uh, ul], 0),
                jnp.concatenate([wh, wm, wh, wm, wl, wh], 0),
                TN,
            )
        return carry

    lax.fori_loop(0, 8, panel, 0)


def flat_rows(ref, count):
    return jnp.concatenate([ref[i : i + 1, :] for i in range(count)], 1)


def blocks_of(ref, first, down, across, stride):
    lines = []
    for i in range(down):
        row = [ref[pl.ds((first + i * stride + j) * 128, 128), :] for j in range(across)]
        lines.append(row[0] if across == 1 else jnp.concatenate(row, 1))
    return lines[0] if down == 1 else jnp.concatenate(lines, 0)


TILE = 256
LOG2E = 1.4426950408889634


def sine_rows(pack_len, half):
    column = np.arange(half)
    period = np.float32(10000.0) ** ((2 * (column // 2)).astype(np.float32) / np.float32(half))
    high = pack_len // IMG_W
    angles = np.arange(max(high, IMG_W)).astype(np.float32)[:, None] / period[None, :].astype(np.float32)
    angles = angles.astype(np.float64)
    table = np.where(column[None, :] % 2 == 0, np.sin(angles), np.cos(angles)).astype(np.float32)
    both = np.zeros((high + IMG_W, 2 * half), np.float32)
    both[:high, :half] = table[:high]
    both[high:, half:] = table[:IMG_W]
    pieces, rest = [], both
    for _ in range(3):
        piece = rest.astype(ml_dtypes.bfloat16)
        pieces.append(piece)
        rest = rest - piece.astype(np.float32)
    return np.concatenate(pieces, 0)


def norm_forward(hidden):
    center = hidden - jnp.mean(hidden, axis=-1, keepdims=True)
    scale = lax.rsqrt(jnp.mean(center * center, axis=-1, keepdims=True) + NORM_EPSILON)
    return center * scale, scale


def norm_backward(grad, gain, unit, scale):
    inner = grad * gain
    mean = jnp.mean(inner, axis=-1, keepdims=True)
    along = jnp.mean(inner * unit, axis=-1, keepdims=True)
    return scale * (inner - mean - unit * along)


def column_sum(values):
    return jnp.sum(values, axis=0, keepdims=True)


def when(condition, action):
    if condition is None:
        action()
    else:
        pl.when(condition)(action)


class Post:
    def __init__(self, copy, send=None, recv=None):
        self.copy, self.send_if, self.recv_if, self.gone = copy, send, recv, False

    def start(self):
        when(self.send_if, lambda: self.copy.start())

    def recv(self):
        when(self.recv_if, lambda: self.copy.wait_recv())

    def sent(self):
        if not self.gone:
            when(self.send_if, lambda: self.copy.wait_send())
        self.gone = True


class Mail:
    def __init__(self, send_sem, recv_sem):
        self.send_sem, self.recv_sem, self.posts = send_sem, recv_sem, []

    def make(self, source, target, device, send=None, recv=None, recv_sem=None):
        index = len(self.posts)
        copy = pltpu.make_async_remote_copy(
            src_ref=source, dst_ref=target,
            send_sem=self.send_sem.at[index],
            recv_sem=self.recv_sem.at[index] if recv_sem is None else recv_sem,
            device_id=device, device_id_type=MESH,
        )
        post = Post(copy, send, recv)
        self.posts.append(post)
        return post

    def put(self, *args, **kinds):
        post = self.make(*args, **kinds)
        post.start()
        return post

    def finish(self):
        assert len(self.posts) <= SEMS
        for post in self.posts:
            post.sent()


def greet(devices):
    barrier = pltpu.get_barrier_semaphore()
    for device in devices:
        pl.semaphore_signal(barrier, inc=1, device_id=device, device_id_type=MESH)
    pl.semaphore_wait(barrier, len(devices))


class Sizes:
    def __init__(self, packs, rows, tok, width, hidden, owned):
        self.packs, self.rows, self.tok, self.width, self.hidden, self.owned = packs, rows, tok, width, hidden, owned
        self.pack_len = rows * tok
        self.heads = HEADS // rows
        self.part = width // rows
        self.head = width // HEADS
        self.lines = width // 128
        self.square = self.lines * self.lines
        self.total = packs * owned
        self.blocks = owned // 128
        self.slots = -(-2 * self.blocks // rows)
        place = Place(packs, rows)
        self.nx, self.ny, self.nz = place.nx, place.ny, place.nz
        self.share = self.total // (packs * rows)
        self.chunks = 5 if self.share % 80 == 0 else 1
        self.size = self.share // self.chunks
        self.late = 3 * self.part * self.lines
        self.joint = max(n for n in range(1, packs + 1) if packs % n == 0 and self.late % (16 * n) == 0)
        self.owners = -(-3 * self.square // self.blocks)


def vmem_scratch(z):
    half, most = z.nx * z.ny * z.nz, max(z.nx, z.ny)
    ring = half // min(z.nx, z.ny)
    f = lambda *shape: pltpu.VMEM(shape, F32)
    b = lambda *shape: pltpu.VMEM(shape, BF16)
    return dict(
        tokens_all=f(z.rows, z.tok, z.width),
        codes_all=pltpu.VMEM((z.rows, 2 * z.tok // 128, 128), jnp.int32),
        weights=b(z.total, 128),
        placed=b(z.pack_len, z.width), plain=b(z.pack_len, z.width),
        kf=b(z.heads, z.pack_len, 128), qf=b(z.heads, 128, z.pack_len), vf=b(z.heads, z.pack_len, 128),
        kt=b(z.part, z.pack_len), vt=b(z.part, z.pack_len), q=b(z.pack_len, z.part), ot=f(z.part, z.pack_len),
        att_post=b(z.rows, z.part, z.tok), att=b(z.rows, z.part, z.tok),
        cot=f(z.tok, z.width), layer=f(z.tok, z.width), branch=f(z.tok, z.width),
        dot_post=b(z.rows, z.part, z.tok), dot=b(z.part, z.pack_len),
        grad=f(z.total, 128), vec_part=f(32, 128),
        stage0=b(z.chunks, half, z.size, 128), recv0=b(z.chunks, half, z.size, 128),
        stage1=b(z.chunks, half * (most - 1) // most, z.size, 128),
        recv1=b(z.chunks, half * (most - 1) // most, z.size, 128),
        kept1=f(z.chunks, ring, z.size, 128),
        stage2=b(z.chunks, (most - 1) * z.nz, z.size, 128), recv2=b(z.chunks, (most - 1) * z.nz, z.size, 128),
        kept2=f(z.chunks, z.nz, z.size, 128),
        stage3=b(z.chunks, z.nz, z.size, 128), recv3=b(z.chunks, z.nz, z.size, 128),
        vec_c=f(2, 32, 128), vec_x=f(z.nx, 32, 128), vec_y=f(z.ny, 32, 128), vec_z=f(z.nz, 32, 128),
        post=b(z.rows, 3 * z.part, z.tok), got=b(z.rows, 3 * z.part, z.tok),
        late=f(z.late, 128), late_post=b(z.late, 128), late_recv=b(z.packs, z.late // z.joint, 128),
        late_share=b(z.late // z.joint, 128), late_all=b(z.rows, z.late, 128),
        owned=b(z.owned, 128),
        first=f(z.owned, 128), second=f(z.owned, 128), left=f(z.owned, 128), right=f(z.owned, 128),
        lbasis=f(z.owned, 128), rbasis=f(z.owned, 128),
        gram=f(z.slots, 128, 256), qt=f(z.slots, 128, 128), bases=f(z.rows * z.slots * 128, 128),
        first_new=f(z.owned, 128), second_new=f(z.owned, 128), master_new=f(z.owned, 128), copy_new=b(z.owned, 128),
        left_new=f(z.owned, 128), right_new=f(z.owned, 128), input=f(z.tok, z.width), vec_new=f(3, 32, 128),
    )


SEMS = 320
LOADS = ("cot", "first", "second", "left", "right", "lbasis", "rbasis")


def layer_kernel(z, names, *refs):
    inputs = (
        "tokens", "codes", "master", "vec", "table", "vec_first", "vec_second",
        "cot_in", "first_in", "second_in", "left_in", "right_in", "lbasis_in", "rbasis_in",
    )
    outputs = (
        "layer_out", "input_out", "first_out", "second_out", "master_out", "copy_out", "left_out", "right_out",
        "lbasis_out", "rbasis_out", "vec_out",
    )
    s = types.SimpleNamespace(**dict(zip(inputs + outputs + tuple(names), refs)))
    send_sem, recv_sem, load_sem, late_sem = refs[-4:]
    loads = [
        pltpu.make_async_copy(getattr(s, name + "_in"), getattr(s, name), load_sem.at[i]) for i, name in enumerate(LOADS)
    ]
    for load in loads:
        load.start()
    stores = []

    def store(source, target):
        copy = pltpu.make_async_copy(source, target, load_sem.at[len(loads) + len(stores)])
        copy.start()
        stores.append(copy)

    place = Place(z.packs, z.rows).locate()
    mail = Mail(send_sem, recv_sem)
    at, me, pack = place.at, place.r, place.p
    nx, ny, nz, rows, tok, part, head, heads = z.nx, z.ny, z.nz, z.rows, z.tok, z.part, z.head, z.heads
    lines, square, width, hidden = z.lines, z.square, z.width, z.hidden
    partner = place.peers("c")[0]
    near = {dim: place.peers(dim) for dim in ("x", "y", "z")}
    row_peers = place.row_peers()

    def source(dim, step):
        return lax.rem(at[dim] + place.size[dim] - 1 - step, place.size[dim])

    half = z.owned // 2
    quarter = half // 2

    def piece(zz, yy, k=None):
        start = (zz * ny + yy) * z.owned + at["c"] * half
        count = half
        if k is not None:
            start, count = start + k * quarter, quarter
        return s.weights.at[pl.ds(pl.multiple_of(start, 16), count), :]

    def to(dim, index):
        return place.device(**{dim: index})

    up, down = lax.rem(at["z"] + 1, nz), lax.rem(at["z"] + nz - 1, nz)
    inner = at["z"] >= 1
    below_top = at["z"] + 1 < nz
    send_codes = [mail.make(s.codes, s.codes_all.at[me], device) for device in row_peers]
    send_x = [mail.make(s.tokens, s.tokens_all.at[me], device) for _, device in near["x"]]
    send_c = mail.make(s.tokens, s.tokens_all.at[me], partner[1])
    relay_x = []
    for step in range(nx - 1):
        row = source("x", step) * 2 + at["c"]
        relay_x.append(mail.make(s.tokens_all.at[row], s.tokens_all.at[row], partner[1]))
    chain, chain_y, chain_c, chain_yc = [], [], [], []
    for k in range(2):
        part_k = piece(0, at["y"], k)
        chain.append(mail.make(part_k, part_k, to("z", up), send=below_top, recv=inner))
        chain_y.append([mail.make(part_k, part_k, device) for _, device in near["y"]])
        chain_c.append(mail.make(part_k, part_k, partner[1], send=inner, recv=inner))
        chain_yc.append([])
        for step in range(ny - 1):
            part_k = piece(0, source("y", step), k)
            chain_yc[k].append(mail.make(part_k, part_k, partner[1]))

    def spread(zz, condition):
        mine = piece(zz, at["y"])
        over_y = [mail.make(mine, mine, device, condition, condition) for _, device in near["y"]]
        theirs = [piece(zz, source("y", step)) for step in range(ny - 1)]
        over_c = [mail.make(ref, ref, partner[1], condition, condition) for ref in theirs]
        return over_y, over_c

    own_y, own_c = spread(at["z"], inner)
    ups, downs = [], []
    for j in range(nz - 2):
        mine, coming = lax.rem(at["z"] + nz - j, nz), lax.rem(at["z"] + nz - 1 - j, nz)
        there = at["z"] - 1 - j >= 1
        hop = mail.make(piece(mine, at["y"]), piece(mine, at["y"]), to("z", up), (at["z"] - j >= 1) & below_top, there)
        core = mail.make(piece(coming, at["y"]), piece(coming, at["y"]), partner[1], there, there)
        ups.append((hop, core) + spread(coming, there))
    for j in range(nz - 1):
        mine, coming = lax.rem(at["z"] + j, nz), lax.rem(at["z"] + 1 + j, nz)
        there = at["z"] + 1 + j < nz
        hop = mail.make(piece(mine, at["y"]), piece(mine, at["y"]), to("z", down), inner & (at["z"] + j < nz), there)
        core = mail.make(piece(coming, at["y"]), piece(coming, at["y"]), partner[1], there, there)
        downs.append((hop, core) + spread(coming, there))

    own = pl.ds(pl.multiple_of(pack * z.owned, 16), z.owned)
    s.weights[own, :] = s.master[...].astype(BF16)
    greet(row_peers + [device for dim in ("y", "z") for _, device in near[dim]])
    for post in send_codes + send_x + [send_c]:
        post.start()

    def first_hop():
        for k in range(2):
            chain[k].start()
            for post in chain_y[k]:
                post.start()

    pl.when(at["z"] == 0)(first_hop)
    s.tokens_all[me] = s.tokens[...]
    s.codes_all[me] = s.codes[...]
    for post in send_codes:
        post.recv()

    groups = tok // 128
    high = z.pack_len // IMG_W
    ids, pad = s.codes_all[:, :groups, :], s.codes_all[:, groups:, :]
    index = (
        lax.broadcasted_iota(jnp.int32, ids.shape, 0) * tok
        + lax.broadcasted_iota(jnp.int32, ids.shape, 1) * 128
        + lax.broadcasted_iota(jnp.int32, ids.shape, 2)
    )
    starts = jnp.zeros(ids.shape, jnp.int32)
    for image in range(8):
        count = jnp.sum(jnp.where(ids == image, 1.0, 0.0)).astype(jnp.int32)
        starts = starts + jnp.where(ids > image, count, 0)
    places = index - starts
    on_y = lax.div(places, IMG_W)
    on_x = places - on_y * IMG_W

    def line(values, r):
        return jnp.concatenate([values[r, g : g + 1, :] for g in range(groups)], 1)

    def vector(first, count=lines):
        return jnp.concatenate([s.vec[first + i : first + i + 1, :] for i in range(count)], 1)

    def projections(pos_ref):
        for r in range(rows):
            sub = lax.broadcasted_iota(jnp.int32, (high, tok), 0)
            hot = jnp.concatenate(
                [
                    jnp.where(sub == line(on_y, r), 1.0, 0.0),
                    jnp.where(sub[:IMG_W] == line(on_x, r), 1.0, 0.0),
                ],
                0,
            ).astype(BF16)
            pos_ref[r] = dot(jnp.concatenate([hot] * 3, 0), s.table[...], TN)
        for k in range(2):

            def forward():
                chain[k].copy.wait_recv()
                chain[k].start()
                chain_c[k].copy.start()
                for post in chain_y[k]:
                    post.start()

            pl.when(inner)(forward)
        for post, relay in zip(send_x, relay_x):
            post.recv()
            relay.start()
        for k in range(2):
            for post, relay in zip(chain_y[k], chain_yc[k]):
                post.recv()
                relay.start()
        for post in [send_c] + relay_x + chain_c + chain_yc[0] + chain_yc[1]:
            post.recv()
        for post in own_y + [ups[0][0], downs[0][0]] if ups else own_y + [downs[0][0]]:
            post.start()
        pick = (
            lax.broadcasted_iota(jnp.int32, (width, part), 0)
            == lax.broadcasted_iota(jnp.int32, (width, part), 1) + me * part
        )
        pick = jnp.where(pick, 1.0, 0.0).astype(BF16)
        wq, wk, wv = [dot(blocks_of(s.weights, n * square, lines, lines, lines), pick).astype(BF16) for n in range(3)]

        def bias(first):
            row = jnp.broadcast_to(vector(first), (8, width))
            return pltpu.roll(row, lax.rem(width - me * part, width), 1)[:1, :part]

        bias_q, bias_v = bias(0), bias(lines)
        scale = LOG2E * head**-0.5
        sub8 = lax.broadcasted_iota(jnp.int32, (8, tok), 0)
        for r in range(rows):
            span = slice(r * tok, (r + 1) * tok)
            rows_in = s.tokens_all[r]
            placed = (rows_in + pos_ref[r]).astype(BF16)
            plain = rows_in.astype(BF16)
            s.placed[span, :] = placed
            s.plain[span, :] = plain
            q = (dot(placed, wq) + bias_q).astype(BF16)
            k = dot(placed, wk).astype(BF16)
            v = (dot(plain, wv) + bias_v).astype(BF16)
            s.q[span, :] = q
            qt, kt, vt = q.astype(F32).T, k.astype(F32).T, v.astype(F32).T
            s.kt[:, span] = kt.astype(BF16)
            s.vt[:, span] = vt.astype(BF16)
            scaled = qt * scale
            q_high = scaled.astype(BF16).astype(F32)
            q_low = scaled - q_high
            same = sub8 == line(ids, r)
            ones = jnp.ones((8, tok), F32)
            free = jnp.zeros((128 - 2 * head - 8, tok), F32)
            barred = jnp.where(same & (line(pad, r) == 0), 0.0, MASKED_SCORE)
            for h in range(heads):
                mine = slice(h * head, (h + 1) * head)
                s.qf[h, :, span] = jnp.concatenate(
                    [q_high[mine], q_low[mine], jnp.where(same, 1.0, 0.0), free], 0
                ).astype(BF16)
                s.kf[h, span, :] = jnp.concatenate([kt[mine], kt[mine], barred, ones, free[8:]], 0).T.astype(BF16)
                s.vf[h, span, :] = jnp.concatenate([vt[mine], vt[mine], ones, free], 0).T.astype(BF16)

    pl.run_scoped(projections, pltpu.VMEM((rows, tok, width), F32))

    att_posts = []
    for step in range(rows - 1):
        device = {"pack": pack, "row": lax.rem(me + 1 + step, rows)}
        att_posts.append(mail.make(s.att_post.at[step], s.att.at[me], device))

    def weight_stage(stage):
        if stage == 0:
            for post, core in zip(own_y, own_c):
                post.recv()
                core.start()
        for moves in (ups, downs):
            if 0 < stage <= len(moves):
                _, _, over_y, over_c = moves[stage - 1]
                for post, core in zip(over_y, over_c):
                    post.recv()
                    core.start()
            if stage < len(moves):
                hop, core, over_y, _ = moves[stage]
                hop.recv()
                if stage + 1 < len(moves):
                    moves[stage + 1][0].start()
                for post in [core] + over_y:
                    post.start()

    stages = nz
    per = tok // TILE
    tiles = rows * per

    def attend_step(number, carry):
        step = lax.div(number, per)
        offset = lax.rem(number, per)
        dest = lax.rem(me + 1 + step, rows)
        span = pl.ds(pl.multiple_of(dest * tok + offset * TILE, TILE), TILE)
        for stage in range(stages):
            pl.when(number == (stage + 1) * tiles // (stages + 1))(functools.partial(weight_stage, stage))
        pieces = []
        for h in range(heads):
            scores = dot(s.kf[h], s.qf[h, :, span])
            largest = jnp.max(scores, axis=0, keepdims=True)
            weights = jnp.exp2(scores - largest)
            total = jnp.sum(weights, axis=0, keepdims=True)
            out = dot(s.vt[h * head : (h + 1) * head, :], weights.astype(BF16))
            pieces.append(out * (1.0 / total))
            lse = -(largest + jnp.log2(total))
            lh = lse.astype(BF16).astype(F32)
            lm = (lse - lh).astype(BF16).astype(F32)
            tail = s.qf[h, 2 * head : 2 * head + 16, span].astype(F32)
            tail = jnp.concatenate([tail[:8], lh, lm, lse - lh - lm, jnp.zeros((5, TILE), F32)], 0)
            s.qf[h, 2 * head : 2 * head + 16, span] = tail.astype(BF16)
        out = pieces[0] if heads == 1 else jnp.concatenate(pieces, 0)
        s.ot[:, span] = out
        s.att_post[step, :, pl.ds(pl.multiple_of(offset * TILE, TILE), TILE)] = out.astype(BF16)
        for there in range(rows - 1):
            pl.when(number == (there + 1) * per - 1)(functools.partial(att_posts[there].start))
        return carry

    lax.fori_loop(0, tiles, attend_step, 0)
    s.att[me] = s.att_post[rows - 1]
    for post in att_posts:
        post.recv()
    for post in own_c + [p for moves in (ups, downs) for move in moves for p in [move[1]] + move[3]]:
        post.recv()

    dot_lanes = pl.ds(pl.multiple_of(me * tok, 128), tok)
    dot_posts = [mail.make(s.dot_post.at[d["row"]], s.dot.at[:, dot_lanes], d) for d in row_peers]
    loads[0].wait()

    def middle(act_ref, slope_ref):
        count = 4
        wide = hidden // count // 128

        def put_vector(first, value):
            for i in range(value.shape[1] // 128):
                s.vec_part[first + i : first + i + 1, :] = value[:, i * 128 : (i + 1) * 128]

        bias_out, gain_one, shift_one = vector(2 * lines), vector(3 * lines), vector(4 * lines)
        last = 5 * lines + hidden // 128
        bias_two, gain_two, shift_two = vector(last), vector(last + lines), vector(last + 2 * lines)

        def w_one(n):
            return blocks_of(s.weights, 4 * square + n * wide, lines, wide, hidden // 128)

        def w_two(n):
            first = 4 * square + lines * hidden // 128
            return blocks_of(s.weights, first + n * wide * lines, wide, lines, lines)

        def put_grad(first, stride, value):
            for i in range(value.shape[0] // 128):
                for j in range(value.shape[1] // 128):
                    row = (3 * square + first + i * stride + j) * 128
                    s.grad[row : row + 128, :] = value[i * 128 : (i + 1) * 128, j * 128 : (j + 1) * 128]

        attended_t = jnp.concatenate([s.att[r] for r in range(rows)], 0)
        w_out = blocks_of(s.weights, 3 * square, lines, lines, lines)
        branch = dot(attended_t, w_out, TN) + bias_out
        unit_one, scale_one = norm_forward(s.tokens[...] + branch)
        normed = unit_one * gain_one + shift_one
        normed_low = normed.astype(BF16)
        second = jnp.zeros((tok, width), F32)
        for n in range(count):
            pre = dot(normed_low, w_one(n)) + vector(5 * lines + n * wide, wide)
            square_pre = pre * pre
            curve = jnp.tanh(0.7978845608028654 * pre * (1.0 + 0.044715 * square_pre))
            half_one = 0.5 * (1.0 + curve)
            act = (pre * half_one).astype(BF16)
            slope_ref[n] = half_one + 0.5 * pre * (1.0 - curve * curve) * (
                0.7978845608028654 * (1.0 + 0.134145 * square_pre)
            )
            act_ref[n] = act
            second = second + dot(act, w_two(n))
        unit_two, scale_two = norm_forward(normed + (second + bias_two))
        s.layer[...] = unit_two * gain_two + shift_two
        cot = s.cot[...]
        put_vector(last + lines, column_sum(cot * unit_two))
        put_vector(last + 2 * lines, column_sum(cot))
        sum_grad = norm_backward(cot, gain_two, unit_two, scale_two)
        second_grad = sum_grad.astype(BF16)
        put_vector(last, column_sum(second_grad.astype(F32)))
        normed_grad = sum_grad
        for n in range(count):
            two = w_two(n)
            hidden_grad = (dot(second_grad, two, NT) * slope_ref[n]).astype(BF16)
            put_vector(5 * lines + n * wide, column_sum(hidden_grad.astype(F32)))
            normed_grad = normed_grad + dot(hidden_grad, w_one(n), NT)
            first = lines * hidden // 128 + square + n * wide * lines
            put_grad(first, lines, dot(act_ref[n], second_grad, TN))
            put_grad(square + n * wide, hidden // 128, dot(normed_low, hidden_grad, TN))
        put_vector(3 * lines, column_sum(normed_grad * unit_one))
        put_vector(4 * lines, column_sum(normed_grad))
        branch_grad = norm_backward(normed_grad, gain_one, unit_one, scale_one)
        s.branch[...] = branch_grad
        branch_low = branch_grad.astype(BF16)
        grad_t = dot(w_out, branch_low, NT).astype(BF16)
        for r in range(rows):
            s.dot_post[r] = grad_t[r * part : (r + 1) * part, :]
        for post in dot_posts:
            post.start()
        s.dot[:, dot_lanes] = s.dot_post[me]
        put_vector(2 * lines, column_sum(branch_low.astype(F32)))
        put_grad(0, lines, dot(attended_t, branch_low))

    pl.run_scoped(middle, pltpu.VMEM((4, tok, hidden // 4), BF16), pltpu.VMEM((4, tok, hidden // 4), F32))

    store(s.layer, s.layer_out)

    chunks, size, share = z.chunks, z.size, z.share
    s.grad[: 3 * square * 128, :] = jnp.zeros((3 * square * 128, 128), F32)

    def grad_rows(chunk, x, c, y, z):
        row = (z * ny + y) * (rows * share) + (x * 2 + c) * share + chunk * size
        return s.grad[pl.ds(pl.multiple_of(row, 16), size), :]

    def order(chunk):
        return ("x", "y") if chunk % 2 == 0 else ("y", "x")

    def spot(chunk, one, two, zz):
        return {order(chunk)[0]: one, order(chunk)[1]: two, "z": zz}

    hops0, hops1, hops2, hops3, hops4 = [], [], [], [], []
    for chunk in range(chunks):
        n2 = place.size[order(chunk)[1]]
        hops0.append(mail.make(s.stage0.at[chunk], s.recv0.at[chunk], partner[1]))
        made = []
        for step, (_, device) in enumerate(near[order(chunk)[0]]):
            span = pl.ds(step * n2 * nz, n2 * nz)
            made.append(mail.make(s.stage1.at[chunk, span], s.recv1.at[chunk, span], device))
        hops1.append(made)
        made = []
        for step, (_, device) in enumerate(near[order(chunk)[1]]):
            span = pl.ds(step * nz, nz)
            made.append(mail.make(s.stage2.at[chunk, span], s.recv2.at[chunk, span], device))
        hops2.append(made)
        hops3.append(
            [mail.make(s.stage3.at[chunk, step], s.recv3.at[chunk, step], d) for step, (_, d) in enumerate(near["z"])]
        )
        mine = pl.ds(pl.multiple_of(me * share + chunk * size, 16), size)
        hops4.append([mail.make(s.owned.at[mine], s.owned.at[mine], device) for device in row_peers])

    def reduce_cores():
        for chunk in range(chunks):
            n1, n2 = [place.size[d] for d in order(chunk)]
            for one in range(n1):
                for two in range(n2):
                    for zz in range(nz):
                        rows_of = grad_rows(chunk, c=partner[0], **spot(chunk, one, two, zz))
                        s.stage0[chunk, (one * n2 + two) * nz + zz] = rows_of.astype(BF16)
            hops0[chunk].start()

    def reduce_first():
        for chunk in range(chunks):
            n1, n2 = [place.size[d] for d in order(chunk)]
            hops0[chunk].recv()

            def summed(one, two, zz):
                slot = (one * n2 + two) * nz + zz
                rows_of = grad_rows(chunk, c=at["c"], **spot(chunk, one, two, zz))
                return rows_of + s.recv0[chunk, slot].astype(F32)

            for step, (there, _) in enumerate(near[order(chunk)[0]]):
                for two in range(n2):
                    for zz in range(nz):
                        s.stage1[chunk, step * n2 * nz + two * nz + zz] = summed(there, two, zz).astype(BF16)
                hops1[chunk][step].start()
            for two in range(n2):
                for zz in range(nz):
                    s.kept1[chunk, two * nz + zz] = summed(at[order(chunk)[0]], two, zz)

    def reduce_second():
        for chunk in range(chunks):
            n1, n2 = [place.size[d] for d in order(chunk)]
            for hop in hops1[chunk]:
                hop.recv()

            def summed(two, zz):
                total = s.kept1[chunk, two * nz + zz]
                for step in range(n1 - 1):
                    total = total + s.recv1[chunk, step * n2 * nz + two * nz + zz].astype(F32)
                return total

            for step, (there, _) in enumerate(near[order(chunk)[1]]):
                for zz in range(nz):
                    s.stage2[chunk, step * nz + zz] = summed(there, zz).astype(BF16)
                hops2[chunk][step].start()
            for zz in range(nz):
                s.kept2[chunk, zz] = summed(at[order(chunk)[1]], zz)

    def reduce_third():
        for chunk in range(chunks):
            n2 = place.size[order(chunk)[1]]
            for hop in hops2[chunk]:
                hop.recv()

            def summed(zz):
                total = s.kept2[chunk, zz]
                for step in range(n2 - 1):
                    total = total + s.recv2[chunk, step * nz + zz].astype(F32)
                return total

            for step, (there, _) in enumerate(near["z"]):
                s.stage3[chunk, step] = summed(there).astype(BF16)
                hops3[chunk][step].start()
            s.kept2[chunk, at["z"]] = summed(at["z"])

    def reduce_last():
        for chunk in range(chunks):
            total = s.kept2[chunk, at["z"]]
            for step, hop in enumerate(hops3[chunk]):
                hop.recv()
                total = total + s.recv3[chunk, step].astype(F32)
            mine = pl.ds(pl.multiple_of(me * share + chunk * size, 16), size)
            s.owned[mine, :] = total.astype(BF16)
            for hop in hops4[chunk]:
                hop.start()

    reduce_stages = (reduce_first, reduce_second, reduce_third, reduce_last)
    reduce_cores()
    for post in dot_posts:
        post.recv()

    scale = head**-0.5
    posts = [mail.make(s.post.at[d["row"]], s.got.at[me], d) for d in row_peers]

    def backward(df_ref, mix_ref, both_ref, pair_ref, qt_ref):
        lane = lax.broadcasted_iota(jnp.int32, (tok, part), 1)
        for r in range(rows):
            span = slice(r * tok, (r + 1) * tok)
            grad_t = s.dot[:, span].astype(F32)
            center = grad_t * s.ot[:, span]
            grad_rows_in = grad_t.T
            queries = s.q[span, :].astype(F32)
            scaled = grad_t * scale
            g_high = scaled.astype(BF16).astype(F32)
            g_low = scaled - g_high
            for h in range(heads):
                own_lines = slice(h * head, (h + 1) * head)
                shift = -scale * column_sum(center[own_lines])
                sh = shift.astype(BF16).astype(F32)
                sm = (shift - sh).astype(BF16).astype(F32)
                rest = jnp.zeros((128 - 2 * head - 3, tok), F32)
                df_ref[h, :, span] = jnp.concatenate(
                    [g_high[own_lines], g_low[own_lines], sh, sm, shift - sh - sm, rest], 0
                ).astype(BF16)
                mine = (lane >= h * head) & (lane < (h + 1) * head)
                none = jnp.zeros((tok, part), F32)
                free = [jnp.zeros((tok, 128 - 2 * part), F32)] if part < 64 else []
                mix_ref[2 * h, span, :] = jnp.concatenate(
                    [jnp.where(mine, grad_rows_in, 0.0), none] + free, 1
                ).astype(BF16)
                mix_ref[2 * h + 1, span, :] = jnp.concatenate(
                    [none, jnp.where(mine, queries, 0.0)] + free, 1
                ).astype(BF16)
        pair_ref[...] = jnp.zeros_like(pair_ref)
        turns = z.pack_len // TILE

        def tile_step(number, carry):
            span = pl.ds(pl.multiple_of(number * TILE, TILE), TILE)
            for stage, action in enumerate(reduce_stages):
                pl.when(number == 1 + stage * (turns - 2) // 3)(action)
            pieces, mix = [], []
            for h in range(heads):
                probs = jnp.exp2(dot(s.kf[h], s.qf[h, :, span]))
                along = dot(s.vf[h], df_ref[h, :, span])
                both_ref[:, 2 * h * TILE : (2 * h + 1) * TILE] = probs.astype(BF16)
                score_grad = (probs * along).astype(BF16)
                both_ref[:, (2 * h + 1) * TILE : (2 * h + 2) * TILE] = score_grad
                pieces.append(dot(s.kt[h * head : (h + 1) * head, :], score_grad))
                mix += [mix_ref[2 * h, span, :], mix_ref[2 * h + 1, span, :]]
            qt_ref[:, span] = pieces[0] if heads == 1 else jnp.concatenate(pieces, 0)
            pair_ref[...] += dot(both_ref[...], jnp.concatenate(mix, 0))
            return carry

        lax.fori_loop(0, turns, tile_step, 0)
        for r in range(rows):
            span = slice(r * tok, (r + 1) * tok)
            pair = pair_ref[span, :].T
            s.post[r] = jnp.concatenate([qt_ref[:, span], pair[part : 2 * part], pair[:part]], 0).astype(BF16)

    pl.run_scoped(
        backward,
        pltpu.VMEM((heads, 128, z.pack_len), BF16),
        pltpu.VMEM((2 * heads, z.pack_len, 128), BF16),
        pltpu.VMEM((z.pack_len, 2 * heads * TILE), BF16),
        pltpu.VMEM((z.pack_len, 128), F32),
        pltpu.VMEM((part, z.pack_len), F32),
    )

    for post in posts:
        post.start()
    s.got[me] = s.post[me]
    joint, owners = z.joint, z.owners
    size_l = z.late // joint
    for kind, first, last in (("placed", 0, 2 * part), ("plain", 2 * part, 3 * part)):
        base = getattr(s, kind)
        total = jnp.zeros((last - first, width), F32)
        for r in range(rows):
            total = total + dot(s.post[r, first:last, :], base[r * tok : (r + 1) * tok, :])
        for i in range(lines):
            row = i * 3 * part + first
            s.late[row : row + last - first, :] = total[:, i * 128 : (i + 1) * 128]
    s.late_post[...] = s.late[...].astype(BF16)
    spread_posts = []
    joined = None if joint == z.packs else pack < joint
    for step in range(1, z.packs):
        there = lax.rem(pack + step, z.packs)
        lands = None if joint == z.packs else there < joint
        rows_of = pl.ds(pl.multiple_of(lax.rem(there, joint) * size_l, 16), size_l)
        spread_posts.append(
            mail.put(
                s.late_post.at[rows_of, :], s.late_recv.at[step - 1], {"pack": there, "row": me}, lands, joined
            )
        )

    for post in posts:
        post.recv()
    total = s.branch[...]
    for n in range(3):
        grad_t = jnp.concatenate([s.got[r, n * part : (n + 1) * part, :] for r in range(rows)], 0)
        weight = blocks_of(s.weights, n * square, lines, lines, lines)
        total = total + dot(grad_t, weight, (((0,), (1,)), ((), ())))
        if n != 1:
            sums = column_sum(grad_t.astype(F32).T)
            for i in range(lines):
                row = (n // 2) * lines + i
                s.vec_part[row : row + 1, :] = sums[:, i * 128 : (i + 1) * 128]
    s.input[...] = total
    store(s.input, s.input_out)

    def vec_step(dim, buffer, value):
        buffer[at[dim]] = value
        return [mail.put(buffer.at[at[dim]], buffer.at[at[dim]], device) for _, device in place.peers(dim)]

    def vec_sum(hops, buffer):
        for hop in hops:
            hop.recv()
        total = buffer[0]
        for number in range(1, buffer.shape[0]):
            total = total + buffer[number]
        return total

    vec_hops = vec_step("c", s.vec_c, s.vec_part[...])
    own_late = pl.ds(pl.multiple_of(lax.rem(pack, joint) * size_l, 16), size_l)
    for post in spread_posts:
        post.recv()
    total = s.late[own_late, :]
    for step in range(z.packs - 1):
        total = total + s.late_recv[step].astype(F32)
    s.late_share[...] = total.astype(BF16)
    s.late_all[me, own_late, :] = total.astype(BF16)
    for owner in range(owners):
        for step in range(rows):
            leaves = [] if joint == z.packs else [pack < joint]
            if step == 0:
                leaves.append(pack != owner)
            leaves = functools.reduce(jnp.logical_and, leaves) if leaves else None
            mail.put(
                s.late_share, s.late_all.at[me, own_late, :],
                {"pack": pack * 0 + owner, "row": lax.rem(me + step, rows)}, leaves, None,
                late_sem.at[lax.rem(pack, joint), step],
            )
    vec_hops = vec_step("x", s.vec_x, vec_sum(vec_hops, s.vec_c))
    for load in loads[1:]:
        load.wait()
    for chunk in range(chunks):
        for hop in hops4[chunk]:
            hop.recv()
            hop.sent()
    vec_hops = vec_step("y", s.vec_y, vec_sum(vec_hops, s.vec_x))

    def late_wait():
        for giver in range(joint):
            for step in range(rows):

                def wait():
                    pltpu.make_async_remote_copy(
                        src_ref=s.late_share, dst_ref=s.late_all.at[0, :size_l, :],
                        send_sem=send_sem.at[0], recv_sem=late_sem.at[giver, step],
                        device_id={"pack": pack, "row": lax.rem(me + 1, rows)}, device_id_type=MESH,
                    ).wait_recv()

                when((pack != giver) if step == 0 else None, wait)
        for b in range(3 * square):
            kind, i, j = b // square, b % square // lines, b % lines

            def place_block():
                start = (i * 3 + kind) * part
                found = [s.late_all[r, start : start + part, :] for r in range(j * 128 // part, (j + 1) * 128 // part)]
                block = jnp.concatenate(found, 0).astype(F32).T
                row = b % z.blocks * 128
                s.owned[row : row + 128, :] = block.astype(BF16)

            pl.when(pack == b // z.blocks)(place_block)

    pl.when(pack < owners)(late_wait)
    vec_hops = vec_step("z", s.vec_z, vec_sum(vec_hops, s.vec_y))

    blocks, slots = z.blocks, z.slots
    for n in range(slots):
        t = jnp.minimum(me * slots + n, 2 * blocks - 1)
        is_right = t >= blocks
        rows_of = pl.ds(pl.multiple_of(jnp.where(is_right, t - blocks, t) * 128, 128), 128)
        g = s.owned[rows_of, :].astype(F32)
        g = jnp.where(is_right, g.T, g).astype(BF16)
        stat = jnp.where(is_right, s.right[rows_of, :], s.left[rows_of, :])
        basis = jnp.where(is_right, s.rbasis[rows_of, :], s.lbasis[rows_of, :])
        new = BETA_TWO * stat + (1.0 - BETA_TWO) * dot(g, g, NT)
        a = dot6(new, basis)
        a_t = a.T
        s.gram[n, :, :128] = dot6(a_t, a)
        s.gram[n, :, 128:] = a_t
    eliminate(s.gram, s.qt, slots)

    def base_at(row, n):
        return s.bases.at[pl.ds(pl.multiple_of((row * slots + n) * 128, 128), 128), :]

    base_c, base_x, base_f = [], [], []
    for n in range(slots):
        s.bases[pl.ds(pl.multiple_of((me * slots + n) * 128, 128), 128), :] = s.qt[n].T
        base_x.append([mail.put(base_at(me, n), base_at(me, n), device) for _, device in near["x"]])
        base_c.append(mail.put(base_at(me, n), base_at(me, n), partner[1]))

    def block_step(number, carry):
        rows_of = pl.ds(pl.multiple_of(number * 128, 128), 128)
        g = s.owned[rows_of, :]
        s.left_new[rows_of, :] = BETA_TWO * s.left[rows_of, :] + (1.0 - BETA_TWO) * dot(g, g, NT)
        s.right_new[rows_of, :] = BETA_TWO * s.right[rows_of, :] + (1.0 - BETA_TWO) * dot(g, g, TN)
        lb, rb = s.lbasis[rows_of, :], s.rbasis[rows_of, :]
        lh, ll = split2(lb)
        turned = dot(jnp.concatenate([lh, ll], 0), jnp.concatenate([g, g], 0), TN)
        rotated = dot3(turned, rb)
        first = BETA_ONE * s.first[rows_of, :] + (1.0 - BETA_ONE) * rotated
        second = BETA_TWO * s.second[rows_of, :] + (1.0 - BETA_TWO) * rotated * rotated
        s.first_new[rows_of, :] = first
        s.second_new[rows_of, :] = second
        ratio = first / (1.0 - BETA_ONE**STEP) / (jnp.sqrt(second / (1.0 - BETA_TWO**STEP)) + EPSILON)
        stepped = dot3(dot3(lb, ratio), rb, NT)
        weights = s.master[rows_of, :]
        weights = weights - LEARN_RATE * (stepped + WEIGHT_DECAY * weights)
        s.master_new[rows_of, :] = weights
        s.copy_new[rows_of, :] = weights.astype(BF16)
        return carry

    for n in range(slots):
        lax.fori_loop(blocks * n // slots, blocks * (n + 1) // slots, block_step, 0)
        for step, hop in enumerate(base_x[n]):
            hop.recv()
            row = source("x", step) * 2 + at["c"]
            base_f.append(mail.put(base_at(row, n), base_at(row, n), partner[1]))
    for name in ("first", "second", "master", "copy", "left", "right"):
        store(getattr(s, name + "_new"), getattr(s, name + "_out"))
    grad = vec_sum(vec_hops, s.vec_z)
    first = BETA_ONE * s.vec_first[...] + (1.0 - BETA_ONE) * grad
    second = BETA_TWO * s.vec_second[...] + (1.0 - BETA_TWO) * grad * grad
    ratio = first / (1.0 - BETA_ONE**STEP) / (jnp.sqrt(second / (1.0 - BETA_TWO**STEP)) + EPSILON)
    s.vec_new[0] = s.vec[...] - LEARN_RATE * ratio
    s.vec_new[1] = first
    s.vec_new[2] = second
    store(s.vec_new, s.vec_out)
    for hop in base_c + base_f:
        hop.recv()
    store(s.bases.at[: z.owned, :], s.lbasis_out)
    store(s.bases.at[z.owned : 2 * z.owned, :], s.rbasis_out)
    for copy in stores:
        copy.wait()
    mail.finish()


def finish_kernel(count, *refs):
    sems = refs[-1]
    loads = [pltpu.make_async_copy(refs[i], refs[2 * count + i], sems.at[i]) for i in range(count)]
    stores = [pltpu.make_async_copy(refs[2 * count + i], refs[count + i], sems.at[count + i]) for i in range(count)]
    for load in loads:
        load.start()
    for load, copy in zip(loads, stores):
        load.wait()
        copy.start()
    for copy in stores:
        copy.wait()


def shards(
    tokens, cotangent, segment_ids, padding, master, moment_first, moment_second,
    stat_left, stat_right, basis_left, basis_right, vec_params, vec_first, vec_second,
):
    packs, rows = lax.axis_size("pack"), lax.axis_size("row")
    tok, width = tokens.shape
    z = Sizes(packs, rows, tok, width, vec_params.shape[0] - 8 * width, master.shape[0])
    codes = jnp.concatenate([segment_ids.reshape(-1, 128), padding.reshape(-1, 128)], 0)
    table = jnp.asarray(sine_rows(z.pack_len, width // 2))
    full = jax.ShapeDtypeStruct(master.shape, F32)
    layer = jax.ShapeDtypeStruct(tokens.shape, F32)
    shapes = (layer, layer, full, full, full, jax.ShapeDtypeStruct(master.shape, BF16), full, full, full, full)
    shapes = shapes + (jax.ShapeDtypeStruct((3, 32, 128), F32),)
    scratch = vmem_scratch(z)
    vm, hbm = pl.BlockSpec(memory_space=pltpu.VMEM), pl.BlockSpec(memory_space=pl.ANY)
    outs = pl.pallas_call(
        functools.partial(layer_kernel, z, tuple(scratch)),
        out_shape=shapes,
        in_specs=[vm] * 7 + [hbm] * 7,
        out_specs=(hbm,) * len(shapes),
        scratch_shapes=list(scratch.values())
        + [
            pltpu.SemaphoreType.DMA((SEMS,)),
            pltpu.SemaphoreType.DMA((SEMS,)),
            pltpu.SemaphoreType.DMA((len(LOADS) + len(shapes),)),
            pltpu.SemaphoreType.DMA((packs, rows)),
        ],
        compiler_params=pltpu.CompilerParams(collective_id=1, has_side_effects=True, vmem_limit_bytes=63 << 20),
        name="layer",
    )(
        tokens, codes, master, vec_params.reshape(32, 128), table,
        vec_first.reshape(32, 128), vec_second.reshape(32, 128),
        cotangent, moment_first, moment_second, stat_left, stat_right, basis_left, basis_right,
    )
    outs = pl.pallas_call(
        functools.partial(finish_kernel, len(shapes)),
        out_shape=shapes,
        in_specs=[hbm] * len(shapes),
        out_specs=(hbm,) * len(shapes),
        scratch_shapes=[pltpu.VMEM(shape.shape, shape.dtype) for shape in shapes]
        + [pltpu.SemaphoreType.DMA((2 * len(shapes),))],
        compiler_params=pltpu.CompilerParams(vmem_limit_bytes=63 << 20),
        name="finish",
    )(*outs)
    vec = outs[-1].reshape(3, -1)
    return outs[:-1] + (vec[0], vec[1], vec[2])


def solution(mesh):
    placed = (
        P(("pack", "row"), None),
        P(("pack", "row"), None),
        P(("pack", "row")),
        P(("pack", "row")),
        P("pack", None),
        P("pack", None),
        P("pack", None),
        P("pack", None),
        P("pack", None),
        P("pack", None),
        P("pack", None),
        P(),
        P(),
        P(),
    )
    return jax.shard_map(
        shards,
        mesh=mesh,
        in_specs=placed,
        out_specs=(
            P(("pack", "row"), None),
            P(("pack", "row"), None),
            P("pack", None),
            P("pack", None),
            P("pack", None),
            P("pack", None),
            P("pack", None),
            P("pack", None),
            P("pack", None),
            P("pack", None),
            P(),
            P(),
            P(),
        ),
        check_vma=False,
    )
```

```python
import functools
import types
import jax
import ml_dtypes
import numpy as np
import jax.numpy as jnp
from jax import lax
from jax.experimental import pallas as pl
from jax.experimental.pallas import tpu as pltpu
from jax.sharding import PartitionSpec as P

HEADS = 8
IMG_W = 32
MASKED_SCORE = -1e30
NORM_EPSILON = 1e-05
STEP = 10
BETA_ONE = 0.9
BETA_TWO = 0.95
LEARN_RATE = 0.25
WEIGHT_DECAY = 0.01
EPSILON = 1e-08
F32 = jnp.float32
BF16 = jnp.bfloat16
NN = (((1,), (0,)), ((), ()))
NT = (((1,), (1,)), ((), ()))
TN = (((0,), (0,)), ((), ()))
MESH = pl.DeviceIdType.MESH


class Place:
    def __init__(self, packs, rows):
        self.packs, self.rows = packs, rows
        self.nx = rows // 2
        self.ny = self.nx if packs % self.nx == 0 else 1
        self.nz = packs // self.ny
        self.size = {"c": 2, "x": self.nx, "y": self.ny, "z": self.nz}

    def locate(self):
        self.p = lax.axis_index("pack")
        self.r = lax.axis_index("row")
        self.at = {
            "c": lax.rem(self.r, 2),
            "x": lax.div(self.r, 2),
            "y": lax.rem(self.p, self.ny),
            "z": lax.div(self.p, self.ny),
        }
        return self

    def device(self, **moved):
        at = {**self.at, **moved}
        return {"pack": at["z"] * self.ny + at["y"], "row": at["x"] * 2 + at["c"]}

    def other(self, dim, step):
        return lax.rem(self.at[dim] + step, self.size[dim])

    def peers(self, dim):
        found = []
        for step in range(1, self.size[dim]):
            there = self.other(dim, step)
            found.append((there, self.device(**{dim: there})))
        return found

    def row_peers(self):
        return [
            {"pack": self.p, "row": lax.rem(self.r + step, self.rows)} for step in range(1, self.rows)
        ]


def dot(left, right, dims=NN):
    return lax.dot_general(left, right, dims, preferred_element_type=F32)


def split2(v):
    high = v.astype(BF16)
    return high, (v - high.astype(F32)).astype(BF16)


def split3(v):
    high = v.astype(BF16)
    rest = v - high.astype(F32)
    mid = rest.astype(BF16)
    return high, mid, (rest - mid.astype(F32)).astype(BF16)


def dot3(left, right, dims=NN):
    la, ra = dims[0][0][0], dims[0][1][0]
    lh, ll = split2(left)
    rh, rl = split2(right)
    return dot(jnp.concatenate([lh, ll, lh], la), jnp.concatenate([rh, rh, rl], ra), dims)


def dot6(left, right, dims=NN):
    la, ra = dims[0][0][0], dims[0][1][0]
    lh, lm, ll = split3(left)
    rh, rm, rl = split3(right)
    return dot(
        jnp.concatenate([lh, lh, lm, lm, lh, ll], la),
        jnp.concatenate([rh, rm, rh, rm, rl, rh], ra),
        dims,
    )


def eliminate(m_ref, qt_ref, count):
    sub = lax.broadcasted_iota(jnp.int32, (16, 128), 0)

    def panel(index, carry):
        base = pl.multiple_of(index * 16, 16)
        back = lax.rem(128 - base, 128)
        gram, rest = [], []
        for s in range(count):
            gram.append(pltpu.roll(m_ref[s, pl.ds(base, 16), :128], back, 1))
            rest.append(m_ref[s, pl.ds(base, 16), 128:])
        for j in range(16):
            for s in range(count):
                g, a = gram[s], rest[s]
                col = jnp.broadcast_to(g[:, j : j + 1], (16, 128))
                inv = lax.rsqrt(col[j : j + 1, :])
                row_g = g[j : j + 1, :] * inv
                row_a = a[j : j + 1, :] * inv
                factor = jnp.where(sub > j, col * inv, 0.0)
                gram[s] = jnp.where(sub == j, row_g, g - factor * row_g)
                rest[s] = jnp.where(sub == j, row_a, a - factor * row_a)
        for s in range(count):
            u = pltpu.roll(gram[s], base, 1)
            qt_ref[s, pl.ds(base, 16), :] = rest[s]
            uh, um, ul = split3(u)
            ah, am, al = split3(rest[s])
            wh, wm, wl = [jnp.concatenate(p, 1) for p in ((uh, ah), (um, am), (ul, al))]
            m_ref[s] -= dot(
                jnp.concatenate([uh, uh, um, um, uh, ul], 0),
                jnp.concatenate([wh, wm, wh, wm, wl, wh], 0),
                TN,
            )
        return carry

    lax.fori_loop(0, 8, panel, 0)


def flat_rows(ref, count):
    return jnp.concatenate([ref[i : i + 1, :] for i in range(count)], 1)


def blocks_of(ref, first, down, across, stride):
    lines = []
    for i in range(down):
        row = [ref[pl.ds((first + i * stride + j) * 128, 128), :] for j in range(across)]
        lines.append(row[0] if across == 1 else jnp.concatenate(row, 1))
    return lines[0] if down == 1 else jnp.concatenate(lines, 0)


TILE = 256
LOG2E = 1.4426950408889634


def sine_rows(pack_len, half):
    column = np.arange(half)
    period = np.float32(10000.0) ** ((2 * (column // 2)).astype(np.float32) / np.float32(half))
    high = pack_len // IMG_W
    angles = np.arange(max(high, IMG_W)).astype(np.float32)[:, None] / period[None, :].astype(np.float32)
    angles = angles.astype(np.float64)
    table = np.where(column[None, :] % 2 == 0, np.sin(angles), np.cos(angles)).astype(np.float32)
    both = np.zeros((high + IMG_W, 2 * half), np.float32)
    both[:high, :half] = table[:high]
    both[high:, half:] = table[:IMG_W]
    pieces, rest = [], both
    for _ in range(3):
        piece = rest.astype(ml_dtypes.bfloat16)
        pieces.append(piece)
        rest = rest - piece.astype(np.float32)
    return np.concatenate(pieces, 0)


def norm_forward(hidden):
    center = hidden - jnp.mean(hidden, axis=-1, keepdims=True)
    scale = lax.rsqrt(jnp.mean(center * center, axis=-1, keepdims=True) + NORM_EPSILON)
    return center * scale, scale


def norm_backward(grad, gain, unit, scale):
    inner = grad * gain
    mean = jnp.mean(inner, axis=-1, keepdims=True)
    along = jnp.mean(inner * unit, axis=-1, keepdims=True)
    return scale * (inner - mean - unit * along)


def column_sum(values):
    return jnp.sum(values, axis=0, keepdims=True)


def when(condition, action):
    if condition is None:
        action()
    else:
        pl.when(condition)(action)


class Post:
    def __init__(self, copy, send=None, recv=None):
        self.copy, self.send_if, self.recv_if, self.gone = copy, send, recv, False

    def start(self):
        when(self.send_if, lambda: self.copy.start())

    def recv(self):
        when(self.recv_if, lambda: self.copy.wait_recv())

    def sent(self):
        if not self.gone:
            when(self.send_if, lambda: self.copy.wait_send())
        self.gone = True


class Mail:
    def __init__(self, send_sem, recv_sem):
        self.send_sem, self.recv_sem, self.posts = send_sem, recv_sem, []

    def make(self, source, target, device, send=None, recv=None, recv_sem=None):
        index = len(self.posts)
        copy = pltpu.make_async_remote_copy(
            src_ref=source, dst_ref=target,
            send_sem=self.send_sem.at[index],
            recv_sem=self.recv_sem.at[index] if recv_sem is None else recv_sem,
            device_id=device, device_id_type=MESH,
        )
        post = Post(copy, send, recv)
        self.posts.append(post)
        return post

    def put(self, *args, **kinds):
        post = self.make(*args, **kinds)
        post.start()
        return post

    def finish(self, count):
        assert len(self.posts) == count
        for post in self.posts:
            post.sent()


def greet(devices):
    barrier = pltpu.get_barrier_semaphore()
    for device in devices:
        pl.semaphore_signal(barrier, inc=1, device_id=device, device_id_type=MESH)
    pl.semaphore_wait(barrier, len(devices))


class Sizes:
    def __init__(self, packs, rows, tok, width, hidden, owned):
        self.packs, self.rows, self.tok, self.width, self.hidden, self.owned = packs, rows, tok, width, hidden, owned
        self.pack_len = rows * tok
        self.heads = HEADS // rows
        self.part = width // rows
        self.head = width // HEADS
        self.lines = width // 128
        self.square = self.lines * self.lines
        self.total = packs * owned
        self.blocks = owned // 128
        self.slots = -(-2 * self.blocks // rows)
        place = Place(packs, rows)
        self.nx, self.ny, self.nz = place.nx, place.ny, place.nz
        self.share = self.total // (packs * rows)
        self.chunks = 2 if self.share % 32 == 0 else 1
        self.size = self.share // self.chunks
        self.late = 3 * self.part * self.lines
        self.joint = max(n for n in range(1, packs + 1) if packs % n == 0 and self.late % (16 * n) == 0)
        self.owners = -(-3 * self.square // self.blocks)
        over_x, over_y, over_z, peers = self.nx - 1, self.ny - 1, self.nz - 1, rows - 1
        gather = peers + 2 * over_x + 1 + 4 * (1 + over_y) + 2 * over_y + (2 * over_z - 1) * (2 + 2 * over_y)
        reduce = self.chunks * (1 + over_x + over_y + over_z + peers)
        vector = 1 + over_x + over_y + over_z
        bases = self.slots * (2 * over_x + 1)
        self.posts = gather + 3 * peers + reduce + packs - 1 + vector + self.owners * rows + bases


def vmem_scratch(z):
    half, most = z.nx * z.ny * z.nz, max(z.nx, z.ny)
    ring = half // min(z.nx, z.ny)
    f = lambda *shape: pltpu.VMEM(shape, F32)
    b = lambda *shape: pltpu.VMEM(shape, BF16)
    return dict(
        tokens_all=f(z.rows, z.tok, z.width),
        codes_all=pltpu.VMEM((z.rows, 2 * z.tok // 128, 128), jnp.int32),
        weights=b(z.total, 128),
        placed=b(z.pack_len, z.width), plain=b(z.pack_len, z.width),
        kf=b(z.heads, z.pack_len, 128), qf=b(z.heads, 128, z.pack_len), vf=b(z.heads, z.pack_len, 128),
        kt=b(z.part, z.pack_len), vt=b(z.part, z.pack_len), q=b(z.pack_len, z.part), ot=f(z.part, z.pack_len),
        att_post=b(z.rows, z.part, z.tok), att=b(z.rows, z.part, z.tok),
        cot=f(z.tok, z.width), layer=f(z.tok, z.width), branch=f(z.tok, z.width),
        dot_post=b(z.rows, z.part, z.tok), dot=b(z.part, z.pack_len),
        grad=f(z.total, 128), vec_part=f(32, 128),
        stage0=b(z.chunks, half, z.size, 128), recv0=b(z.chunks, half, z.size, 128),
        stage1=b(z.chunks, half * (most - 1) // most, z.size, 128),
        recv1=b(z.chunks, half * (most - 1) // most, z.size, 128),
        kept1=f(z.chunks, ring, z.size, 128),
        stage2=b(z.chunks, (most - 1) * z.nz, z.size, 128), recv2=b(z.chunks, (most - 1) * z.nz, z.size, 128),
        kept2=f(z.chunks, z.nz, z.size, 128),
        stage3=b(z.chunks, z.nz, z.size, 128), recv3=b(z.chunks, z.nz, z.size, 128),
        vec_c=f(2, 32, 128), vec_x=f(z.nx, 32, 128), vec_y=f(z.ny, 32, 128), vec_z=f(z.nz, 32, 128),
        post=b(z.rows, 3 * z.part, z.tok), got=b(z.rows, 3 * z.part, z.tok),
        late=f(z.late, 128), late_post=b(z.late, 128), late_recv=b(z.packs, z.late // z.joint, 128),
        late_share=b(z.late // z.joint, 128), late_all=b(z.rows, z.late, 128),
        owned=b(z.owned, 128),
        first=f(z.owned, 128), second=f(z.owned, 128), left=f(z.owned, 128), right=f(z.owned, 128),
        lbasis=f(z.owned, 128), rbasis=f(z.owned, 128),
        gram=f(z.slots, 128, 256), qt=f(z.slots, 128, 128), bases=f(z.rows * z.slots * 128, 128),
        first_new=f(z.owned, 128), second_new=f(z.owned, 128), master_new=f(z.owned, 128), copy_new=b(z.owned, 128),
        left_new=f(z.owned, 128), right_new=f(z.owned, 128), input=f(z.tok, z.width), vec_new=f(3, 32, 128),
    )


LOADS = ("cot", "first", "second", "left", "right", "lbasis", "rbasis")


def layer_kernel(z, names, *refs):
    inputs = (
        "tokens", "codes", "master", "vec", "table", "vec_first", "vec_second",
        "cot_in", "first_in", "second_in", "left_in", "right_in", "lbasis_in", "rbasis_in",
    )
    outputs = (
        "layer_out", "input_out", "first_out", "second_out", "master_out", "copy_out", "left_out", "right_out",
        "lbasis_out", "rbasis_out", "vec_out", "vec_first_out", "vec_second_out",
    )
    s = types.SimpleNamespace(**dict(zip(inputs + outputs + tuple(names), refs)))
    send_sem, recv_sem, load_sem, late_sem = refs[-4:]
    loads = [
        pltpu.make_async_copy(getattr(s, name + "_in"), getattr(s, name), load_sem.at[i]) for i, name in enumerate(LOADS)
    ]
    for load in loads:
        load.start()
    stores = []

    def store(source, target):
        copy = pltpu.make_async_copy(source, target, load_sem.at[len(loads) + len(stores)])
        copy.start()
        stores.append(copy)

    place = Place(z.packs, z.rows).locate()
    mail = Mail(send_sem, recv_sem)
    at, me, pack = place.at, place.r, place.p
    nx, ny, nz, rows, tok, part, head, heads = z.nx, z.ny, z.nz, z.rows, z.tok, z.part, z.head, z.heads
    lines, square, width, hidden = z.lines, z.square, z.width, z.hidden
    partner = place.peers("c")[0]
    near = {dim: place.peers(dim) for dim in ("x", "y", "z")}
    row_peers = place.row_peers()

    def source(dim, step):
        return lax.rem(at[dim] + place.size[dim] - 1 - step, place.size[dim])

    half = z.owned // 2
    quarter = half // 2

    def piece(zz, yy, k=None):
        start = (zz * ny + yy) * z.owned + at["c"] * half
        count = half
        if k is not None:
            start, count = start + k * quarter, quarter
        return s.weights.at[pl.ds(pl.multiple_of(start, 16), count), :]

    def to(dim, index):
        return place.device(**{dim: index})

    up, down = lax.rem(at["z"] + 1, nz), lax.rem(at["z"] + nz - 1, nz)
    inner = at["z"] >= 1
    below_top = at["z"] + 1 < nz
    send_codes = [mail.make(s.codes, s.codes_all.at[me], device) for device in row_peers]
    send_x = [mail.make(s.tokens, s.tokens_all.at[me], device) for _, device in near["x"]]
    send_c = mail.make(s.tokens, s.tokens_all.at[me], partner[1])
    relay_x = []
    for step in range(nx - 1):
        row = source("x", step) * 2 + at["c"]
        relay_x.append(mail.make(s.tokens_all.at[row], s.tokens_all.at[row], partner[1]))
    chain, chain_y, chain_c, chain_yc = [], [], [], []
    for k in range(2):
        part_k = piece(0, at["y"], k)
        chain.append(mail.make(part_k, part_k, to("z", up), send=below_top, recv=inner))
        chain_y.append([mail.make(part_k, part_k, device) for _, device in near["y"]])
        chain_c.append(mail.make(part_k, part_k, partner[1], send=inner, recv=inner))
        chain_yc.append([])
        for step in range(ny - 1):
            part_k = piece(0, source("y", step), k)
            chain_yc[k].append(mail.make(part_k, part_k, partner[1]))

    def spread(zz, condition):
        mine = piece(zz, at["y"])
        over_y = [mail.make(mine, mine, device, condition, condition) for _, device in near["y"]]
        theirs = [piece(zz, source("y", step)) for step in range(ny - 1)]
        over_c = [mail.make(ref, ref, partner[1], condition, condition) for ref in theirs]
        return over_y, over_c

    own_y, own_c = spread(at["z"], inner)
    ups, downs = [], []
    for j in range(nz - 2):
        mine, coming = lax.rem(at["z"] + nz - j, nz), lax.rem(at["z"] + nz - 1 - j, nz)
        there = at["z"] - 1 - j >= 1
        hop = mail.make(piece(mine, at["y"]), piece(mine, at["y"]), to("z", up), (at["z"] - j >= 1) & below_top, there)
        core = mail.make(piece(coming, at["y"]), piece(coming, at["y"]), partner[1], there, there)
        ups.append((hop, core) + spread(coming, there))
    for j in range(nz - 1):
        mine, coming = lax.rem(at["z"] + j, nz), lax.rem(at["z"] + 1 + j, nz)
        there = at["z"] + 1 + j < nz
        hop = mail.make(piece(mine, at["y"]), piece(mine, at["y"]), to("z", down), inner & (at["z"] + j < nz), there)
        core = mail.make(piece(coming, at["y"]), piece(coming, at["y"]), partner[1], there, there)
        downs.append((hop, core) + spread(coming, there))

    own = pl.ds(pl.multiple_of(pack * z.owned, 16), z.owned)
    s.weights[own, :] = s.master[...].astype(BF16)
    greet(row_peers + [device for dim in ("y", "z") for _, device in near[dim]])
    for post in send_codes + send_x + [send_c]:
        post.start()

    def first_hop():
        for k in range(2):
            chain[k].start()
            for post in chain_y[k]:
                post.start()

    pl.when(at["z"] == 0)(first_hop)
    s.tokens_all[me] = s.tokens[...]
    s.codes_all[me] = s.codes[...]
    for post in send_codes:
        post.recv()

    groups = tok // 128
    high = z.pack_len // IMG_W
    ids, pad = s.codes_all[:, :groups, :], s.codes_all[:, groups:, :]
    index = (
        lax.broadcasted_iota(jnp.int32, ids.shape, 0) * tok
        + lax.broadcasted_iota(jnp.int32, ids.shape, 1) * 128
        + lax.broadcasted_iota(jnp.int32, ids.shape, 2)
    )
    starts = jnp.zeros(ids.shape, jnp.int32)
    for image in range(8):
        count = jnp.sum(jnp.where(ids == image, 1.0, 0.0)).astype(jnp.int32)
        starts = starts + jnp.where(ids > image, count, 0)
    places = index - starts
    on_y = lax.div(places, IMG_W)
    on_x = places - on_y * IMG_W

    def line(values, r):
        return jnp.concatenate([values[r, g : g + 1, :] for g in range(groups)], 1)

    def vector(first, count=lines):
        return jnp.concatenate([s.vec[first + i : first + i + 1, :] for i in range(count)], 1)

    def projections(pos_ref):
        for r in range(rows):
            sub = lax.broadcasted_iota(jnp.int32, (high, tok), 0)
            hot = jnp.concatenate(
                [
                    jnp.where(sub == line(on_y, r), 1.0, 0.0),
                    jnp.where(sub[:IMG_W] == line(on_x, r), 1.0, 0.0),
                ],
                0,
            ).astype(BF16)
            pos_ref[r] = dot(jnp.concatenate([hot] * 3, 0), s.table[...], TN)
        for k in range(2):

            def forward():
                chain[k].copy.wait_recv()
                chain[k].start()
                chain_c[k].copy.start()
                for post in chain_y[k]:
                    post.start()

            pl.when(inner)(forward)
        for post, relay in zip(send_x, relay_x):
            post.recv()
            relay.start()
        for k in range(2):
            for post, relay in zip(chain_y[k], chain_yc[k]):
                post.recv()
                relay.start()
        for post in [send_c] + relay_x + chain_c + chain_yc[0] + chain_yc[1]:
            post.recv()
        for post in own_y + [ups[0][0], downs[0][0]] if ups else own_y + [downs[0][0]]:
            post.start()
        pick = (
            lax.broadcasted_iota(jnp.int32, (width, part), 0)
            == lax.broadcasted_iota(jnp.int32, (width, part), 1) + me * part
        )
        pick = jnp.where(pick, 1.0, 0.0).astype(BF16)
        wq, wk, wv = [dot(blocks_of(s.weights, n * square, lines, lines, lines), pick).astype(BF16) for n in range(3)]

        def bias(first):
            row = jnp.broadcast_to(vector(first), (8, width))
            return pltpu.roll(row, lax.rem(width - me * part, width), 1)[:1, :part]

        bias_q, bias_v = bias(0), bias(lines)
        scale = LOG2E * head**-0.5
        sub8 = lax.broadcasted_iota(jnp.int32, (8, tok), 0)
        for r in range(rows):
            span = slice(r * tok, (r + 1) * tok)
            rows_in = s.tokens_all[r]
            placed = (rows_in + pos_ref[r]).astype(BF16)
            plain = rows_in.astype(BF16)
            s.placed[span, :] = placed
            s.plain[span, :] = plain
            q = (dot(placed, wq) + bias_q).astype(BF16)
            k = dot(placed, wk).astype(BF16)
            v = (dot(plain, wv) + bias_v).astype(BF16)
            s.q[span, :] = q
            qt, kt, vt = q.astype(F32).T, k.astype(F32).T, v.astype(F32).T
            s.kt[:, span] = kt.astype(BF16)
            s.vt[:, span] = vt.astype(BF16)
            scaled = qt * scale
            q_high = scaled.astype(BF16).astype(F32)
            q_low = scaled - q_high
            same = sub8 == line(ids, r)
            ones = jnp.ones((8, tok), F32)
            free = jnp.zeros((128 - 2 * head - 8, tok), F32)
            barred = jnp.where(same & (line(pad, r) == 0), 0.0, MASKED_SCORE)
            for h in range(heads):
                mine = slice(h * head, (h + 1) * head)
                s.qf[h, :, span] = jnp.concatenate(
                    [q_high[mine], q_low[mine], jnp.where(same, 1.0, 0.0), free], 0
                ).astype(BF16)
                s.kf[h, span, :] = jnp.concatenate([kt[mine], kt[mine], barred, ones, free[8:]], 0).T.astype(BF16)
                s.vf[h, span, :] = jnp.concatenate([vt[mine], vt[mine], ones, free], 0).T.astype(BF16)

    pl.run_scoped(projections, pltpu.VMEM((rows, tok, width), F32))

    att_posts = []
    for step in range(rows - 1):
        device = {"pack": pack, "row": lax.rem(me + 1 + step, rows)}
        att_posts.append(mail.make(s.att_post.at[step], s.att.at[me], device))

    def weight_stage(stage):
        if stage == 0:
            for post, core in zip(own_y, own_c):
                post.recv()
                core.start()
        for moves in (ups, downs):
            if 0 < stage <= len(moves):
                _, _, over_y, over_c = moves[stage - 1]
                for post, core in zip(over_y, over_c):
                    post.recv()
                    core.start()
            if stage < len(moves):
                hop, core, over_y, _ = moves[stage]
                hop.recv()
                if stage + 1 < len(moves):
                    moves[stage + 1][0].start()
                for post in [core] + over_y:
                    post.start()

    stages = nz
    per = tok // TILE
    tiles = rows * per

    def attend_step(number, carry):
        step = lax.div(number, per)
        offset = lax.rem(number, per)
        dest = lax.rem(me + 1 + step, rows)
        span = pl.ds(pl.multiple_of(dest * tok + offset * TILE, TILE), TILE)
        for stage in range(stages - 1):
            pl.when(number == (stage + 1) * tiles // stages)(functools.partial(weight_stage, stage))
        pieces = []
        for h in range(heads):
            scores = dot(s.kf[h], s.qf[h, :, span])
            largest = jnp.max(scores, axis=0, keepdims=True)
            weights = jnp.exp2(scores - largest)
            total = jnp.sum(weights, axis=0, keepdims=True)
            out = dot(s.vt[h * head : (h + 1) * head, :], weights.astype(BF16))
            pieces.append(out * (1.0 / total))
            lse = -(largest + jnp.log2(total))
            lh = lse.astype(BF16).astype(F32)
            lm = (lse - lh).astype(BF16).astype(F32)
            tail = s.qf[h, 2 * head : 2 * head + 16, span].astype(F32)
            tail = jnp.concatenate([tail[:8], lh, lm, lse - lh - lm, jnp.zeros((5, TILE), F32)], 0)
            s.qf[h, 2 * head : 2 * head + 16, span] = tail.astype(BF16)
        out = pieces[0] if heads == 1 else jnp.concatenate(pieces, 0)
        s.ot[:, span] = out
        s.att_post[step, :, pl.ds(pl.multiple_of(offset * TILE, TILE), TILE)] = out.astype(BF16)
        for there in range(rows - 1):
            pl.when(number == (there + 1) * per - 1)(functools.partial(att_posts[there].start))
        return carry

    lax.fori_loop(0, tiles, attend_step, 0)
    weight_stage(stages - 1)
    s.att[me] = s.att_post[rows - 1]
    for post in att_posts:
        post.recv()
    for post in own_c + [p for moves in (ups, downs) for move in moves for p in [move[1]] + move[3]]:
        post.recv()

    dot_lanes = pl.ds(pl.multiple_of(me * tok, 128), tok)
    dot_posts = [mail.make(s.dot_post.at[d["row"]], s.dot.at[:, dot_lanes], d) for d in row_peers]
    loads[0].wait()

    def middle(act_ref, slope_ref):
        count = 4
        wide = hidden // count // 128

        def put_vector(first, value):
            for i in range(value.shape[1] // 128):
                s.vec_part[first + i : first + i + 1, :] = value[:, i * 128 : (i + 1) * 128]

        bias_out, gain_one, shift_one = vector(2 * lines), vector(3 * lines), vector(4 * lines)
        last = 5 * lines + hidden // 128
        bias_two, gain_two, shift_two = vector(last), vector(last + lines), vector(last + 2 * lines)

        def w_one(n):
            return blocks_of(s.weights, 4 * square + n * wide, lines, wide, hidden // 128)

        def w_two(n):
            first = 4 * square + lines * hidden // 128
            return blocks_of(s.weights, first + n * wide * lines, wide, lines, lines)

        def put_grad(first, stride, value):
            for i in range(value.shape[0] // 128):
                for j in range(value.shape[1] // 128):
                    row = (3 * square + first + i * stride + j) * 128
                    s.grad[row : row + 128, :] = value[i * 128 : (i + 1) * 128, j * 128 : (j + 1) * 128]

        attended_t = jnp.concatenate([s.att[r] for r in range(rows)], 0)
        w_out = blocks_of(s.weights, 3 * square, lines, lines, lines)
        branch = dot(attended_t, w_out, TN) + bias_out
        unit_one, scale_one = norm_forward(s.tokens[...] + branch)
        normed = unit_one * gain_one + shift_one
        normed_low = normed.astype(BF16)
        second = jnp.zeros((tok, width), F32)
        for n in range(count):
            pre = dot(normed_low, w_one(n)) + vector(5 * lines + n * wide, wide)
            square_pre = pre * pre
            curve = jnp.tanh(0.7978845608028654 * pre * (1.0 + 0.044715 * square_pre))
            half_one = 0.5 * (1.0 + curve)
            act = (pre * half_one).astype(BF16)
            slope_ref[n] = half_one + 0.5 * pre * (1.0 - curve * curve) * (
                0.7978845608028654 * (1.0 + 0.134145 * square_pre)
            )
            act_ref[n] = act
            second = second + dot(act, w_two(n))
        unit_two, scale_two = norm_forward(normed + (second + bias_two))
        s.layer[...] = unit_two * gain_two + shift_two
        cot = s.cot[...]
        put_vector(last + lines, column_sum(cot * unit_two))
        put_vector(last + 2 * lines, column_sum(cot))
        sum_grad = norm_backward(cot, gain_two, unit_two, scale_two)
        second_grad = sum_grad.astype(BF16)
        put_vector(last, column_sum(second_grad.astype(F32)))
        normed_grad = sum_grad
        for n in range(count):
            two = w_two(n)
            hidden_grad = (dot(second_grad, two, NT) * slope_ref[n]).astype(BF16)
            put_vector(5 * lines + n * wide, column_sum(hidden_grad.astype(F32)))
            normed_grad = normed_grad + dot(hidden_grad, w_one(n), NT)
            first = lines * hidden // 128 + square + n * wide * lines
            put_grad(first, lines, dot(act_ref[n], second_grad, TN))
            put_grad(square + n * wide, hidden // 128, dot(normed_low, hidden_grad, TN))
        put_vector(3 * lines, column_sum(normed_grad * unit_one))
        put_vector(4 * lines, column_sum(normed_grad))
        branch_grad = norm_backward(normed_grad, gain_one, unit_one, scale_one)
        s.branch[...] = branch_grad
        branch_low = branch_grad.astype(BF16)
        grad_t = dot(w_out, branch_low, NT).astype(BF16)
        for r in range(rows):
            s.dot_post[r] = grad_t[r * part : (r + 1) * part, :]
        for post in dot_posts:
            post.start()
        s.dot[:, dot_lanes] = s.dot_post[me]
        put_vector(2 * lines, column_sum(branch_low.astype(F32)))
        put_grad(0, lines, dot(attended_t, branch_low))

    pl.run_scoped(middle, pltpu.VMEM((4, tok, hidden // 4), BF16), pltpu.VMEM((4, tok, hidden // 4), F32))

    store(s.layer, s.layer_out)

    chunks, size, share = z.chunks, z.size, z.share
    s.grad[: 3 * square * 128, :] = jnp.zeros((3 * square * 128, 128), F32)

    def grad_rows(chunk, x, c, y, z):
        row = (z * ny + y) * (rows * share) + (x * 2 + c) * share + chunk * size
        return s.grad[pl.ds(pl.multiple_of(row, 16), size), :]

    def order(chunk):
        return ("x", "y") if chunk % 2 == 0 else ("y", "x")

    def spot(chunk, one, two, zz):
        return {order(chunk)[0]: one, order(chunk)[1]: two, "z": zz}

    hops0, hops1, hops2, hops3, hops4 = [], [], [], [], []
    for chunk in range(chunks):
        n2 = place.size[order(chunk)[1]]
        hops0.append(mail.make(s.stage0.at[chunk], s.recv0.at[chunk], partner[1]))
        made = []
        for step, (_, device) in enumerate(near[order(chunk)[0]]):
            span = pl.ds(step * n2 * nz, n2 * nz)
            made.append(mail.make(s.stage1.at[chunk, span], s.recv1.at[chunk, span], device))
        hops1.append(made)
        made = []
        for step, (_, device) in enumerate(near[order(chunk)[1]]):
            span = pl.ds(step * nz, nz)
            made.append(mail.make(s.stage2.at[chunk, span], s.recv2.at[chunk, span], device))
        hops2.append(made)
        hops3.append(
            [mail.make(s.stage3.at[chunk, step], s.recv3.at[chunk, step], d) for step, (_, d) in enumerate(near["z"])]
        )
        mine = pl.ds(pl.multiple_of(me * share + chunk * size, 16), size)
        hops4.append([mail.make(s.owned.at[mine], s.owned.at[mine], device) for device in row_peers])

    def reduce_cores():
        for chunk in range(chunks):
            n1, n2 = [place.size[d] for d in order(chunk)]
            for one in range(n1):
                for two in range(n2):
                    for zz in range(nz):
                        rows_of = grad_rows(chunk, c=partner[0], **spot(chunk, one, two, zz))
                        s.stage0[chunk, (one * n2 + two) * nz + zz] = rows_of.astype(BF16)
            hops0[chunk].start()

    def reduce_first():
        for chunk in range(chunks):
            n1, n2 = [place.size[d] for d in order(chunk)]
            hops0[chunk].recv()

            def summed(one, two, zz):
                slot = (one * n2 + two) * nz + zz
                rows_of = grad_rows(chunk, c=at["c"], **spot(chunk, one, two, zz))
                return rows_of + s.recv0[chunk, slot].astype(F32)

            for step, (there, _) in enumerate(near[order(chunk)[0]]):
                for two in range(n2):
                    for zz in range(nz):
                        s.stage1[chunk, step * n2 * nz + two * nz + zz] = summed(there, two, zz).astype(BF16)
                hops1[chunk][step].start()
            for two in range(n2):
                for zz in range(nz):
                    s.kept1[chunk, two * nz + zz] = summed(at[order(chunk)[0]], two, zz)

    def reduce_second():
        for chunk in range(chunks):
            n1, n2 = [place.size[d] for d in order(chunk)]
            for hop in hops1[chunk]:
                hop.recv()

            def summed(two, zz):
                total = s.kept1[chunk, two * nz + zz]
                for step in range(n1 - 1):
                    total = total + s.recv1[chunk, step * n2 * nz + two * nz + zz].astype(F32)
                return total

            for step, (there, _) in enumerate(near[order(chunk)[1]]):
                for zz in range(nz):
                    s.stage2[chunk, step * nz + zz] = summed(there, zz).astype(BF16)
                hops2[chunk][step].start()
            for zz in range(nz):
                s.kept2[chunk, zz] = summed(at[order(chunk)[1]], zz)

    def reduce_third():
        for chunk in range(chunks):
            n2 = place.size[order(chunk)[1]]
            for hop in hops2[chunk]:
                hop.recv()

            def summed(zz):
                total = s.kept2[chunk, zz]
                for step in range(n2 - 1):
                    total = total + s.recv2[chunk, step * nz + zz].astype(F32)
                return total

            for step, (there, _) in enumerate(near["z"]):
                s.stage3[chunk, step] = summed(there).astype(BF16)
                hops3[chunk][step].start()
            s.kept2[chunk, at["z"]] = summed(at["z"])

    def reduce_last():
        for chunk in range(chunks):
            total = s.kept2[chunk, at["z"]]
            for step, hop in enumerate(hops3[chunk]):
                hop.recv()
                total = total + s.recv3[chunk, step].astype(F32)
            mine = pl.ds(pl.multiple_of(me * share + chunk * size, 16), size)
            s.owned[mine, :] = total.astype(BF16)
            for hop in hops4[chunk]:
                hop.start()

    reduce_stages = ((0, reduce_first), (3, reduce_second), (5, reduce_third))
    reduce_cores()
    for post in dot_posts:
        post.recv()

    scale = head**-0.5
    posts = [mail.make(s.post.at[d["row"]], s.got.at[me], d) for d in row_peers]

    def backward(df_ref, mix_ref, both_ref, pair_ref, qt_ref):
        lane = lax.broadcasted_iota(jnp.int32, (tok, part), 1)
        for r in range(rows):
            span = slice(r * tok, (r + 1) * tok)
            grad_t = s.dot[:, span].astype(F32)
            center = grad_t * s.ot[:, span]
            grad_rows_in = grad_t.T
            queries = s.q[span, :].astype(F32)
            scaled = grad_t * scale
            g_high = scaled.astype(BF16).astype(F32)
            g_low = scaled - g_high
            for h in range(heads):
                own_lines = slice(h * head, (h + 1) * head)
                shift = -scale * column_sum(center[own_lines])
                sh = shift.astype(BF16).astype(F32)
                sm = (shift - sh).astype(BF16).astype(F32)
                rest = jnp.zeros((128 - 2 * head - 3, tok), F32)
                df_ref[h, :, span] = jnp.concatenate(
                    [g_high[own_lines], g_low[own_lines], sh, sm, shift - sh - sm, rest], 0
                ).astype(BF16)
                mine = (lane >= h * head) & (lane < (h + 1) * head)
                none = jnp.zeros((tok, part), F32)
                free = [jnp.zeros((tok, 128 - 2 * part), F32)] if part < 64 else []
                mix_ref[2 * h, span, :] = jnp.concatenate(
                    [jnp.where(mine, grad_rows_in, 0.0), none] + free, 1
                ).astype(BF16)
                mix_ref[2 * h + 1, span, :] = jnp.concatenate(
                    [none, jnp.where(mine, queries, 0.0)] + free, 1
                ).astype(BF16)
        pair_ref[...] = jnp.zeros_like(pair_ref)
        turns = z.pack_len // TILE

        def tile_step(number, carry):
            span = pl.ds(pl.multiple_of(number * TILE, TILE), TILE)
            for eighth, action in reduce_stages:
                pl.when(number == eighth * turns // 8)(action)
            pieces, mix = [], []
            for h in range(heads):
                probs = jnp.exp2(dot(s.kf[h], s.qf[h, :, span]))
                along = dot(s.vf[h], df_ref[h, :, span])
                both_ref[:, 2 * h * TILE : (2 * h + 1) * TILE] = probs.astype(BF16)
                score_grad = (probs * along).astype(BF16)
                both_ref[:, (2 * h + 1) * TILE : (2 * h + 2) * TILE] = score_grad
                pieces.append(dot(s.kt[h * head : (h + 1) * head, :], score_grad))
                mix += [mix_ref[2 * h, span, :], mix_ref[2 * h + 1, span, :]]
            qt_ref[:, span] = pieces[0] if heads == 1 else jnp.concatenate(pieces, 0)
            pair_ref[...] += dot(both_ref[...], jnp.concatenate(mix, 0))
            return carry

        lax.fori_loop(0, turns, tile_step, 0)
        for r in range(rows):
            span = slice(r * tok, (r + 1) * tok)
            pair = pair_ref[span, :].T
            s.post[r] = jnp.concatenate([qt_ref[:, span], pair[part : 2 * part], pair[:part]], 0).astype(BF16)

    pl.run_scoped(
        backward,
        pltpu.VMEM((heads, 128, z.pack_len), BF16),
        pltpu.VMEM((2 * heads, z.pack_len, 128), BF16),
        pltpu.VMEM((z.pack_len, 2 * heads * TILE), BF16),
        pltpu.VMEM((z.pack_len, 128), F32),
        pltpu.VMEM((part, z.pack_len), F32),
    )

    joint, owners = z.joint, z.owners
    size_l = z.late // joint
    for kind, first, last in (("placed", 0, 2 * part), ("plain", 2 * part, 3 * part)):
        base = getattr(s, kind)
        total = jnp.zeros((last - first, width), F32)
        for r in range(rows):
            total = total + dot(s.post[r, first:last, :], base[r * tok : (r + 1) * tok, :])
        for i in range(lines):
            row = i * 3 * part + first
            s.late[row : row + last - first, :] = total[:, i * 128 : (i + 1) * 128]
    s.late_post[...] = s.late[...].astype(BF16)
    spread_posts = []
    joined = None if joint == z.packs else pack < joint
    for step in range(1, z.packs):
        there = lax.rem(pack + step, z.packs)
        lands = None if joint == z.packs else there < joint
        rows_of = pl.ds(pl.multiple_of(lax.rem(there, joint) * size_l, 16), size_l)
        spread_posts.append(
            mail.put(
                s.late_post.at[rows_of, :], s.late_recv.at[step - 1], {"pack": there, "row": me}, lands, joined
            )
        )

    ones = jnp.ones((16, tok), BF16)
    sums = jnp.zeros((16, 3 * part), F32)
    for r in range(rows):
        sums = sums + dot(ones, s.post[r], NT)
    for n in (0, 2):
        row = jnp.concatenate([sums[:8, n * part : (n + 1) * part], jnp.zeros((8, width - part), F32)], 1)
        row = pltpu.roll(row, me * part, 1)
        for i in range(lines):
            line_of = (n // 2) * lines + i
            s.vec_part[line_of : line_of + 1, :] = row[:1, i * 128 : (i + 1) * 128]

    def vec_step(dim, buffer, value):
        buffer[at[dim]] = value
        return [mail.put(buffer.at[at[dim]], buffer.at[at[dim]], device) for _, device in place.peers(dim)]

    def vec_sum(hops, buffer):
        for hop in hops:
            hop.recv()
        total = buffer[0]
        for number in range(1, buffer.shape[0]):
            total = total + buffer[number]
        return total

    vec_hops = vec_step("c", s.vec_c, s.vec_part[...])
    reduce_last()
    own_late = pl.ds(pl.multiple_of(lax.rem(pack, joint) * size_l, 16), size_l)
    for post in spread_posts:
        post.recv()
    total = s.late[own_late, :]
    for step in range(z.packs - 1):
        total = total + s.late_recv[step].astype(F32)
    s.late_share[...] = total.astype(BF16)
    s.late_all[me, own_late, :] = total.astype(BF16)
    for owner in range(owners):
        for step in range(rows):
            leaves = [] if joint == z.packs else [pack < joint]
            if step == 0:
                leaves.append(pack != owner)
            leaves = functools.reduce(jnp.logical_and, leaves) if leaves else None
            mail.put(
                s.late_share, s.late_all.at[me, own_late, :],
                {"pack": pack * 0 + owner, "row": lax.rem(me + step, rows)}, leaves, None,
                late_sem.at[lax.rem(pack, joint), step],
            )
    vec_hops = vec_step("x", s.vec_x, vec_sum(vec_hops, s.vec_c))
    for post in posts:
        post.start()
    s.got[me] = s.post[me]
    for load in loads[1:]:
        load.wait()
    for chunk in range(chunks):
        for hop in hops4[chunk]:
            hop.recv()
            hop.sent()
    vec_hops = vec_step("y", s.vec_y, vec_sum(vec_hops, s.vec_x))

    def late_wait():
        for giver in range(joint):
            for step in range(rows):

                def wait():
                    pltpu.make_async_remote_copy(
                        src_ref=s.late_share, dst_ref=s.late_all.at[0, :size_l, :],
                        send_sem=send_sem.at[0], recv_sem=late_sem.at[giver, step],
                        device_id={"pack": pack, "row": lax.rem(me + 1, rows)}, device_id_type=MESH,
                    ).wait_recv()

                when((pack != giver) if step == 0 else None, wait)
        for b in range(3 * square):
            kind, i, j = b // square, b % square // lines, b % lines

            def place_block():
                start = (i * 3 + kind) * part
                found = [s.late_all[r, start : start + part, :] for r in range(j * 128 // part, (j + 1) * 128 // part)]
                block = jnp.concatenate(found, 0).astype(F32).T
                row = b % z.blocks * 128
                s.owned[row : row + 128, :] = block.astype(BF16)

            pl.when(pack == b // z.blocks)(place_block)

    pl.when(pack < owners)(late_wait)
    vec_hops = vec_step("z", s.vec_z, vec_sum(vec_hops, s.vec_y))

    blocks, slots = z.blocks, z.slots
    for n in range(slots):
        t = jnp.minimum(me * slots + n, 2 * blocks - 1)
        is_right = t >= blocks
        rows_of = pl.ds(pl.multiple_of(jnp.where(is_right, t - blocks, t) * 128, 128), 128)
        g = s.owned[rows_of, :].astype(F32)
        g = jnp.where(is_right, g.T, g).astype(BF16)
        stat = jnp.where(is_right, s.right[rows_of, :], s.left[rows_of, :])
        basis = jnp.where(is_right, s.rbasis[rows_of, :], s.lbasis[rows_of, :])
        new = BETA_TWO * stat + (1.0 - BETA_TWO) * dot(g, g, NT)
        a = dot6(new, basis)
        a_t = a.T
        s.gram[n, :, :128] = dot6(a_t, a)
        s.gram[n, :, 128:] = a_t
    eliminate(s.gram, s.qt, slots)

    def base_at(row, n):
        return s.bases.at[pl.ds(pl.multiple_of((row * slots + n) * 128, 128), 128), :]

    base_c, base_x, base_f = [], [], []
    for n in range(slots):
        s.bases[pl.ds(pl.multiple_of((me * slots + n) * 128, 128), 128), :] = s.qt[n].T
        base_x.append([mail.put(base_at(me, n), base_at(me, n), device) for _, device in near["x"]])
        base_c.append(mail.put(base_at(me, n), base_at(me, n), partner[1]))

    def block_step(number, carry):
        rows_of = pl.ds(pl.multiple_of(number * 128, 128), 128)
        g = s.owned[rows_of, :]
        s.left_new[rows_of, :] = BETA_TWO * s.left[rows_of, :] + (1.0 - BETA_TWO) * dot(g, g, NT)
        s.right_new[rows_of, :] = BETA_TWO * s.right[rows_of, :] + (1.0 - BETA_TWO) * dot(g, g, TN)
        lb, rb = s.lbasis[rows_of, :], s.rbasis[rows_of, :]
        lh, ll = split2(lb)
        turned = dot(jnp.concatenate([lh, ll], 0), jnp.concatenate([g, g], 0), TN)
        rotated = dot3(turned, rb)
        first = BETA_ONE * s.first[rows_of, :] + (1.0 - BETA_ONE) * rotated
        second = BETA_TWO * s.second[rows_of, :] + (1.0 - BETA_TWO) * rotated * rotated
        s.first_new[rows_of, :] = first
        s.second_new[rows_of, :] = second
        ratio = first / (1.0 - BETA_ONE**STEP) / (jnp.sqrt(second / (1.0 - BETA_TWO**STEP)) + EPSILON)
        stepped = dot3(dot3(lb, ratio), rb, NT)
        weights = s.master[rows_of, :]
        weights = weights - LEARN_RATE * (stepped + WEIGHT_DECAY * weights)
        s.master_new[rows_of, :] = weights
        s.copy_new[rows_of, :] = weights.astype(BF16)
        return carry

    for n in range(slots):
        lax.fori_loop(blocks * n // slots, blocks * (n + 1) // slots, block_step, 0)
        for step, hop in enumerate(base_x[n]):
            hop.recv()
            row = source("x", step) * 2 + at["c"]
            base_f.append(mail.put(base_at(row, n), base_at(row, n), partner[1]))
    for post in posts:
        post.recv()
    total = s.branch[...]
    for n in range(3):
        grad_t = jnp.concatenate([s.got[r, n * part : (n + 1) * part, :] for r in range(rows)], 0)
        weight = blocks_of(s.weights, n * square, lines, lines, lines)
        total = total + dot(grad_t, weight, (((0,), (1,)), ((), ())))
    s.input[...] = total
    store(s.input, s.input_out)
    for name in ("first", "second", "master", "copy", "left", "right"):
        store(getattr(s, name + "_new"), getattr(s, name + "_out"))
    grad = vec_sum(vec_hops, s.vec_z)
    first = BETA_ONE * s.vec_first[...] + (1.0 - BETA_ONE) * grad
    second = BETA_TWO * s.vec_second[...] + (1.0 - BETA_TWO) * grad * grad
    ratio = first / (1.0 - BETA_ONE**STEP) / (jnp.sqrt(second / (1.0 - BETA_TWO**STEP)) + EPSILON)
    s.vec_new[0] = s.vec[...] - LEARN_RATE * ratio
    s.vec_new[1] = first
    s.vec_new[2] = second
    for number, name in enumerate(("vec", "vec_first", "vec_second")):
        store(s.vec_new.at[number], getattr(s, name + "_out"))
    for hop in base_c + base_f:
        hop.recv()
    store(s.bases.at[: z.owned, :], s.lbasis_out)
    store(s.bases.at[z.owned : 2 * z.owned, :], s.rbasis_out)
    for copy in stores:
        copy.wait()
    mail.finish(z.posts)


def finish_kernel(count, *refs):
    sems = refs[-1]
    loads = [pltpu.make_async_copy(refs[i], refs[2 * count + i], sems.at[i]) for i in range(count)]
    stores = [pltpu.make_async_copy(refs[2 * count + i], refs[count + i], sems.at[count + i]) for i in range(count)]
    for load in loads:
        load.start()
    for load, copy in zip(loads, stores):
        load.wait()
        copy.start()
    for copy in stores:
        copy.wait()


def shards(
    tokens, cotangent, segment_ids, padding, master, moment_first, moment_second,
    stat_left, stat_right, basis_left, basis_right, vec_params, vec_first, vec_second,
):
    packs, rows = lax.axis_size("pack"), lax.axis_size("row")
    tok, width = tokens.shape
    z = Sizes(packs, rows, tok, width, vec_params.shape[0] - 8 * width, master.shape[0])
    codes = jnp.concatenate([segment_ids.reshape(-1, 128), padding.reshape(-1, 128)], 0)
    table = jnp.asarray(sine_rows(z.pack_len, width // 2))
    full = jax.ShapeDtypeStruct(master.shape, F32)
    layer = jax.ShapeDtypeStruct(tokens.shape, F32)
    shapes = (layer, layer, full, full, full, jax.ShapeDtypeStruct(master.shape, BF16), full, full, full, full)
    shapes = shapes + (jax.ShapeDtypeStruct((32, 128), F32),) * 3
    scratch = vmem_scratch(z)
    vm, hbm = pl.BlockSpec(memory_space=pltpu.VMEM), pl.BlockSpec(memory_space=pl.ANY)
    outs = pl.pallas_call(
        functools.partial(layer_kernel, z, tuple(scratch)),
        out_shape=shapes,
        in_specs=[vm] * 7 + [hbm] * 7,
        out_specs=(hbm,) * len(shapes),
        scratch_shapes=list(scratch.values())
        + [
            pltpu.SemaphoreType.DMA((z.posts,)),
            pltpu.SemaphoreType.DMA((z.posts,)),
            pltpu.SemaphoreType.DMA((len(LOADS) + len(shapes),)),
            pltpu.SemaphoreType.DMA((packs, rows)),
        ],
        compiler_params=pltpu.CompilerParams(collective_id=1, has_side_effects=True, vmem_limit_bytes=63 << 20),
        name="layer",
    )(
        tokens, codes, master, vec_params.reshape(32, 128), table,
        vec_first.reshape(32, 128), vec_second.reshape(32, 128),
        cotangent, moment_first, moment_second, stat_left, stat_right, basis_left, basis_right,
    )
    outs = pl.pallas_call(
        functools.partial(finish_kernel, len(shapes)),
        out_shape=shapes,
        in_specs=[hbm] * len(shapes),
        out_specs=(hbm,) * len(shapes),
        scratch_shapes=[pltpu.VMEM(shape.shape, shape.dtype) for shape in shapes]
        + [pltpu.SemaphoreType.DMA((2 * len(shapes),))],
        compiler_params=pltpu.CompilerParams(vmem_limit_bytes=63 << 20),
        name="finish",
    )(*outs)
    return outs[:-3] + tuple(out.reshape(-1) for out in outs[-3:])


def solution(mesh):
    placed = (
        P(("pack", "row"), None),
        P(("pack", "row"), None),
        P(("pack", "row")),
        P(("pack", "row")),
        P("pack", None),
        P("pack", None),
        P("pack", None),
        P("pack", None),
        P("pack", None),
        P("pack", None),
        P("pack", None),
        P(),
        P(),
        P(),
    )
    return jax.shard_map(
        shards,
        mesh=mesh,
        in_specs=placed,
        out_specs=(
            P(("pack", "row"), None),
            P(("pack", "row"), None),
            P("pack", None),
            P("pack", None),
            P("pack", None),
            P("pack", None),
            P("pack", None),
            P("pack", None),
            P("pack", None),
            P("pack", None),
            P(),
            P(),
            P(),
        ),
        check_vma=False,
    )
```

```python
import functools
import types
import jax
import ml_dtypes
import numpy as np
import jax.numpy as jnp
from jax import lax
from jax.experimental import pallas as pl
from jax.experimental.pallas import tpu as pltpu
from jax.sharding import PartitionSpec as P

HEADS = 8
IMG_W = 32
MASKED_SCORE = -1e30
NORM_EPSILON = 1e-05
STEP = 10
BETA_ONE = 0.9
BETA_TWO = 0.95
LEARN_RATE = 0.25
WEIGHT_DECAY = 0.01
EPSILON = 1e-08
F32 = jnp.float32
BF16 = jnp.bfloat16
NN = (((1,), (0,)), ((), ()))
NT = (((1,), (1,)), ((), ()))
TN = (((0,), (0,)), ((), ()))
MESH = pl.DeviceIdType.MESH


class Place:
    def __init__(self, packs, rows):
        self.packs, self.rows = packs, rows
        self.nx = rows // 2
        self.ny = self.nx if packs % self.nx == 0 else 1
        self.nz = packs // self.ny
        self.size = {"c": 2, "x": self.nx, "y": self.ny, "z": self.nz}

    def locate(self):
        self.p = lax.axis_index("pack")
        self.r = lax.axis_index("row")
        self.at = {
            "c": lax.rem(self.r, 2),
            "x": lax.div(self.r, 2),
            "y": lax.rem(self.p, self.ny),
            "z": lax.div(self.p, self.ny),
        }
        return self

    def device(self, **moved):
        at = {**self.at, **moved}
        return {"pack": at["z"] * self.ny + at["y"], "row": at["x"] * 2 + at["c"]}

    def other(self, dim, step):
        return lax.rem(self.at[dim] + step, self.size[dim])

    def peers(self, dim):
        found = []
        for step in range(1, self.size[dim]):
            there = self.other(dim, step)
            found.append((there, self.device(**{dim: there})))
        return found

    def row_peers(self):
        return [
            {"pack": self.p, "row": lax.rem(self.r + step, self.rows)} for step in range(1, self.rows)
        ]


def dot(left, right, dims=NN):
    return lax.dot_general(left, right, dims, preferred_element_type=F32)


def split2(v):
    high = v.astype(BF16)
    return high, (v - high.astype(F32)).astype(BF16)


def split3(v):
    high = v.astype(BF16)
    rest = v - high.astype(F32)
    mid = rest.astype(BF16)
    return high, mid, (rest - mid.astype(F32)).astype(BF16)


def dot3(left, right, dims=NN):
    la, ra = dims[0][0][0], dims[0][1][0]
    lh, ll = split2(left)
    rh, rl = split2(right)
    return dot(jnp.concatenate([lh, ll, lh], la), jnp.concatenate([rh, rh, rl], ra), dims)


def dot6(left, right, dims=NN):
    la, ra = dims[0][0][0], dims[0][1][0]
    lh, lm, ll = split3(left)
    rh, rm, rl = split3(right)
    return dot(
        jnp.concatenate([lh, lh, lm, lm, lh, ll], la),
        jnp.concatenate([rh, rm, rh, rm, rl, rh], ra),
        dims,
    )


def four_pivots(g, a, first, sub):
    cols = [jnp.broadcast_to(g[:, first + k : first + k + 1], (16, 128)) for k in range(4)]
    lower, inverse, factors, rows_g, rows_a = {}, [], [], [], []
    for k in range(4):
        pivot = cols[k][first + k : first + k + 1, :]
        column, row_g, row_a = cols[k], g[first + k : first + k + 1, :], a[first + k : first + k + 1, :]
        for m in range(k):
            pivot = pivot - lower[k, m] * lower[k, m]
            column = column - factors[m] * lower[k, m]
            row_g = row_g - rows_g[m] * lower[k, m]
            row_a = row_a - rows_a[m] * lower[k, m]
        inverse = lax.rsqrt(pivot)
        for n in range(k + 1, 4):
            entry = cols[k][first + n : first + n + 1, :]
            for m in range(k):
                entry = entry - lower[n, m] * lower[k, m]
            lower[n, k] = entry * inverse
        factors.append(column * inverse)
        rows_g.append(row_g * inverse)
        rows_a.append(row_a * inverse)
    below = sub > first + 3
    for k in range(4):
        factor = jnp.where(below, factors[k], 0.0)
        g = g - factor * rows_g[k]
        a = a - factor * rows_a[k]
    for k in range(4):
        g = jnp.where(sub == first + k, rows_g[k], g)
        a = jnp.where(sub == first + k, rows_a[k], a)
    return g, a


def panel_step(base, m_ref, out_ref, count):
    sub = lax.broadcasted_iota(jnp.int32, (16, 128), 0)
    back = lax.rem(128 - base, 128)
    gram = [pltpu.roll(m_ref[n, pl.ds(base, 16), :128], back, 1) for n in range(count)]
    rest = [m_ref[n, pl.ds(base, 16), 128:] for n in range(count)]
    for first in range(0, 16, 4):
        for n in range(count):
            gram[n], rest[n] = four_pivots(gram[n], rest[n], first, sub)
    for n in range(count):
        out_ref[n, pl.ds(base, 16), :] = rest[n]
    for n in range(count):
        uh, um, ul = split3(pltpu.roll(gram[n], base, 1))
        ah, am, al = split3(rest[n])
        wh, wm, wl = [jnp.concatenate(p, 1) for p in ((uh, ah), (um, am), (ul, al))]
        m_ref[n] -= dot(
            jnp.concatenate([uh, uh, um, um, uh, ul], 0),
            jnp.concatenate([wh, wm, wh, wm, wl, wh], 0),
            TN,
        )


def flat_rows(ref, count):
    return jnp.concatenate([ref[i : i + 1, :] for i in range(count)], 1)


def blocks_of(ref, first, down, across, stride):
    lines = []
    for i in range(down):
        row = [ref[pl.ds((first + i * stride + j) * 128, 128), :] for j in range(across)]
        lines.append(row[0] if across == 1 else jnp.concatenate(row, 1))
    return lines[0] if down == 1 else jnp.concatenate(lines, 0)


TILE = 256
LOG2E = 1.4426950408889634


def sine_rows(pack_len, half):
    column = np.arange(half)
    period = np.float32(10000.0) ** ((2 * (column // 2)).astype(np.float32) / np.float32(half))
    high = pack_len // IMG_W
    angles = np.arange(max(high, IMG_W)).astype(np.float32)[:, None] / period[None, :].astype(np.float32)
    angles = angles.astype(np.float64)
    table = np.where(column[None, :] % 2 == 0, np.sin(angles), np.cos(angles)).astype(np.float32)
    both = np.zeros((high + IMG_W, 2 * half), np.float32)
    both[:high, :half] = table[:high]
    both[high:, half:] = table[:IMG_W]
    pieces, rest = [], both
    for _ in range(3):
        piece = rest.astype(ml_dtypes.bfloat16)
        pieces.append(piece)
        rest = rest - piece.astype(np.float32)
    return np.concatenate(pieces, 0)


def norm_forward(hidden):
    center = hidden - jnp.mean(hidden, axis=-1, keepdims=True)
    scale = lax.rsqrt(jnp.mean(center * center, axis=-1, keepdims=True) + NORM_EPSILON)
    return center * scale, scale


def norm_backward(grad, gain, unit, scale):
    inner = grad * gain
    mean = jnp.mean(inner, axis=-1, keepdims=True)
    along = jnp.mean(inner * unit, axis=-1, keepdims=True)
    return scale * (inner - mean - unit * along)


def column_sum(values):
    return jnp.sum(values, axis=0, keepdims=True)


def when(condition, action):
    if condition is None:
        action()
    else:
        pl.when(condition)(action)


class Post:
    def __init__(self, copy, send=None, recv=None):
        self.copy, self.send_if, self.recv_if, self.gone = copy, send, recv, False

    def start(self):
        when(self.send_if, lambda: self.copy.start())

    def recv(self):
        when(self.recv_if, lambda: self.copy.wait_recv())

    def sent(self):
        if not self.gone:
            when(self.send_if, lambda: self.copy.wait_send())
        self.gone = True


class Mail:
    def __init__(self, send_sem, recv_sem):
        self.send_sem, self.recv_sem, self.posts = send_sem, recv_sem, []

    def make(self, source, target, device, send=None, recv=None, recv_sem=None):
        index = len(self.posts)
        copy = pltpu.make_async_remote_copy(
            src_ref=source, dst_ref=target,
            send_sem=self.send_sem.at[index],
            recv_sem=self.recv_sem.at[index] if recv_sem is None else recv_sem,
            device_id=device, device_id_type=MESH,
        )
        post = Post(copy, send, recv)
        self.posts.append(post)
        return post

    def reserve(self, count):
        start = len(self.posts)
        self.posts += [None] * count
        return start

    def put(self, *args, **kinds):
        post = self.make(*args, **kinds)
        post.start()
        return post

    def finish(self, count):
        assert len(self.posts) == count
        for post in self.posts:
            if post is not None:
                post.sent()


def greet(devices):
    barrier = pltpu.get_barrier_semaphore()
    for device in devices:
        pl.semaphore_signal(barrier, inc=1, device_id=device, device_id_type=MESH)
    pl.semaphore_wait(barrier, len(devices))


class Sizes:
    def __init__(self, packs, rows, tok, width, hidden, owned):
        self.packs, self.rows, self.tok, self.width, self.hidden, self.owned = packs, rows, tok, width, hidden, owned
        self.pack_len = rows * tok
        self.heads = HEADS // rows
        self.part = width // rows
        self.head = width // HEADS
        self.lines = width // 128
        self.square = self.lines * self.lines
        self.total = packs * owned
        self.blocks = owned // 128
        self.slots = -(-2 * self.blocks // rows)
        place = Place(packs, rows)
        self.nx, self.ny, self.nz = place.nx, place.ny, place.nz
        self.share = self.total // (packs * rows)
        self.chunks = 2 if self.share % 32 == 0 else 1
        self.size = self.share // self.chunks
        self.late = 3 * self.part * self.lines
        self.joint = max(n for n in range(1, packs + 1) if packs % n == 0 and self.late % (16 * n) == 0)
        self.owners = -(-3 * self.square // self.blocks)
        over_x, over_y, over_z, peers = self.nx - 1, self.ny - 1, self.nz - 1, rows - 1
        gather = peers + 2 * over_x + 1 + 4 * (1 + over_y) + 2 * over_y + (2 * over_z - 1) * (2 + 2 * over_y)
        reduce = self.chunks * (1 + over_x + over_y + over_z + peers)
        vector = 1 + over_x + over_y + over_z
        bases = 8 * (over_x + 1) + over_x
        self.posts = gather + 3 * peers + reduce + packs - 1 + vector + self.owners * rows + bases


def vmem_scratch(z):
    half, most = z.nx * z.ny * z.nz, max(z.nx, z.ny)
    ring = half // min(z.nx, z.ny)
    f = lambda *shape: pltpu.VMEM(shape, F32)
    b = lambda *shape: pltpu.VMEM(shape, BF16)
    return dict(
        tokens_all=f(z.rows, z.tok, z.width),
        codes_all=pltpu.VMEM((z.rows, 2 * z.tok // 128, 128), jnp.int32),
        weights=b(z.total, 128),
        placed=b(z.pack_len, z.width), plain=b(z.pack_len, z.width),
        kf=b(z.heads, z.pack_len, 128), qf=b(z.heads, 128, z.pack_len), vf=b(z.heads, z.pack_len, 128),
        kt=b(z.part, z.pack_len), vt=b(z.part, z.pack_len), q=b(z.pack_len, z.part), ot=f(z.part, z.pack_len),
        att_post=b(z.rows, z.part, z.tok), att=b(z.rows, z.part, z.tok),
        cot=f(z.tok, z.width), layer=f(z.tok, z.width), branch=f(z.tok, z.width),
        dot_post=b(z.rows, z.part, z.tok), dot=b(z.part, z.pack_len),
        grad=f(z.total, 128), vec_part=f(32, 128),
        stage0=b(z.chunks, half, z.size, 128), recv0=b(z.chunks, half, z.size, 128),
        stage1=b(z.chunks, half * (most - 1) // most, z.size, 128),
        recv1=b(z.chunks, half * (most - 1) // most, z.size, 128),
        kept1=f(z.chunks, ring, z.size, 128),
        stage2=b(z.chunks, (most - 1) * z.nz, z.size, 128), recv2=b(z.chunks, (most - 1) * z.nz, z.size, 128),
        kept2=f(z.chunks, z.nz, z.size, 128),
        stage3=b(z.chunks, z.nz, z.size, 128), recv3=b(z.chunks, z.nz, z.size, 128),
        vec_c=f(2, 32, 128), vec_x=f(z.nx, 32, 128), vec_y=f(z.ny, 32, 128), vec_z=f(z.nz, 32, 128),
        post=b(z.rows, 3 * z.part, z.tok), got=b(z.rows, 3 * z.part, z.tok),
        late=f(z.late, 128), late_post=b(z.late, 128), late_recv=b(z.packs, z.late // z.joint, 128),
        late_share=b(z.late // z.joint, 128), late_all=b(z.rows, z.late, 128),
        owned=b(z.owned, 128),
        first=f(z.owned, 128), second=f(z.owned, 128), left=f(z.owned, 128), right=f(z.owned, 128),
        lbasis=f(z.owned, 128), rbasis=f(z.owned, 128),
        gram=f(z.slots, 128, 256), turned=f(z.rows, z.slots, 128, 128), bases=f(2 * z.owned, 128),
        first_new=f(z.owned, 128), second_new=f(z.owned, 128), master_new=f(z.owned, 128), copy_new=b(z.owned, 128),
        left_new=f(z.owned, 128), right_new=f(z.owned, 128), input=f(z.tok, z.width), vec_new=f(3, 32, 128),
    )


LOADS = ("cot", "first", "second", "left", "right", "lbasis", "rbasis")


def layer_kernel(z, names, *refs):
    inputs = (
        "tokens", "codes", "master", "vec", "table", "vec_first", "vec_second",
        "cot_in", "first_in", "second_in", "left_in", "right_in", "lbasis_in", "rbasis_in",
    )
    outputs = (
        "layer_out", "input_out", "first_out", "second_out", "master_out", "copy_out", "left_out", "right_out",
        "lbasis_out", "rbasis_out", "vec_out", "vec_first_out", "vec_second_out",
    )
    s = types.SimpleNamespace(**dict(zip(inputs + outputs + tuple(names), refs)))
    send_sem, recv_sem, load_sem, late_sem = refs[-4:]
    loads = [
        pltpu.make_async_copy(getattr(s, name + "_in"), getattr(s, name), load_sem.at[i]) for i, name in enumerate(LOADS)
    ]
    for load in loads:
        load.start()
    stores = []

    def store(source, target):
        copy = pltpu.make_async_copy(source, target, load_sem.at[len(loads) + len(stores)])
        copy.start()
        stores.append(copy)

    place = Place(z.packs, z.rows).locate()
    mail = Mail(send_sem, recv_sem)
    at, me, pack = place.at, place.r, place.p
    nx, ny, nz, rows, tok, part, head, heads = z.nx, z.ny, z.nz, z.rows, z.tok, z.part, z.head, z.heads
    lines, square, width, hidden = z.lines, z.square, z.width, z.hidden
    partner = place.peers("c")[0]
    near = {dim: place.peers(dim) for dim in ("x", "y", "z")}
    row_peers = place.row_peers()

    def source(dim, step):
        return lax.rem(at[dim] + place.size[dim] - 1 - step, place.size[dim])

    half = z.owned // 2
    quarter = half // 2

    def piece(zz, yy, k=None):
        start = (zz * ny + yy) * z.owned + at["c"] * half
        count = half
        if k is not None:
            start, count = start + k * quarter, quarter
        return s.weights.at[pl.ds(pl.multiple_of(start, 16), count), :]

    def to(dim, index):
        return place.device(**{dim: index})

    up, down = lax.rem(at["z"] + 1, nz), lax.rem(at["z"] + nz - 1, nz)
    inner = at["z"] >= 1
    below_top = at["z"] + 1 < nz
    send_codes = [mail.make(s.codes, s.codes_all.at[me], device) for device in row_peers]
    send_x = [mail.make(s.tokens, s.tokens_all.at[me], device) for _, device in near["x"]]
    send_c = mail.make(s.tokens, s.tokens_all.at[me], partner[1])
    relay_x = []
    for step in range(nx - 1):
        row = source("x", step) * 2 + at["c"]
        relay_x.append(mail.make(s.tokens_all.at[row], s.tokens_all.at[row], partner[1]))
    chain, chain_y, chain_c, chain_yc = [], [], [], []
    for k in range(2):
        part_k = piece(0, at["y"], k)
        chain.append(mail.make(part_k, part_k, to("z", up), send=below_top, recv=inner))
        chain_y.append([mail.make(part_k, part_k, device) for _, device in near["y"]])
        chain_c.append(mail.make(part_k, part_k, partner[1], send=inner, recv=inner))
        chain_yc.append([])
        for step in range(ny - 1):
            part_k = piece(0, source("y", step), k)
            chain_yc[k].append(mail.make(part_k, part_k, partner[1]))

    def spread(zz, condition):
        mine = piece(zz, at["y"])
        over_y = [mail.make(mine, mine, device, condition, condition) for _, device in near["y"]]
        theirs = [piece(zz, source("y", step)) for step in range(ny - 1)]
        over_c = [mail.make(ref, ref, partner[1], condition, condition) for ref in theirs]
        return over_y, over_c

    own_y, own_c = spread(at["z"], inner)
    ups, downs = [], []
    for j in range(nz - 2):
        mine, coming = lax.rem(at["z"] + nz - j, nz), lax.rem(at["z"] + nz - 1 - j, nz)
        there = at["z"] - 1 - j >= 1
        hop = mail.make(piece(mine, at["y"]), piece(mine, at["y"]), to("z", up), (at["z"] - j >= 1) & below_top, there)
        core = mail.make(piece(coming, at["y"]), piece(coming, at["y"]), partner[1], there, there)
        ups.append((hop, core) + spread(coming, there))
    for j in range(nz - 1):
        mine, coming = lax.rem(at["z"] + j, nz), lax.rem(at["z"] + 1 + j, nz)
        there = at["z"] + 1 + j < nz
        hop = mail.make(piece(mine, at["y"]), piece(mine, at["y"]), to("z", down), inner & (at["z"] + j < nz), there)
        core = mail.make(piece(coming, at["y"]), piece(coming, at["y"]), partner[1], there, there)
        downs.append((hop, core) + spread(coming, there))

    own = pl.ds(pl.multiple_of(pack * z.owned, 16), z.owned)
    s.weights[own, :] = s.master[...].astype(BF16)
    greet(row_peers + [device for dim in ("y", "z") for _, device in near[dim]])
    for post in send_codes + send_x + [send_c]:
        post.start()

    def first_hop():
        for k in range(2):
            chain[k].start()
            for post in chain_y[k]:
                post.start()

    pl.when(at["z"] == 0)(first_hop)
    s.tokens_all[me] = s.tokens[...]
    s.codes_all[me] = s.codes[...]
    for post in send_codes:
        post.recv()

    groups = tok // 128
    high = z.pack_len // IMG_W
    ids, pad = s.codes_all[:, :groups, :], s.codes_all[:, groups:, :]
    index = (
        lax.broadcasted_iota(jnp.int32, ids.shape, 0) * tok
        + lax.broadcasted_iota(jnp.int32, ids.shape, 1) * 128
        + lax.broadcasted_iota(jnp.int32, ids.shape, 2)
    )
    starts = jnp.zeros(ids.shape, jnp.int32)
    for image in range(8):
        count = jnp.sum(jnp.where(ids == image, 1.0, 0.0)).astype(jnp.int32)
        starts = starts + jnp.where(ids > image, count, 0)
    places = index - starts
    on_y = lax.div(places, IMG_W)
    on_x = places - on_y * IMG_W

    def line(values, r):
        return jnp.concatenate([values[r, g : g + 1, :] for g in range(groups)], 1)

    def vector(first, count=lines):
        return jnp.concatenate([s.vec[first + i : first + i + 1, :] for i in range(count)], 1)

    def projections(pos_ref):
        for r in range(rows):
            sub = lax.broadcasted_iota(jnp.int32, (high, tok), 0)
            hot = jnp.concatenate(
                [
                    jnp.where(sub == line(on_y, r), 1.0, 0.0),
                    jnp.where(sub[:IMG_W] == line(on_x, r), 1.0, 0.0),
                ],
                0,
            ).astype(BF16)
            pos_ref[r] = dot(jnp.concatenate([hot] * 3, 0), s.table[...], TN)
        for k in range(2):

            def forward():
                chain[k].copy.wait_recv()
                chain[k].start()
                chain_c[k].copy.start()
                for post in chain_y[k]:
                    post.start()

            pl.when(inner)(forward)
        for post, relay in zip(send_x, relay_x):
            post.recv()
            relay.start()
        for k in range(2):
            for post, relay in zip(chain_y[k], chain_yc[k]):
                post.recv()
                relay.start()
        for post in [send_c] + relay_x + chain_c + chain_yc[0] + chain_yc[1]:
            post.recv()
        for post in own_y + [ups[0][0], downs[0][0]] if ups else own_y + [downs[0][0]]:
            post.start()
        pick = (
            lax.broadcasted_iota(jnp.int32, (width, part), 0)
            == lax.broadcasted_iota(jnp.int32, (width, part), 1) + me * part
        )
        pick = jnp.where(pick, 1.0, 0.0).astype(BF16)
        wq, wk, wv = [dot(blocks_of(s.weights, n * square, lines, lines, lines), pick).astype(BF16) for n in range(3)]

        def bias(first):
            row = jnp.broadcast_to(vector(first), (8, width))
            return pltpu.roll(row, lax.rem(width - me * part, width), 1)[:1, :part]

        bias_q, bias_v = bias(0), bias(lines)
        scale = LOG2E * head**-0.5
        sub8 = lax.broadcasted_iota(jnp.int32, (8, tok), 0)
        for r in range(rows):
            span = slice(r * tok, (r + 1) * tok)
            rows_in = s.tokens_all[r]
            placed = (rows_in + pos_ref[r]).astype(BF16)
            plain = rows_in.astype(BF16)
            s.placed[span, :] = placed
            s.plain[span, :] = plain
            q = (dot(placed, wq) + bias_q).astype(BF16)
            k = dot(placed, wk).astype(BF16)
            v = (dot(plain, wv) + bias_v).astype(BF16)
            s.q[span, :] = q
            qt, kt, vt = q.astype(F32).T, k.astype(F32).T, v.astype(F32).T
            s.kt[:, span] = kt.astype(BF16)
            s.vt[:, span] = vt.astype(BF16)
            scaled = qt * scale
            q_high = scaled.astype(BF16).astype(F32)
            q_low = scaled - q_high
            same = sub8 == line(ids, r)
            ones = jnp.ones((8, tok), F32)
            free = jnp.zeros((128 - 2 * head - 8, tok), F32)
            barred = jnp.where(same & (line(pad, r) == 0), 0.0, MASKED_SCORE)
            for h in range(heads):
                mine = slice(h * head, (h + 1) * head)
                s.qf[h, :, span] = jnp.concatenate(
                    [q_high[mine], q_low[mine], jnp.where(same, 1.0, 0.0), free], 0
                ).astype(BF16)
                s.kf[h, span, :] = jnp.concatenate([kt[mine], kt[mine], barred, ones, free[8:]], 0).T.astype(BF16)
                s.vf[h, span, :] = jnp.concatenate([vt[mine], vt[mine], ones, free], 0).T.astype(BF16)

    pl.run_scoped(projections, pltpu.VMEM((rows, tok, width), F32))

    att_posts = []
    for step in range(rows - 1):
        device = {"pack": pack, "row": lax.rem(me + 1 + step, rows)}
        att_posts.append(mail.make(s.att_post.at[step], s.att.at[me], device))

    def weight_stage(stage):
        if stage == 0:
            for post, core in zip(own_y, own_c):
                post.recv()
                core.start()
        for moves in (ups, downs):
            if 0 < stage <= len(moves):
                _, _, over_y, over_c = moves[stage - 1]
                for post, core in zip(over_y, over_c):
                    post.recv()
                    core.start()
            if stage < len(moves):
                hop, core, over_y, _ = moves[stage]
                hop.recv()
                if stage + 1 < len(moves):
                    moves[stage + 1][0].start()
                for post in [core] + over_y:
                    post.start()

    stages = nz
    per = tok // TILE
    tiles = rows * per

    def attend_step(number, carry):
        step = lax.div(number, per)
        offset = lax.rem(number, per)
        dest = lax.rem(me + 1 + step, rows)
        span = pl.ds(pl.multiple_of(dest * tok + offset * TILE, TILE), TILE)
        for stage in range(stages - 1):
            pl.when(number == (stage + 1) * tiles // stages)(functools.partial(weight_stage, stage))
        pieces = []
        for h in range(heads):
            scores = dot(s.kf[h], s.qf[h, :, span])
            largest = jnp.max(scores, axis=0, keepdims=True)
            weights = jnp.exp2(scores - largest)
            total = jnp.sum(weights, axis=0, keepdims=True)
            out = dot(s.vt[h * head : (h + 1) * head, :], weights.astype(BF16))
            pieces.append(out * (1.0 / total))
            lse = -(largest + jnp.log2(total))
            lh = lse.astype(BF16).astype(F32)
            lm = (lse - lh).astype(BF16).astype(F32)
            tail = s.qf[h, 2 * head : 2 * head + 16, span].astype(F32)
            tail = jnp.concatenate([tail[:8], lh, lm, lse - lh - lm, jnp.zeros((5, TILE), F32)], 0)
            s.qf[h, 2 * head : 2 * head + 16, span] = tail.astype(BF16)
        out = pieces[0] if heads == 1 else jnp.concatenate(pieces, 0)
        s.ot[:, span] = out
        s.att_post[step, :, pl.ds(pl.multiple_of(offset * TILE, TILE), TILE)] = out.astype(BF16)
        for there in range(rows - 1):
            pl.when(number == (there + 1) * per - 1)(functools.partial(att_posts[there].start))
        return carry

    lax.fori_loop(0, tiles, attend_step, 0)
    weight_stage(stages - 1)
    s.att[me] = s.att_post[rows - 1]
    for post in att_posts:
        post.recv()
    for post in own_c + [p for moves in (ups, downs) for move in moves for p in [move[1]] + move[3]]:
        post.recv()

    dot_lanes = pl.ds(pl.multiple_of(me * tok, 128), tok)
    dot_posts = [mail.make(s.dot_post.at[d["row"]], s.dot.at[:, dot_lanes], d) for d in row_peers]
    loads[0].wait()

    def middle(act_ref, slope_ref):
        count = 4
        wide = hidden // count // 128

        def put_vector(first, value):
            for i in range(value.shape[1] // 128):
                s.vec_part[first + i : first + i + 1, :] = value[:, i * 128 : (i + 1) * 128]

        bias_out, gain_one, shift_one = vector(2 * lines), vector(3 * lines), vector(4 * lines)
        last = 5 * lines + hidden // 128
        bias_two, gain_two, shift_two = vector(last), vector(last + lines), vector(last + 2 * lines)

        def w_one(n):
            return blocks_of(s.weights, 4 * square + n * wide, lines, wide, hidden // 128)

        def w_two(n):
            first = 4 * square + lines * hidden // 128
            return blocks_of(s.weights, first + n * wide * lines, wide, lines, lines)

        def put_grad(first, stride, value):
            for i in range(value.shape[0] // 128):
                for j in range(value.shape[1] // 128):
                    row = (3 * square + first + i * stride + j) * 128
                    s.grad[row : row + 128, :] = value[i * 128 : (i + 1) * 128, j * 128 : (j + 1) * 128]

        attended_t = jnp.concatenate([s.att[r] for r in range(rows)], 0)
        w_out = blocks_of(s.weights, 3 * square, lines, lines, lines)
        branch = dot(attended_t, w_out, TN) + bias_out
        unit_one, scale_one = norm_forward(s.tokens[...] + branch)
        normed = unit_one * gain_one + shift_one
        normed_low = normed.astype(BF16)
        second = jnp.zeros((tok, width), F32)
        for n in range(count):
            pre = dot(normed_low, w_one(n)) + vector(5 * lines + n * wide, wide)
            square_pre = pre * pre
            curve = jnp.tanh(0.7978845608028654 * pre * (1.0 + 0.044715 * square_pre))
            half_one = 0.5 * (1.0 + curve)
            act = (pre * half_one).astype(BF16)
            slope_ref[n] = half_one + 0.5 * pre * (1.0 - curve * curve) * (
                0.7978845608028654 * (1.0 + 0.134145 * square_pre)
            )
            act_ref[n] = act
            second = second + dot(act, w_two(n))
        unit_two, scale_two = norm_forward(normed + (second + bias_two))
        s.layer[...] = unit_two * gain_two + shift_two
        cot = s.cot[...]
        put_vector(last + lines, column_sum(cot * unit_two))
        put_vector(last + 2 * lines, column_sum(cot))
        sum_grad = norm_backward(cot, gain_two, unit_two, scale_two)
        second_grad = sum_grad.astype(BF16)
        put_vector(last, column_sum(second_grad.astype(F32)))
        normed_grad = sum_grad
        for n in range(count):
            two = w_two(n)
            hidden_grad = (dot(second_grad, two, NT) * slope_ref[n]).astype(BF16)
            put_vector(5 * lines + n * wide, column_sum(hidden_grad.astype(F32)))
            normed_grad = normed_grad + dot(hidden_grad, w_one(n), NT)
            first = lines * hidden // 128 + square + n * wide * lines
            put_grad(first, lines, dot(act_ref[n], second_grad, TN))
            put_grad(square + n * wide, hidden // 128, dot(normed_low, hidden_grad, TN))
        put_vector(3 * lines, column_sum(normed_grad * unit_one))
        put_vector(4 * lines, column_sum(normed_grad))
        branch_grad = norm_backward(normed_grad, gain_one, unit_one, scale_one)
        s.branch[...] = branch_grad
        branch_low = branch_grad.astype(BF16)
        grad_t = dot(w_out, branch_low, NT).astype(BF16)
        for r in range(rows):
            s.dot_post[r] = grad_t[r * part : (r + 1) * part, :]
        for post in dot_posts:
            post.start()
        s.dot[:, dot_lanes] = s.dot_post[me]
        put_vector(2 * lines, column_sum(branch_low.astype(F32)))
        put_grad(0, lines, dot(attended_t, branch_low))

    pl.run_scoped(middle, pltpu.VMEM((4, tok, hidden // 4), BF16), pltpu.VMEM((4, tok, hidden // 4), F32))

    store(s.layer, s.layer_out)

    chunks, size, share = z.chunks, z.size, z.share
    s.grad[: 3 * square * 128, :] = jnp.zeros((3 * square * 128, 128), F32)

    def grad_rows(chunk, x, c, y, z):
        row = (z * ny + y) * (rows * share) + (x * 2 + c) * share + chunk * size
        return s.grad[pl.ds(pl.multiple_of(row, 16), size), :]

    def order(chunk):
        return ("x", "y") if chunk % 2 == 0 else ("y", "x")

    def spot(chunk, one, two, zz):
        return {order(chunk)[0]: one, order(chunk)[1]: two, "z": zz}

    hops0, hops1, hops2, hops3, hops4 = [], [], [], [], []
    for chunk in range(chunks):
        n2 = place.size[order(chunk)[1]]
        hops0.append(mail.make(s.stage0.at[chunk], s.recv0.at[chunk], partner[1]))
        made = []
        for step, (_, device) in enumerate(near[order(chunk)[0]]):
            span = pl.ds(step * n2 * nz, n2 * nz)
            made.append(mail.make(s.stage1.at[chunk, span], s.recv1.at[chunk, span], device))
        hops1.append(made)
        made = []
        for step, (_, device) in enumerate(near[order(chunk)[1]]):
            span = pl.ds(step * nz, nz)
            made.append(mail.make(s.stage2.at[chunk, span], s.recv2.at[chunk, span], device))
        hops2.append(made)
        hops3.append(
            [mail.make(s.stage3.at[chunk, step], s.recv3.at[chunk, step], d) for step, (_, d) in enumerate(near["z"])]
        )
        mine = pl.ds(pl.multiple_of(me * share + chunk * size, 16), size)
        hops4.append([mail.make(s.owned.at[mine], s.owned.at[mine], device) for device in row_peers])

    def reduce_cores():
        for chunk in range(chunks):
            n1, n2 = [place.size[d] for d in order(chunk)]
            for one in range(n1):
                for two in range(n2):
                    for zz in range(nz):
                        rows_of = grad_rows(chunk, c=partner[0], **spot(chunk, one, two, zz))
                        s.stage0[chunk, (one * n2 + two) * nz + zz] = rows_of.astype(BF16)
            hops0[chunk].start()

    def reduce_first():
        for chunk in range(chunks):
            n1, n2 = [place.size[d] for d in order(chunk)]
            hops0[chunk].recv()

            def summed(one, two, zz):
                slot = (one * n2 + two) * nz + zz
                rows_of = grad_rows(chunk, c=at["c"], **spot(chunk, one, two, zz))
                return rows_of + s.recv0[chunk, slot].astype(F32)

            for step, (there, _) in enumerate(near[order(chunk)[0]]):
                for two in range(n2):
                    for zz in range(nz):
                        s.stage1[chunk, step * n2 * nz + two * nz + zz] = summed(there, two, zz).astype(BF16)
                hops1[chunk][step].start()
            for two in range(n2):
                for zz in range(nz):
                    s.kept1[chunk, two * nz + zz] = summed(at[order(chunk)[0]], two, zz)

    def reduce_second():
        for chunk in range(chunks):
            n1, n2 = [place.size[d] for d in order(chunk)]
            for hop in hops1[chunk]:
                hop.recv()

            def summed(two, zz):
                total = s.kept1[chunk, two * nz + zz]
                for step in range(n1 - 1):
                    total = total + s.recv1[chunk, step * n2 * nz + two * nz + zz].astype(F32)
                return total

            for step, (there, _) in enumerate(near[order(chunk)[1]]):
                for zz in range(nz):
                    s.stage2[chunk, step * nz + zz] = summed(there, zz).astype(BF16)
                hops2[chunk][step].start()
            for zz in range(nz):
                s.kept2[chunk, zz] = summed(at[order(chunk)[1]], zz)

    def reduce_third():
        for chunk in range(chunks):
            n2 = place.size[order(chunk)[1]]
            for hop in hops2[chunk]:
                hop.recv()

            def summed(zz):
                total = s.kept2[chunk, zz]
                for step in range(n2 - 1):
                    total = total + s.recv2[chunk, step * nz + zz].astype(F32)
                return total

            for step, (there, _) in enumerate(near["z"]):
                s.stage3[chunk, step] = summed(there).astype(BF16)
                hops3[chunk][step].start()
            s.kept2[chunk, at["z"]] = summed(at["z"])

    def reduce_last():
        for chunk in range(chunks):
            total = s.kept2[chunk, at["z"]]
            for step, hop in enumerate(hops3[chunk]):
                hop.recv()
                total = total + s.recv3[chunk, step].astype(F32)
            mine = pl.ds(pl.multiple_of(me * share + chunk * size, 16), size)
            s.owned[mine, :] = total.astype(BF16)
            for hop in hops4[chunk]:
                hop.start()

    reduce_stages = ((0, reduce_first), (3, reduce_second), (5, reduce_third))
    reduce_cores()
    for post in dot_posts:
        post.recv()

    scale = head**-0.5
    posts = [mail.make(s.post.at[d["row"]], s.got.at[me], d) for d in row_peers]

    def backward(df_ref, mix_ref, both_ref, pair_ref, qt_ref):
        lane = lax.broadcasted_iota(jnp.int32, (tok, part), 1)
        for r in range(rows):
            span = slice(r * tok, (r + 1) * tok)
            grad_t = s.dot[:, span].astype(F32)
            center = grad_t * s.ot[:, span]
            grad_rows_in = grad_t.T
            queries = s.q[span, :].astype(F32)
            scaled = grad_t * scale
            g_high = scaled.astype(BF16).astype(F32)
            g_low = scaled - g_high
            for h in range(heads):
                own_lines = slice(h * head, (h + 1) * head)
                shift = -scale * column_sum(center[own_lines])
                sh = shift.astype(BF16).astype(F32)
                sm = (shift - sh).astype(BF16).astype(F32)
                rest = jnp.zeros((128 - 2 * head - 3, tok), F32)
                df_ref[h, :, span] = jnp.concatenate(
                    [g_high[own_lines], g_low[own_lines], sh, sm, shift - sh - sm, rest], 0
                ).astype(BF16)
                mine = (lane >= h * head) & (lane < (h + 1) * head)
                none = jnp.zeros((tok, part), F32)
                free = [jnp.zeros((tok, 128 - 2 * part), F32)] if part < 64 else []
                mix_ref[2 * h, span, :] = jnp.concatenate(
                    [jnp.where(mine, grad_rows_in, 0.0), none] + free, 1
                ).astype(BF16)
                mix_ref[2 * h + 1, span, :] = jnp.concatenate(
                    [none, jnp.where(mine, queries, 0.0)] + free, 1
                ).astype(BF16)
        pair_ref[...] = jnp.zeros_like(pair_ref)
        turns = z.pack_len // TILE

        def tile_step(number, carry):
            span = pl.ds(pl.multiple_of(number * TILE, TILE), TILE)
            for eighth, action in reduce_stages:
                pl.when(number == eighth * turns // 8)(action)
            pieces, mix = [], []
            for h in range(heads):
                probs = jnp.exp2(dot(s.kf[h], s.qf[h, :, span]))
                along = dot(s.vf[h], df_ref[h, :, span])
                both_ref[:, 2 * h * TILE : (2 * h + 1) * TILE] = probs.astype(BF16)
                score_grad = (probs * along).astype(BF16)
                both_ref[:, (2 * h + 1) * TILE : (2 * h + 2) * TILE] = score_grad
                pieces.append(dot(s.kt[h * head : (h + 1) * head, :], score_grad))
                mix += [mix_ref[2 * h, span, :], mix_ref[2 * h + 1, span, :]]
            qt_ref[:, span] = pieces[0] if heads == 1 else jnp.concatenate(pieces, 0)
            pair_ref[...] += dot(both_ref[...], jnp.concatenate(mix, 0))
            return carry

        lax.fori_loop(0, turns, tile_step, 0)
        for r in range(rows):
            span = slice(r * tok, (r + 1) * tok)
            pair = pair_ref[span, :].T
            s.post[r] = jnp.concatenate([qt_ref[:, span], pair[part : 2 * part], pair[:part]], 0).astype(BF16)

    pl.run_scoped(
        backward,
        pltpu.VMEM((heads, 128, z.pack_len), BF16),
        pltpu.VMEM((2 * heads, z.pack_len, 128), BF16),
        pltpu.VMEM((z.pack_len, 2 * heads * TILE), BF16),
        pltpu.VMEM((z.pack_len, 128), F32),
        pltpu.VMEM((part, z.pack_len), F32),
    )

    joint, owners = z.joint, z.owners
    size_l = z.late // joint
    for kind, first, last in (("placed", 0, 2 * part), ("plain", 2 * part, 3 * part)):
        base = getattr(s, kind)
        total = jnp.zeros((last - first, width), F32)
        for r in range(rows):
            total = total + dot(s.post[r, first:last, :], base[r * tok : (r + 1) * tok, :])
        for i in range(lines):
            row = i * 3 * part + first
            s.late[row : row + last - first, :] = total[:, i * 128 : (i + 1) * 128]
    s.late_post[...] = s.late[...].astype(BF16)
    spread_posts = []
    joined = None if joint == z.packs else pack < joint
    for step in range(1, z.packs):
        there = lax.rem(pack + step, z.packs)
        lands = None if joint == z.packs else there < joint
        rows_of = pl.ds(pl.multiple_of(lax.rem(there, joint) * size_l, 16), size_l)
        spread_posts.append(
            mail.put(
                s.late_post.at[rows_of, :], s.late_recv.at[step - 1], {"pack": there, "row": me}, lands, joined
            )
        )

    ones = jnp.ones((16, tok), BF16)
    sums = jnp.zeros((16, 3 * part), F32)
    for r in range(rows):
        sums = sums + dot(ones, s.post[r], NT)
    for n in (0, 2):
        row = jnp.concatenate([sums[:8, n * part : (n + 1) * part], jnp.zeros((8, width - part), F32)], 1)
        row = pltpu.roll(row, me * part, 1)
        for i in range(lines):
            line_of = (n // 2) * lines + i
            s.vec_part[line_of : line_of + 1, :] = row[:1, i * 128 : (i + 1) * 128]

    def vec_step(dim, buffer, value):
        buffer[at[dim]] = value
        return [mail.put(buffer.at[at[dim]], buffer.at[at[dim]], device) for _, device in place.peers(dim)]

    def vec_sum(hops, buffer):
        for hop in hops:
            hop.recv()
        total = buffer[0]
        for number in range(1, buffer.shape[0]):
            total = total + buffer[number]
        return total

    vec_hops = vec_step("c", s.vec_c, s.vec_part[...])
    reduce_last()
    own_late = pl.ds(pl.multiple_of(lax.rem(pack, joint) * size_l, 16), size_l)
    for post in spread_posts:
        post.recv()
    total = s.late[own_late, :]
    for step in range(z.packs - 1):
        total = total + s.late_recv[step].astype(F32)
    s.late_share[...] = total.astype(BF16)
    s.late_all[me, own_late, :] = total.astype(BF16)
    for owner in range(owners):
        for step in range(rows):
            leaves = [] if joint == z.packs else [pack < joint]
            if step == 0:
                leaves.append(pack != owner)
            leaves = functools.reduce(jnp.logical_and, leaves) if leaves else None
            mail.put(
                s.late_share, s.late_all.at[me, own_late, :],
                {"pack": pack * 0 + owner, "row": lax.rem(me + step, rows)}, leaves, None,
                late_sem.at[lax.rem(pack, joint), step],
            )
    vec_hops = vec_step("x", s.vec_x, vec_sum(vec_hops, s.vec_c))
    for post in posts:
        post.start()
    s.got[me] = s.post[me]
    for load in loads[1:]:
        load.wait()
    for chunk in range(chunks):
        for hop in hops4[chunk]:
            hop.recv()
            hop.sent()

    def late_wait():
        for giver in range(joint):
            for step in range(rows):

                def wait():
                    pltpu.make_async_remote_copy(
                        src_ref=s.late_share, dst_ref=s.late_all.at[0, :size_l, :],
                        send_sem=send_sem.at[0], recv_sem=late_sem.at[giver, step],
                        device_id={"pack": pack, "row": lax.rem(me + 1, rows)}, device_id_type=MESH,
                    ).wait_recv()

                when((pack != giver) if step == 0 else None, wait)
        for b in range(3 * square):
            kind, i, j = b // square, b % square // lines, b % lines

            def place_block():
                start = (i * 3 + kind) * part
                found = [s.late_all[r, start : start + part, :] for r in range(j * 128 // part, (j + 1) * 128 // part)]
                block = jnp.concatenate(found, 0).astype(F32).T
                row = b % z.blocks * 128
                s.owned[row : row + 128, :] = block.astype(BF16)

            pl.when(pack == b // z.blocks)(place_block)

    pl.when(pack < owners)(late_wait)
    vec_hops = vec_step("y", s.vec_y, vec_sum(vec_hops, s.vec_x))
    blocks, slots = z.blocks, z.slots
    for n in range(slots):
        t = jnp.minimum(me * slots + n, 2 * blocks - 1)
        is_right = t >= blocks
        rows_of = pl.ds(pl.multiple_of(jnp.where(is_right, t - blocks, t) * 128, 128), 128)
        g = s.owned[rows_of, :].astype(F32)
        g = jnp.where(is_right, g.T, g).astype(BF16)
        stat = jnp.where(is_right, s.right[rows_of, :], s.left[rows_of, :])
        basis = jnp.where(is_right, s.rbasis[rows_of, :], s.lbasis[rows_of, :])
        new = BETA_TWO * stat + (1.0 - BETA_TWO) * dot(g, g, NT)
        a = dot6(new, basis)
        a_t = a.T
        s.gram[n, :, :128] = dot6(a_t, a)
        s.gram[n, :, 128:] = a_t
    def block_step(number, carry):
        rows_of = pl.ds(pl.multiple_of(number * 128, 128), 128)
        g = s.owned[rows_of, :]
        s.left_new[rows_of, :] = BETA_TWO * s.left[rows_of, :] + (1.0 - BETA_TWO) * dot(g, g, NT)
        s.right_new[rows_of, :] = BETA_TWO * s.right[rows_of, :] + (1.0 - BETA_TWO) * dot(g, g, TN)
        lb, rb = s.lbasis[rows_of, :], s.rbasis[rows_of, :]
        lh, ll = split2(lb)
        turned = dot(jnp.concatenate([lh, ll], 0), jnp.concatenate([g, g], 0), TN)
        rotated = dot3(turned, rb)
        first = BETA_ONE * s.first[rows_of, :] + (1.0 - BETA_ONE) * rotated
        second = BETA_TWO * s.second[rows_of, :] + (1.0 - BETA_TWO) * rotated * rotated
        s.first_new[rows_of, :] = first
        s.second_new[rows_of, :] = second
        ratio = first / (1.0 - BETA_ONE**STEP) / (jnp.sqrt(second / (1.0 - BETA_TWO**STEP)) + EPSILON)
        stepped = dot3(dot3(lb, ratio), rb, NT)
        weights = s.master[rows_of, :]
        weights = weights - LEARN_RATE * (stepped + WEIGHT_DECAY * weights)
        s.master_new[rows_of, :] = weights
        s.copy_new[rows_of, :] = weights.astype(BF16)
        return carry

    targets = [partner[1]] + [device for _, device in near["x"]]
    panel_first = mail.reserve(8 * len(targets))

    def panel_post(index, number):
        rows_of = pl.ds(pl.multiple_of(index * 16, 16), 16)
        place_in = s.turned.at[me, :, rows_of, :]
        sem = panel_first + number * 8 + index
        return pltpu.make_async_remote_copy(
            src_ref=place_in, dst_ref=place_in, send_sem=send_sem.at[sem], recv_sem=recv_sem.at[sem],
            device_id=targets[number], device_id_type=MESH,
        )

    def panel(index, carry):
        block_step(jnp.minimum(index, blocks - 1), 0)
        panel_step(pl.multiple_of(index * 16, 16), s.gram, s.turned.at[me], slots)
        for number in range(len(targets)):
            panel_post(index, number).start()
        return carry

    lax.fori_loop(0, 8, panel, 0)
    vec_hops = vec_step("z", s.vec_z, vec_sum(vec_hops, s.vec_y))
    lax.fori_loop(8, max(blocks, 8), block_step, 0)

    def turn(row):
        for n in range(slots):
            t = row * slots + n

            @pl.when(t < 2 * blocks)
            def _():
                s.bases[pl.ds(pl.multiple_of(t * 128, 128), 128), :] = s.turned[row, n].T

    relays = []
    for step in range(nx - 1):
        for index in range(8):
            panel_post(index, 1 + step).wait_recv()
        row = source("x", step) * 2 + at["c"]
        relays.append(mail.put(s.turned.at[row], s.turned.at[row], partner[1]))
    for row in [me] + [source("x", step) * 2 + at["c"] for step in range(nx - 1)]:
        turn(row)
    for post in posts:
        post.recv()
    total = s.branch[...]
    for n in range(3):
        grad_t = jnp.concatenate([s.got[r, n * part : (n + 1) * part, :] for r in range(rows)], 0)
        weight = blocks_of(s.weights, n * square, lines, lines, lines)
        total = total + dot(grad_t, weight, (((0,), (1,)), ((), ())))
    s.input[...] = total
    store(s.input, s.input_out)
    for name in ("first", "second", "master", "copy", "left", "right"):
        store(getattr(s, name + "_new"), getattr(s, name + "_out"))
    grad = vec_sum(vec_hops, s.vec_z)
    first = BETA_ONE * s.vec_first[...] + (1.0 - BETA_ONE) * grad
    second = BETA_TWO * s.vec_second[...] + (1.0 - BETA_TWO) * grad * grad
    ratio = first / (1.0 - BETA_ONE**STEP) / (jnp.sqrt(second / (1.0 - BETA_TWO**STEP)) + EPSILON)
    s.vec_new[0] = s.vec[...] - LEARN_RATE * ratio
    s.vec_new[1] = first
    s.vec_new[2] = second
    for number, name in enumerate(("vec", "vec_first", "vec_second")):
        store(s.vec_new.at[number], getattr(s, name + "_out"))
    for index in range(8):
        panel_post(index, 0).wait_recv()
    turn(lax.div(me, 2) * 2 + partner[0])
    for step, relay in enumerate(relays):
        relay.recv()
        turn(source("x", step) * 2 + partner[0])
    store(s.bases.at[: z.owned, :], s.lbasis_out)
    store(s.bases.at[z.owned : 2 * z.owned, :], s.rbasis_out)
    for copy in stores:
        copy.wait()
    for index in range(8):
        for number in range(len(targets)):
            panel_post(index, number).wait_send()
    mail.finish(z.posts)


def finish_kernel(count, *refs):
    sems = refs[-1]
    loads = [pltpu.make_async_copy(refs[i], refs[2 * count + i], sems.at[i]) for i in range(count)]
    stores = [pltpu.make_async_copy(refs[2 * count + i], refs[count + i], sems.at[count + i]) for i in range(count)]
    for load in loads:
        load.start()
    for load, copy in zip(loads, stores):
        load.wait()
        copy.start()
    for copy in stores:
        copy.wait()


def shards(
    tokens, cotangent, segment_ids, padding, master, moment_first, moment_second,
    stat_left, stat_right, basis_left, basis_right, vec_params, vec_first, vec_second,
):
    packs, rows = lax.axis_size("pack"), lax.axis_size("row")
    tok, width = tokens.shape
    z = Sizes(packs, rows, tok, width, vec_params.shape[0] - 8 * width, master.shape[0])
    codes = jnp.concatenate([segment_ids.reshape(-1, 128), padding.reshape(-1, 128)], 0)
    table = jnp.asarray(sine_rows(z.pack_len, width // 2))
    full = jax.ShapeDtypeStruct(master.shape, F32)
    layer = jax.ShapeDtypeStruct(tokens.shape, F32)
    shapes = (layer, layer, full, full, full, jax.ShapeDtypeStruct(master.shape, BF16), full, full, full, full)
    shapes = shapes + (jax.ShapeDtypeStruct((32, 128), F32),) * 3
    scratch = vmem_scratch(z)
    vm, hbm = pl.BlockSpec(memory_space=pltpu.VMEM), pl.BlockSpec(memory_space=pl.ANY)
    outs = pl.pallas_call(
        functools.partial(layer_kernel, z, tuple(scratch)),
        out_shape=shapes,
        in_specs=[vm] * 7 + [hbm] * 7,
        out_specs=(hbm,) * len(shapes),
        scratch_shapes=list(scratch.values())
        + [
            pltpu.SemaphoreType.DMA((z.posts,)),
            pltpu.SemaphoreType.DMA((z.posts,)),
            pltpu.SemaphoreType.DMA((len(LOADS) + len(shapes),)),
            pltpu.SemaphoreType.DMA((packs, rows)),
        ],
        compiler_params=pltpu.CompilerParams(collective_id=1, has_side_effects=True, vmem_limit_bytes=63 << 20),
        name="layer",
    )(
        tokens, codes, master, vec_params.reshape(32, 128), table,
        vec_first.reshape(32, 128), vec_second.reshape(32, 128),
        cotangent, moment_first, moment_second, stat_left, stat_right, basis_left, basis_right,
    )
    outs = pl.pallas_call(
        functools.partial(finish_kernel, len(shapes)),
        out_shape=shapes,
        in_specs=[hbm] * len(shapes),
        out_specs=(hbm,) * len(shapes),
        scratch_shapes=[pltpu.VMEM(shape.shape, shape.dtype) for shape in shapes]
        + [pltpu.SemaphoreType.DMA((2 * len(shapes),))],
        compiler_params=pltpu.CompilerParams(vmem_limit_bytes=63 << 20),
        name="finish",
    )(*outs)
    return outs[:-3] + tuple(out.reshape(-1) for out in outs[-3:])


def solution(mesh):
    placed = (
        P(("pack", "row"), None),
        P(("pack", "row"), None),
        P(("pack", "row")),
        P(("pack", "row")),
        P("pack", None),
        P("pack", None),
        P("pack", None),
        P("pack", None),
        P("pack", None),
        P("pack", None),
        P("pack", None),
        P(),
        P(),
        P(),
    )
    return jax.shard_map(
        shards,
        mesh=mesh,
        in_specs=placed,
        out_specs=(
            P(("pack", "row"), None),
            P(("pack", "row"), None),
            P("pack", None),
            P("pack", None),
            P("pack", None),
            P("pack", None),
            P("pack", None),
            P("pack", None),
            P("pack", None),
            P("pack", None),
            P(),
            P(),
            P(),
        ),
        check_vma=False,
    )
```

```python
import functools
import types
import jax
import ml_dtypes
import numpy as np
import jax.numpy as jnp
from jax import lax
from jax.experimental import pallas as pl
from jax.experimental.pallas import tpu as pltpu
from jax.sharding import PartitionSpec as P

HEADS = 8
IMG_W = 32
MASKED_SCORE = -1e30
NORM_EPSILON = 1e-05
STEP = 10
BETA_ONE = 0.9
BETA_TWO = 0.95
LEARN_RATE = 0.25
WEIGHT_DECAY = 0.01
EPSILON = 1e-08
F32 = jnp.float32
BF16 = jnp.bfloat16
NN = (((1,), (0,)), ((), ()))
NT = (((1,), (1,)), ((), ()))
TN = (((0,), (0,)), ((), ()))
MESH = pl.DeviceIdType.MESH


class Place:
    def __init__(self, packs, rows):
        self.packs, self.rows = packs, rows
        self.nx = rows // 2
        self.ny = self.nx if packs % self.nx == 0 else 1
        self.nz = packs // self.ny
        self.size = {"c": 2, "x": self.nx, "y": self.ny, "z": self.nz}

    def locate(self):
        self.p = lax.axis_index("pack")
        self.r = lax.axis_index("row")
        self.at = {
            "c": lax.rem(self.r, 2),
            "x": lax.div(self.r, 2),
            "y": lax.rem(self.p, self.ny),
            "z": lax.div(self.p, self.ny),
        }
        return self

    def device(self, **moved):
        at = {**self.at, **moved}
        return {"pack": at["z"] * self.ny + at["y"], "row": at["x"] * 2 + at["c"]}

    def other(self, dim, step):
        return lax.rem(self.at[dim] + step, self.size[dim])

    def peers(self, dim):
        found = []
        for step in range(1, self.size[dim]):
            there = self.other(dim, step)
            found.append((there, self.device(**{dim: there})))
        return found

    def row_peers(self):
        return [
            {"pack": self.p, "row": lax.rem(self.r + step, self.rows)} for step in range(1, self.rows)
        ]


def dot(left, right, dims=NN):
    return lax.dot_general(left, right, dims, preferred_element_type=F32)


def split2(v):
    high = v.astype(BF16)
    return high, (v - high.astype(F32)).astype(BF16)


def split3(v):
    high = v.astype(BF16)
    rest = v - high.astype(F32)
    mid = rest.astype(BF16)
    return high, mid, (rest - mid.astype(F32)).astype(BF16)


def dot3(left, right, dims=NN):
    la, ra = dims[0][0][0], dims[0][1][0]
    lh, ll = split2(left)
    rh, rl = split2(right)
    return dot(jnp.concatenate([lh, ll, lh], la), jnp.concatenate([rh, rh, rl], ra), dims)


def dot6(left, right, dims=NN):
    la, ra = dims[0][0][0], dims[0][1][0]
    lh, lm, ll = split3(left)
    rh, rm, rl = split3(right)
    return dot(
        jnp.concatenate([lh, lh, lm, lm, lh, ll], la),
        jnp.concatenate([rh, rm, rh, rm, rl, rh], ra),
        dims,
    )


def four_pivots(g, a, first, sub):
    cols = [jnp.broadcast_to(g[:, first + k : first + k + 1], (16, 128)) for k in range(4)]
    lower, inverse, factors, rows_g, rows_a = {}, [], [], [], []
    for k in range(4):
        pivot = cols[k][first + k : first + k + 1, :]
        column, row_g, row_a = cols[k], g[first + k : first + k + 1, :], a[first + k : first + k + 1, :]
        for m in range(k):
            pivot = pivot - lower[k, m] * lower[k, m]
            column = column - factors[m] * lower[k, m]
            row_g = row_g - rows_g[m] * lower[k, m]
            row_a = row_a - rows_a[m] * lower[k, m]
        inverse = lax.rsqrt(pivot)
        for n in range(k + 1, 4):
            entry = cols[k][first + n : first + n + 1, :]
            for m in range(k):
                entry = entry - lower[n, m] * lower[k, m]
            lower[n, k] = entry * inverse
        factors.append(column * inverse)
        rows_g.append(row_g * inverse)
        rows_a.append(row_a * inverse)
    below = sub > first + 3
    for k in range(4):
        factor = jnp.where(below, factors[k], 0.0)
        g = g - factor * rows_g[k]
        a = a - factor * rows_a[k]
    for k in range(4):
        g = jnp.where(sub == first + k, rows_g[k], g)
        a = jnp.where(sub == first + k, rows_a[k], a)
    return g, a


def panel_step(base, m_ref, out_ref, count):
    sub = lax.broadcasted_iota(jnp.int32, (16, 128), 0)
    back = lax.rem(128 - base, 128)
    gram = [pltpu.roll(m_ref[n, pl.ds(base, 16), :128], back, 1) for n in range(count)]
    rest = [m_ref[n, pl.ds(base, 16), 128:] for n in range(count)]
    for first in range(0, 16, 4):
        for n in range(count):
            gram[n], rest[n] = four_pivots(gram[n], rest[n], first, sub)
    for n in range(count):
        out_ref[n, pl.ds(base, 16), :] = rest[n]
    for n in range(count):
        uh, um, ul = split3(pltpu.roll(gram[n], base, 1))
        ah, am, al = split3(rest[n])
        wh, wm, wl = [jnp.concatenate(p, 1) for p in ((uh, ah), (um, am), (ul, al))]
        m_ref[n] -= dot(
            jnp.concatenate([uh, uh, um, um, uh, ul], 0),
            jnp.concatenate([wh, wm, wh, wm, wl, wh], 0),
            TN,
        )


def flat_rows(ref, count):
    return jnp.concatenate([ref[i : i + 1, :] for i in range(count)], 1)


def blocks_of(ref, first, down, across, stride):
    lines = []
    for i in range(down):
        row = [ref[pl.ds((first + i * stride + j) * 128, 128), :] for j in range(across)]
        lines.append(row[0] if across == 1 else jnp.concatenate(row, 1))
    return lines[0] if down == 1 else jnp.concatenate(lines, 0)


TILE = 256
LOG2E = 1.4426950408889634


def sine_rows(pack_len, half):
    column = np.arange(half)
    period = np.float32(10000.0) ** ((2 * (column // 2)).astype(np.float32) / np.float32(half))
    high = pack_len // IMG_W
    angles = np.arange(max(high, IMG_W)).astype(np.float32)[:, None] / period[None, :].astype(np.float32)
    angles = angles.astype(np.float64)
    table = np.where(column[None, :] % 2 == 0, np.sin(angles), np.cos(angles)).astype(np.float32)
    both = np.zeros((high + IMG_W, 2 * half), np.float32)
    both[:high, :half] = table[:high]
    both[high:, half:] = table[:IMG_W]
    pieces, rest = [], both
    for _ in range(3):
        piece = rest.astype(ml_dtypes.bfloat16)
        pieces.append(piece)
        rest = rest - piece.astype(np.float32)
    return np.concatenate(pieces, 0)


def norm_forward(hidden):
    center = hidden - jnp.mean(hidden, axis=-1, keepdims=True)
    scale = lax.rsqrt(jnp.mean(center * center, axis=-1, keepdims=True) + NORM_EPSILON)
    return center * scale, scale


def norm_backward(grad, gain, unit, scale):
    inner = grad * gain
    mean = jnp.mean(inner, axis=-1, keepdims=True)
    along = jnp.mean(inner * unit, axis=-1, keepdims=True)
    return scale * (inner - mean - unit * along)


def column_sum(values):
    return jnp.sum(values, axis=0, keepdims=True)


def when(condition, action):
    if condition is None:
        action()
    else:
        pl.when(condition)(action)


def either(conditions):
    return functools.reduce(jnp.logical_or, conditions)


class Post:
    def __init__(self, copy, send=None, recv=None):
        self.copy, self.send_if, self.recv_if, self.gone = copy, send, recv, False

    def start(self):
        when(self.send_if, lambda: self.copy.start())

    def recv(self):
        when(self.recv_if, lambda: self.copy.wait_recv())

    def sent(self):
        if not self.gone:
            when(self.send_if, lambda: self.copy.wait_send())
        self.gone = True


class Mail:
    def __init__(self, send_sem, recv_sem):
        self.send_sem, self.recv_sem, self.posts = send_sem, recv_sem, []

    def make(self, source, target, device, send=None, recv=None, recv_sem=None):
        index = len(self.posts)
        copy = pltpu.make_async_remote_copy(
            src_ref=source, dst_ref=target,
            send_sem=self.send_sem.at[index],
            recv_sem=self.recv_sem.at[index] if recv_sem is None else recv_sem,
            device_id=device, device_id_type=MESH,
        )
        post = Post(copy, send, recv)
        self.posts.append(post)
        return post

    def reserve(self, count):
        start = len(self.posts)
        self.posts += [None] * count
        return start

    def put(self, *args, **kinds):
        post = self.make(*args, **kinds)
        post.start()
        return post

    def finish(self, count):
        assert len(self.posts) == count
        for post in self.posts:
            if post is not None:
                post.sent()


def greet(devices):
    barrier = pltpu.get_barrier_semaphore()
    for device in devices:
        pl.semaphore_signal(barrier, inc=1, device_id=device, device_id_type=MESH)
    pl.semaphore_wait(barrier, len(devices))


class Sizes:
    def __init__(self, packs, rows, tok, width, hidden, owned):
        self.packs, self.rows, self.tok, self.width, self.hidden, self.owned = packs, rows, tok, width, hidden, owned
        self.pack_len = rows * tok
        self.heads = HEADS // rows
        self.part = width // rows
        self.head = width // HEADS
        self.lines = width // 128
        self.square = self.lines * self.lines
        self.total = packs * owned
        self.blocks = owned // 128
        self.slots = -(-2 * self.blocks // rows)
        place = Place(packs, rows)
        self.nx, self.ny, self.nz = place.nx, place.ny, place.nz
        self.share = self.total // (packs * rows)
        self.chunks = 2 if self.share % 32 == 0 else 1
        self.size = self.share // self.chunks
        self.late = 3 * self.part * self.lines
        self.joint = max(n for n in range(1, packs + 1) if packs % n == 0 and self.late % (16 * n) == 0)
        self.owners = -(-3 * self.square // self.blocks)
        self.givers = [set() for _ in range(self.owners)]
        for b in range(3 * self.square):
            kind, i = b // self.square, b % self.square // self.lines
            start = (i * 3 + kind) * self.part
            size = self.late // self.joint
            self.givers[b // self.blocks] |= set(range(start // size, (start + self.part - 1) // size + 1))
        over_x, over_y, over_z, peers = self.nx - 1, self.ny - 1, self.nz - 1, rows - 1
        gather = peers + 2 * over_x + 1 + 4 * (1 + over_y) + 2 * over_y + (2 * over_z - 1) * (2 + 2 * over_y)
        reduce = self.chunks * (1 + over_x + over_y + over_z + peers)
        vector = 1 + over_x + over_y + over_z
        bases = 8 * (over_x + 1) + over_x
        self.posts = gather + 3 * peers + reduce + packs - 1 + vector + self.owners * rows + bases


def vmem_scratch(z):
    half, most = z.nx * z.ny * z.nz, max(z.nx, z.ny)
    ring = half // min(z.nx, z.ny)
    f = lambda *shape: pltpu.VMEM(shape, F32)
    b = lambda *shape: pltpu.VMEM(shape, BF16)
    return dict(
        tokens_all=f(z.rows, z.tok, z.width),
        codes_all=pltpu.VMEM((z.rows, 2 * z.tok // 128, 128), jnp.int32),
        weights=b(z.total, 128),
        placed=b(z.pack_len, z.width), plain=b(z.pack_len, z.width),
        kf=b(z.heads, z.pack_len, 128), qf=b(z.heads, 128, z.pack_len), vf=b(z.heads, z.pack_len, 128),
        kt=b(z.part, z.pack_len), vt=b(z.part, z.pack_len), q=b(z.pack_len, z.part), ot=f(z.part, z.pack_len),
        att_post=b(z.rows, z.part, z.tok), att=b(z.rows, z.part, z.tok),
        tokens=f(z.tok, z.width), codes=pltpu.VMEM((2 * z.tok // 128, 128), jnp.int32),
        master=f(z.owned, 128), table=b(3 * (z.pack_len // IMG_W + IMG_W), z.width),
        cot=f(z.tok, z.width), layer=f(z.tok, z.width), branch=f(z.tok, z.width),
        dot_post=b(z.rows, z.part, z.tok), dot=b(z.part, z.pack_len),
        grad=f(z.total, 128), vec_part=f(32, 128),
        stage0=b(z.chunks, half, z.size, 128), recv0=b(z.chunks, half, z.size, 128),
        stage1=b(z.chunks, half * (most - 1) // most, z.size, 128),
        recv1=b(z.chunks, half * (most - 1) // most, z.size, 128),
        kept1=f(z.chunks, ring, z.size, 128),
        stage2=b(z.chunks, (most - 1) * z.nz, z.size, 128), recv2=b(z.chunks, (most - 1) * z.nz, z.size, 128),
        kept2=f(z.chunks, z.nz, z.size, 128),
        stage3=b(z.chunks, z.nz, z.size, 128), recv3=b(z.chunks, z.nz, z.size, 128),
        vec_c=f(2, 32, 128), vec_x=f(z.nx, 32, 128), vec_y=f(z.ny, 32, 128), vec_z=f(z.nz, 32, 128),
        post=b(z.rows, 3 * z.part, z.tok), got=b(z.rows, 3 * z.part, z.tok),
        late=f(z.late, 128), late_post=b(z.late, 128), late_recv=b(z.packs, z.late // z.joint, 128),
        late_share=b(z.late // z.joint, 128), late_all=b(z.rows, z.late, 128),
        owned=b(z.owned, 128),
        first=f(z.owned, 128), second=f(z.owned, 128), left=f(z.owned, 128), right=f(z.owned, 128),
        lbasis=f(z.owned, 128), rbasis=f(z.owned, 128),
        gram=f(z.slots, 128, 256), turned=f(z.rows, z.slots, 128, 128), bases=f(2 * z.owned, 128),
        first_new=f(z.owned, 128), second_new=f(z.owned, 128), master_new=f(z.owned, 128), copy_new=b(z.owned, 128),
        left_new=f(z.owned, 128), right_new=f(z.owned, 128), input=f(z.tok, z.width), vec_new=f(3, 32, 128),
    )


LOADS = ("tokens", "master", "table", "cot", "first", "second", "left", "right", "lbasis", "rbasis")


def layer_kernel(z, names, *refs):
    inputs = (
        "ids", "pad", "vec", "vec_first", "vec_second", "tokens_in", "master_in", "table_in",
        "cot_in", "first_in", "second_in", "left_in", "right_in", "lbasis_in", "rbasis_in",
    )
    outputs = (
        "layer_out", "input_out", "first_out", "second_out", "master_out", "copy_out", "left_out", "right_out",
        "lbasis_out", "rbasis_out", "vec_out", "vec_first_out", "vec_second_out",
    )
    s = types.SimpleNamespace(**dict(zip(inputs + outputs + tuple(names), refs)))
    send_sem, recv_sem, load_sem, late_sem = refs[-4:]
    loads = [
        pltpu.make_async_copy(getattr(s, name + "_in"), getattr(s, name), load_sem.at[i]) for i, name in enumerate(LOADS)
    ]
    for load in loads:
        load.start()
    stores = []

    def store(source, target):
        copy = pltpu.make_async_copy(source, target, load_sem.at[len(loads) + len(stores)])
        copy.start()
        stores.append(copy)

    place = Place(z.packs, z.rows).locate()
    mail = Mail(send_sem, recv_sem)
    at, me, pack = place.at, place.r, place.p
    nx, ny, nz, rows, tok, part, head, heads = z.nx, z.ny, z.nz, z.rows, z.tok, z.part, z.head, z.heads
    lines, square, width, hidden = z.lines, z.square, z.width, z.hidden
    partner = place.peers("c")[0]
    near = {dim: place.peers(dim) for dim in ("x", "y", "z")}
    row_peers = place.row_peers()

    def source(dim, step):
        return lax.rem(at[dim] + place.size[dim] - 1 - step, place.size[dim])

    half = z.owned // 2
    quarter = half // 2

    def piece(zz, yy, k=None):
        start = (zz * ny + yy) * z.owned + at["c"] * half
        count = half
        if k is not None:
            start, count = start + k * quarter, quarter
        return s.weights.at[pl.ds(pl.multiple_of(start, 16), count), :]

    def to(dim, index):
        return place.device(**{dim: index})

    up, down = lax.rem(at["z"] + 1, nz), lax.rem(at["z"] + nz - 1, nz)
    inner = at["z"] >= 1
    below_top = at["z"] + 1 < nz
    send_codes = [mail.make(s.codes, s.codes_all.at[me], device) for device in row_peers]
    send_x = [mail.make(s.tokens, s.tokens_all.at[me], device) for _, device in near["x"]]
    send_c = mail.make(s.tokens, s.tokens_all.at[me], partner[1])
    relay_x = []
    for step in range(nx - 1):
        row = source("x", step) * 2 + at["c"]
        relay_x.append(mail.make(s.tokens_all.at[row], s.tokens_all.at[row], partner[1]))
    chain, chain_y, chain_c, chain_yc = [], [], [], []
    for k in range(2):
        part_k = piece(0, at["y"], k)
        chain.append(mail.make(part_k, part_k, to("z", up), send=below_top, recv=inner))
        chain_y.append([mail.make(part_k, part_k, device) for _, device in near["y"]])
        chain_c.append(mail.make(part_k, part_k, partner[1], send=inner, recv=inner))
        chain_yc.append([])
        for step in range(ny - 1):
            part_k = piece(0, source("y", step), k)
            chain_yc[k].append(mail.make(part_k, part_k, partner[1]))

    def spread(zz, condition):
        mine = piece(zz, at["y"])
        over_y = [mail.make(mine, mine, device, condition, condition) for _, device in near["y"]]
        theirs = [piece(zz, source("y", step)) for step in range(ny - 1)]
        over_c = [mail.make(ref, ref, partner[1], condition, condition) for ref in theirs]
        return over_y, over_c

    own_y, own_c = spread(at["z"], inner)
    ups, downs = [], []
    for j in range(nz - 2):
        mine, coming = lax.rem(at["z"] + nz - j, nz), lax.rem(at["z"] + nz - 1 - j, nz)
        there = at["z"] - 1 - j >= 1
        hop = mail.make(piece(mine, at["y"]), piece(mine, at["y"]), to("z", up), (at["z"] - j >= 1) & below_top, there)
        core = mail.make(piece(coming, at["y"]), piece(coming, at["y"]), partner[1], there, there)
        ups.append((hop, core) + spread(coming, there))
    for j in range(nz - 1):
        mine, coming = lax.rem(at["z"] + j, nz), lax.rem(at["z"] + 1 + j, nz)
        there = at["z"] + 1 + j < nz
        hop = mail.make(piece(mine, at["y"]), piece(mine, at["y"]), to("z", down), inner & (at["z"] + j < nz), there)
        core = mail.make(piece(coming, at["y"]), piece(coming, at["y"]), partner[1], there, there)
        downs.append((hop, core) + spread(coming, there))

    own = pl.ds(pl.multiple_of(pack * z.owned, 16), z.owned)
    loads[1].wait()
    s.weights[own, :] = s.master[...].astype(BF16)
    s.codes[: tok // 128, :] = s.ids[...]
    s.codes[tok // 128 :, :] = s.pad[...]
    greet(row_peers + [device for dim in ("y", "z") for _, device in near[dim]])
    loads[0].wait()
    for post in send_codes + send_x + [send_c]:
        post.start()

    def first_hop():
        for k in range(2):
            chain[k].start()
            for post in chain_y[k]:
                post.start()

    pl.when(at["z"] == 0)(first_hop)
    s.tokens_all[me] = s.tokens[...]
    s.codes_all[me] = s.codes[...]
    for post in send_codes:
        post.recv()

    groups = tok // 128
    high = z.pack_len // IMG_W
    ids, pad = s.codes_all[:, :groups, :], s.codes_all[:, groups:, :]
    index = (
        lax.broadcasted_iota(jnp.int32, ids.shape, 0) * tok
        + lax.broadcasted_iota(jnp.int32, ids.shape, 1) * 128
        + lax.broadcasted_iota(jnp.int32, ids.shape, 2)
    )
    starts = jnp.zeros(ids.shape, jnp.int32)
    for image in range(8):
        count = jnp.sum(jnp.where(ids == image, 1.0, 0.0)).astype(jnp.int32)
        starts = starts + jnp.where(ids > image, count, 0)
    places = index - starts
    on_y = lax.div(places, IMG_W)
    on_x = places - on_y * IMG_W

    def line(values, r):
        return jnp.concatenate([values[r, g : g + 1, :] for g in range(groups)], 1)

    def vector(first, count=lines):
        return jnp.concatenate([s.vec[first + i : first + i + 1, :] for i in range(count)], 1)

    loads[2].wait()

    def projections(pos_ref):
        for r in range(rows):
            sub = lax.broadcasted_iota(jnp.int32, (high, tok), 0)
            hot = jnp.concatenate(
                [
                    jnp.where(sub == line(on_y, r), 1.0, 0.0),
                    jnp.where(sub[:IMG_W] == line(on_x, r), 1.0, 0.0),
                ],
                0,
            ).astype(BF16)
            pos_ref[r] = dot(jnp.concatenate([hot] * 3, 0), s.table[...], TN)
        for k in range(2):

            def forward():
                chain[k].copy.wait_recv()
                chain[k].start()
                chain_c[k].copy.start()
                for post in chain_y[k]:
                    post.start()

            pl.when(inner)(forward)
        for post, relay in zip(send_x, relay_x):
            post.recv()
            relay.start()
        for k in range(2):
            for post, relay in zip(chain_y[k], chain_yc[k]):
                post.recv()
                relay.start()
        for post in [send_c] + relay_x + chain_c + chain_yc[0] + chain_yc[1]:
            post.recv()
        for post in own_y + [ups[0][0], downs[0][0]] if ups else own_y + [downs[0][0]]:
            post.start()
        pick = (
            lax.broadcasted_iota(jnp.int32, (width, part), 0)
            == lax.broadcasted_iota(jnp.int32, (width, part), 1) + me * part
        )
        pick = jnp.where(pick, 1.0, 0.0).astype(BF16)
        wq, wk, wv = [dot(blocks_of(s.weights, n * square, lines, lines, lines), pick).astype(BF16) for n in range(3)]

        def bias(first):
            row = jnp.broadcast_to(vector(first), (8, width))
            return pltpu.roll(row, lax.rem(width - me * part, width), 1)[:1, :part]

        bias_q, bias_v = bias(0), bias(lines)
        scale = LOG2E * head**-0.5
        sub8 = lax.broadcasted_iota(jnp.int32, (8, tok), 0)
        for r in range(rows):
            span = slice(r * tok, (r + 1) * tok)
            rows_in = s.tokens_all[r]
            placed = (rows_in + pos_ref[r]).astype(BF16)
            plain = rows_in.astype(BF16)
            s.placed[span, :] = placed
            s.plain[span, :] = plain
            q = (dot(placed, wq) + bias_q).astype(BF16)
            k = dot(placed, wk).astype(BF16)
            v = (dot(plain, wv) + bias_v).astype(BF16)
            s.q[span, :] = q
            qt, kt, vt = q.astype(F32).T, k.astype(F32).T, v.astype(F32).T
            s.kt[:, span] = kt.astype(BF16)
            s.vt[:, span] = vt.astype(BF16)
            scaled = qt * scale
            q_high = scaled.astype(BF16).astype(F32)
            q_low = scaled - q_high
            same = sub8 == line(ids, r)
            ones = jnp.ones((8, tok), F32)
            free = jnp.zeros((128 - 2 * head - 8, tok), F32)
            barred = jnp.where(same & (line(pad, r) == 0), 0.0, MASKED_SCORE)
            for h in range(heads):
                mine = slice(h * head, (h + 1) * head)
                s.qf[h, :, span] = jnp.concatenate(
                    [q_high[mine], q_low[mine], jnp.where(same, 1.0, 0.0), free], 0
                ).astype(BF16)
                s.kf[h, span, :] = jnp.concatenate([kt[mine], kt[mine], barred, ones, free[8:]], 0).T.astype(BF16)
                s.vf[h, span, :] = jnp.concatenate([vt[mine], vt[mine], ones, free], 0).T.astype(BF16)

    pl.run_scoped(projections, pltpu.VMEM((rows, tok, width), F32))

    att_posts = []
    for step in range(rows - 1):
        device = {"pack": pack, "row": lax.rem(me + 1 + step, rows)}
        att_posts.append(mail.make(s.att_post.at[step], s.att.at[me], device))

    def weight_stage(stage):
        if stage == 0:
            for post, core in zip(own_y, own_c):
                post.recv()
                core.start()
        for moves in (ups, downs):
            if 0 < stage <= len(moves):
                _, _, over_y, over_c = moves[stage - 1]
                for post, core in zip(over_y, over_c):
                    post.recv()
                    core.start()
            if stage < len(moves):
                hop, core, over_y, _ = moves[stage]
                hop.recv()
                if stage + 1 < len(moves):
                    moves[stage + 1][0].start()
                for post in [core] + over_y:
                    post.start()

    stages = nz
    per = tok // TILE
    tiles = rows * per

    def attend_step(number, carry):
        step = lax.div(number, per)
        offset = lax.rem(number, per)
        dest = lax.rem(me + 1 + step, rows)
        span = pl.ds(pl.multiple_of(dest * tok + offset * TILE, TILE), TILE)
        for stage in range(stages - 1):
            pl.when(number == (stage + 1) * tiles // stages)(functools.partial(weight_stage, stage))
        pieces = []
        for h in range(heads):
            scores = dot(s.kf[h], s.qf[h, :, span])
            largest = jnp.max(scores, axis=0, keepdims=True)
            weights = jnp.exp2(scores - largest)
            total = jnp.sum(weights, axis=0, keepdims=True)
            out = dot(s.vt[h * head : (h + 1) * head, :], weights.astype(BF16))
            pieces.append(out * (1.0 / total))
            lse = -(largest + jnp.log2(total))
            lh = lse.astype(BF16).astype(F32)
            lm = (lse - lh).astype(BF16).astype(F32)
            tail = s.qf[h, 2 * head : 2 * head + 16, span].astype(F32)
            tail = jnp.concatenate([tail[:8], lh, lm, lse - lh - lm, jnp.zeros((5, TILE), F32)], 0)
            s.qf[h, 2 * head : 2 * head + 16, span] = tail.astype(BF16)
        out = pieces[0] if heads == 1 else jnp.concatenate(pieces, 0)
        s.ot[:, span] = out
        s.att_post[step, :, pl.ds(pl.multiple_of(offset * TILE, TILE), TILE)] = out.astype(BF16)
        for there in range(rows - 1):
            pl.when(number == (there + 1) * per - 1)(functools.partial(att_posts[there].start))
        return carry

    lax.fori_loop(0, tiles, attend_step, 0)
    weight_stage(stages - 1)
    s.att[me] = s.att_post[rows - 1]
    for post in att_posts:
        post.recv()
    for post in own_c + [p for moves in (ups, downs) for move in moves for p in [move[1]] + move[3]]:
        post.recv()

    dot_lanes = pl.ds(pl.multiple_of(me * tok, 128), tok)
    dot_posts = [mail.make(s.dot_post.at[d["row"]], s.dot.at[:, dot_lanes], d) for d in row_peers]
    loads[3].wait()

    def middle(act_ref, slope_ref):
        count = 4
        wide = hidden // count // 128

        def put_vector(first, value):
            for i in range(value.shape[1] // 128):
                s.vec_part[first + i : first + i + 1, :] = value[:, i * 128 : (i + 1) * 128]

        bias_out, gain_one, shift_one = vector(2 * lines), vector(3 * lines), vector(4 * lines)
        last = 5 * lines + hidden // 128
        bias_two, gain_two, shift_two = vector(last), vector(last + lines), vector(last + 2 * lines)

        def w_one(n):
            return blocks_of(s.weights, 4 * square + n * wide, lines, wide, hidden // 128)

        def w_two(n):
            first = 4 * square + lines * hidden // 128
            return blocks_of(s.weights, first + n * wide * lines, wide, lines, lines)

        def put_grad(first, stride, value):
            for i in range(value.shape[0] // 128):
                for j in range(value.shape[1] // 128):
                    row = (3 * square + first + i * stride + j) * 128
                    s.grad[row : row + 128, :] = value[i * 128 : (i + 1) * 128, j * 128 : (j + 1) * 128]

        attended_t = jnp.concatenate([s.att[r] for r in range(rows)], 0)
        w_out = blocks_of(s.weights, 3 * square, lines, lines, lines)
        branch = dot(attended_t, w_out, TN) + bias_out
        unit_one, scale_one = norm_forward(s.tokens[...] + branch)
        normed = unit_one * gain_one + shift_one
        normed_low = normed.astype(BF16)
        second = jnp.zeros((tok, width), F32)
        for n in range(count):
            pre = dot(normed_low, w_one(n)) + vector(5 * lines + n * wide, wide)
            square_pre = pre * pre
            curve = jnp.tanh(0.7978845608028654 * pre * (1.0 + 0.044715 * square_pre))
            half_one = 0.5 * (1.0 + curve)
            act = (pre * half_one).astype(BF16)
            slope_ref[n] = half_one + 0.5 * pre * (1.0 - curve * curve) * (
                0.7978845608028654 * (1.0 + 0.134145 * square_pre)
            )
            act_ref[n] = act
            second = second + dot(act, w_two(n))
        unit_two, scale_two = norm_forward(normed + (second + bias_two))
        s.layer[...] = unit_two * gain_two + shift_two
        cot = s.cot[...]
        put_vector(last + lines, column_sum(cot * unit_two))
        put_vector(last + 2 * lines, column_sum(cot))
        sum_grad = norm_backward(cot, gain_two, unit_two, scale_two)
        second_grad = sum_grad.astype(BF16)
        put_vector(last, column_sum(second_grad.astype(F32)))
        normed_grad = sum_grad
        for n in range(count):
            two = w_two(n)
            hidden_grad = (dot(second_grad, two, NT) * slope_ref[n]).astype(BF16)
            put_vector(5 * lines + n * wide, column_sum(hidden_grad.astype(F32)))
            normed_grad = normed_grad + dot(hidden_grad, w_one(n), NT)
            first = lines * hidden // 128 + square + n * wide * lines
            put_grad(first, lines, dot(act_ref[n], second_grad, TN))
            put_grad(square + n * wide, hidden // 128, dot(normed_low, hidden_grad, TN))
        put_vector(3 * lines, column_sum(normed_grad * unit_one))
        put_vector(4 * lines, column_sum(normed_grad))
        branch_grad = norm_backward(normed_grad, gain_one, unit_one, scale_one)
        s.branch[...] = branch_grad
        branch_low = branch_grad.astype(BF16)
        grad_t = dot(w_out, branch_low, NT).astype(BF16)
        for r in range(rows):
            s.dot_post[r] = grad_t[r * part : (r + 1) * part, :]
        for post in dot_posts:
            post.start()
        s.dot[:, dot_lanes] = s.dot_post[me]
        put_vector(2 * lines, column_sum(branch_low.astype(F32)))
        put_grad(0, lines, dot(attended_t, branch_low))

    pl.run_scoped(middle, pltpu.VMEM((4, tok, hidden // 4), BF16), pltpu.VMEM((4, tok, hidden // 4), F32))

    store(s.layer, s.layer_out)

    chunks, size, share = z.chunks, z.size, z.share
    s.grad[: 3 * square * 128, :] = jnp.zeros((3 * square * 128, 128), F32)

    def grad_rows(chunk, x, c, y, z):
        row = (z * ny + y) * (rows * share) + (x * 2 + c) * share + chunk * size
        return s.grad[pl.ds(pl.multiple_of(row, 16), size), :]

    def order(chunk):
        return ("x", "y") if chunk % 2 == 0 else ("y", "x")

    def spot(chunk, one, two, zz):
        return {order(chunk)[0]: one, order(chunk)[1]: two, "z": zz}

    hops0, hops1, hops2, hops3, hops4 = [], [], [], [], []
    for chunk in range(chunks):
        n2 = place.size[order(chunk)[1]]
        hops0.append(mail.make(s.stage0.at[chunk], s.recv0.at[chunk], partner[1]))
        made = []
        for step, (_, device) in enumerate(near[order(chunk)[0]]):
            span = pl.ds(step * n2 * nz, n2 * nz)
            made.append(mail.make(s.stage1.at[chunk, span], s.recv1.at[chunk, span], device))
        hops1.append(made)
        made = []
        for step, (_, device) in enumerate(near[order(chunk)[1]]):
            span = pl.ds(step * nz, nz)
            made.append(mail.make(s.stage2.at[chunk, span], s.recv2.at[chunk, span], device))
        hops2.append(made)
        hops3.append(
            [mail.make(s.stage3.at[chunk, step], s.recv3.at[chunk, step], d) for step, (_, d) in enumerate(near["z"])]
        )
        mine = pl.ds(pl.multiple_of(me * share + chunk * size, 16), size)
        hops4.append([mail.make(s.owned.at[mine], s.owned.at[mine], device) for device in row_peers])

    def reduce_cores():
        for chunk in range(chunks):
            n1, n2 = [place.size[d] for d in order(chunk)]
            for one in range(n1):
                for two in range(n2):
                    for zz in range(nz):
                        rows_of = grad_rows(chunk, c=partner[0], **spot(chunk, one, two, zz))
                        s.stage0[chunk, (one * n2 + two) * nz + zz] = rows_of.astype(BF16)
            hops0[chunk].start()

    def reduce_first():
        for chunk in range(chunks):
            n1, n2 = [place.size[d] for d in order(chunk)]
            hops0[chunk].recv()

            def summed(one, two, zz):
                slot = (one * n2 + two) * nz + zz
                rows_of = grad_rows(chunk, c=at["c"], **spot(chunk, one, two, zz))
                return rows_of + s.recv0[chunk, slot].astype(F32)

            for step, (there, _) in enumerate(near[order(chunk)[0]]):
                for two in range(n2):
                    for zz in range(nz):
                        s.stage1[chunk, step * n2 * nz + two * nz + zz] = summed(there, two, zz).astype(BF16)
                hops1[chunk][step].start()
            for two in range(n2):
                for zz in range(nz):
                    s.kept1[chunk, two * nz + zz] = summed(at[order(chunk)[0]], two, zz)

    def reduce_second():
        for chunk in range(chunks):
            n1, n2 = [place.size[d] for d in order(chunk)]
            for hop in hops1[chunk]:
                hop.recv()

            def summed(two, zz):
                total = s.kept1[chunk, two * nz + zz]
                for step in range(n1 - 1):
                    total = total + s.recv1[chunk, step * n2 * nz + two * nz + zz].astype(F32)
                return total

            for step, (there, _) in enumerate(near[order(chunk)[1]]):
                for zz in range(nz):
                    s.stage2[chunk, step * nz + zz] = summed(there, zz).astype(BF16)
                hops2[chunk][step].start()
            for zz in range(nz):
                s.kept2[chunk, zz] = summed(at[order(chunk)[1]], zz)

    def reduce_third():
        for chunk in range(chunks):
            n2 = place.size[order(chunk)[1]]
            for hop in hops2[chunk]:
                hop.recv()

            def summed(zz):
                total = s.kept2[chunk, zz]
                for step in range(n2 - 1):
                    total = total + s.recv2[chunk, step * nz + zz].astype(F32)
                return total

            for step, (there, _) in enumerate(near["z"]):
                s.stage3[chunk, step] = summed(there).astype(BF16)
                hops3[chunk][step].start()
            s.kept2[chunk, at["z"]] = summed(at["z"])

    def reduce_last():
        for chunk in range(chunks):
            total = s.kept2[chunk, at["z"]]
            for step, hop in enumerate(hops3[chunk]):
                hop.recv()
                total = total + s.recv3[chunk, step].astype(F32)
            mine = pl.ds(pl.multiple_of(me * share + chunk * size, 16), size)
            s.owned[mine, :] = total.astype(BF16)
            for hop in hops4[chunk]:
                hop.start()

    reduce_stages = ((0, reduce_first), (3, reduce_second), (5, reduce_third))
    reduce_cores()
    for post in dot_posts:
        post.recv()

    scale = head**-0.5
    posts = [mail.make(s.post.at[d["row"]], s.got.at[me], d) for d in row_peers]

    def backward(df_ref, mix_ref, both_ref, pair_ref, qt_ref):
        lane = lax.broadcasted_iota(jnp.int32, (tok, part), 1)
        for r in range(rows):
            span = slice(r * tok, (r + 1) * tok)
            grad_t = s.dot[:, span].astype(F32)
            center = grad_t * s.ot[:, span]
            grad_rows_in = grad_t.T
            queries = s.q[span, :].astype(F32)
            scaled = grad_t * scale
            g_high = scaled.astype(BF16).astype(F32)
            g_low = scaled - g_high
            for h in range(heads):
                own_lines = slice(h * head, (h + 1) * head)
                shift = -scale * column_sum(center[own_lines])
                sh = shift.astype(BF16).astype(F32)
                sm = (shift - sh).astype(BF16).astype(F32)
                rest = jnp.zeros((128 - 2 * head - 3, tok), F32)
                df_ref[h, :, span] = jnp.concatenate(
                    [g_high[own_lines], g_low[own_lines], sh, sm, shift - sh - sm, rest], 0
                ).astype(BF16)
                mine = (lane >= h * head) & (lane < (h + 1) * head)
                none = jnp.zeros((tok, part), F32)
                free = [jnp.zeros((tok, 128 - 2 * part), F32)] if part < 64 else []
                mix_ref[2 * h, span, :] = jnp.concatenate(
                    [jnp.where(mine, grad_rows_in, 0.0), none] + free, 1
                ).astype(BF16)
                mix_ref[2 * h + 1, span, :] = jnp.concatenate(
                    [none, jnp.where(mine, queries, 0.0)] + free, 1
                ).astype(BF16)
        pair_ref[...] = jnp.zeros_like(pair_ref)
        turns = z.pack_len // TILE

        def tile_step(number, carry):
            span = pl.ds(pl.multiple_of(number * TILE, TILE), TILE)
            for eighth, action in reduce_stages:
                pl.when(number == eighth * turns // 8)(action)
            pieces, mix = [], []
            for h in range(heads):
                probs = jnp.exp2(dot(s.kf[h], s.qf[h, :, span]))
                along = dot(s.vf[h], df_ref[h, :, span])
                both_ref[:, 2 * h * TILE : (2 * h + 1) * TILE] = probs.astype(BF16)
                score_grad = (probs * along).astype(BF16)
                both_ref[:, (2 * h + 1) * TILE : (2 * h + 2) * TILE] = score_grad
                pieces.append(dot(s.kt[h * head : (h + 1) * head, :], score_grad))
                mix += [mix_ref[2 * h, span, :], mix_ref[2 * h + 1, span, :]]
            qt_ref[:, span] = pieces[0] if heads == 1 else jnp.concatenate(pieces, 0)
            pair_ref[...] += dot(both_ref[...], jnp.concatenate(mix, 0))
            return carry

        lax.fori_loop(0, turns, tile_step, 0)
        for r in range(rows):
            span = slice(r * tok, (r + 1) * tok)
            pair = pair_ref[span, :].T
            s.post[r] = jnp.concatenate([qt_ref[:, span], pair[part : 2 * part], pair[:part]], 0).astype(BF16)

    pl.run_scoped(
        backward,
        pltpu.VMEM((heads, 128, z.pack_len), BF16),
        pltpu.VMEM((2 * heads, z.pack_len, 128), BF16),
        pltpu.VMEM((z.pack_len, 2 * heads * TILE), BF16),
        pltpu.VMEM((z.pack_len, 128), F32),
        pltpu.VMEM((part, z.pack_len), F32),
    )

    joint, owners = z.joint, z.owners
    size_l = z.late // joint
    for kind, first, last in (("placed", 0, 2 * part), ("plain", 2 * part, 3 * part)):
        base = getattr(s, kind)
        total = jnp.zeros((last - first, width), F32)
        for r in range(rows):
            total = total + dot(s.post[r, first:last, :], base[r * tok : (r + 1) * tok, :])
        for i in range(lines):
            row = i * 3 * part + first
            s.late[row : row + last - first, :] = total[:, i * 128 : (i + 1) * 128]
    s.late_post[...] = s.late[...].astype(BF16)
    spread_posts = []
    joined = None if joint == z.packs else pack < joint
    for step in range(1, z.packs):
        there = lax.rem(pack + step, z.packs)
        lands = None if joint == z.packs else there < joint
        rows_of = pl.ds(pl.multiple_of(lax.rem(there, joint) * size_l, 16), size_l)
        spread_posts.append(
            mail.put(
                s.late_post.at[rows_of, :], s.late_recv.at[step - 1], {"pack": there, "row": me}, lands, joined
            )
        )

    ones = jnp.ones((16, tok), BF16)
    sums = jnp.zeros((16, 3 * part), F32)
    for r in range(rows):
        sums = sums + dot(ones, s.post[r], NT)
    for n in (0, 2):
        row = jnp.concatenate([sums[:8, n * part : (n + 1) * part], jnp.zeros((8, width - part), F32)], 1)
        row = pltpu.roll(row, me * part, 1)
        for i in range(lines):
            line_of = (n // 2) * lines + i
            s.vec_part[line_of : line_of + 1, :] = row[:1, i * 128 : (i + 1) * 128]

    def vec_step(dim, buffer, value):
        buffer[at[dim]] = value
        return [mail.put(buffer.at[at[dim]], buffer.at[at[dim]], device) for _, device in place.peers(dim)]

    def vec_sum(hops, buffer):
        for hop in hops:
            hop.recv()
        total = buffer[0]
        for number in range(1, buffer.shape[0]):
            total = total + buffer[number]
        return total

    vec_hops = vec_step("c", s.vec_c, s.vec_part[...])
    reduce_last()
    own_late = pl.ds(pl.multiple_of(lax.rem(pack, joint) * size_l, 16), size_l)
    for post in spread_posts:
        post.recv()
    total = s.late[own_late, :]
    for step in range(z.packs - 1):
        total = total + s.late_recv[step].astype(F32)
    s.late_share[...] = total.astype(BF16)
    s.late_all[me, own_late, :] = total.astype(BF16)
    for owner in range(owners):
        for step in range(rows):
            leaves = either([pack == giver for giver in sorted(z.givers[owner]) if step or giver != owner])
            mail.put(
                s.late_share, s.late_all.at[me, own_late, :],
                {"pack": pack * 0 + owner, "row": lax.rem(me + step, rows)}, leaves, None,
                late_sem.at[lax.rem(pack, joint), step],
            )
    vec_hops = vec_step("x", s.vec_x, vec_sum(vec_hops, s.vec_c))
    for post in posts:
        post.start()
    s.got[me] = s.post[me]
    for load in loads[4:]:
        load.wait()
    for chunk in range(chunks):
        for hop in hops4[chunk]:
            hop.recv()
            hop.sent()

    def late_wait():
        for giver in range(joint):
            for step in range(rows):

                def wait():
                    pltpu.make_async_remote_copy(
                        src_ref=s.late_share, dst_ref=s.late_all.at[0, :size_l, :],
                        send_sem=send_sem.at[0], recv_sem=late_sem.at[giver, step],
                        device_id={"pack": pack, "row": lax.rem(me + 1, rows)}, device_id_type=MESH,
                    ).wait_recv()

                takers = [n for n in range(owners) if giver in z.givers[n] and (step or n != giver)]
                if takers:
                    pl.when(either([pack == n for n in takers]))(wait)
        for b in range(3 * square):
            kind, i, j = b // square, b % square // lines, b % lines

            def place_block():
                start = (i * 3 + kind) * part
                found = [s.late_all[r, start : start + part, :] for r in range(j * 128 // part, (j + 1) * 128 // part)]
                block = jnp.concatenate(found, 0).astype(F32).T
                row = b % z.blocks * 128
                s.owned[row : row + 128, :] = block.astype(BF16)

            pl.when(pack == b // z.blocks)(place_block)

    pl.when(pack < owners)(late_wait)
    vec_hops = vec_step("y", s.vec_y, vec_sum(vec_hops, s.vec_x))
    blocks, slots = z.blocks, z.slots
    for n in range(slots):
        t = jnp.minimum(me * slots + n, 2 * blocks - 1)
        is_right = t >= blocks
        rows_of = pl.ds(pl.multiple_of(jnp.where(is_right, t - blocks, t) * 128, 128), 128)
        g = s.owned[rows_of, :].astype(F32)
        g = jnp.where(is_right, g.T, g).astype(BF16)
        stat = jnp.where(is_right, s.right[rows_of, :], s.left[rows_of, :])
        basis = jnp.where(is_right, s.rbasis[rows_of, :], s.lbasis[rows_of, :])
        new = BETA_TWO * stat + (1.0 - BETA_TWO) * dot(g, g, NT)
        a = dot6(new, basis)
        a_t = a.T
        s.gram[n, :, :128] = dot6(a_t, a)
        s.gram[n, :, 128:] = a_t
    def block_step(number, carry):
        rows_of = pl.ds(pl.multiple_of(number * 128, 128), 128)
        g = s.owned[rows_of, :]
        s.left_new[rows_of, :] = BETA_TWO * s.left[rows_of, :] + (1.0 - BETA_TWO) * dot(g, g, NT)
        s.right_new[rows_of, :] = BETA_TWO * s.right[rows_of, :] + (1.0 - BETA_TWO) * dot(g, g, TN)
        lb, rb = s.lbasis[rows_of, :], s.rbasis[rows_of, :]
        lh, ll = split2(lb)
        turned = dot(jnp.concatenate([lh, ll], 0), jnp.concatenate([g, g], 0), TN)
        rotated = dot3(turned, rb)
        first = BETA_ONE * s.first[rows_of, :] + (1.0 - BETA_ONE) * rotated
        second = BETA_TWO * s.second[rows_of, :] + (1.0 - BETA_TWO) * rotated * rotated
        s.first_new[rows_of, :] = first
        s.second_new[rows_of, :] = second
        ratio = first / (1.0 - BETA_ONE**STEP) / (jnp.sqrt(second / (1.0 - BETA_TWO**STEP)) + EPSILON)
        stepped = dot3(dot3(lb, ratio), rb, NT)
        weights = s.master[rows_of, :]
        weights = weights - LEARN_RATE * (stepped + WEIGHT_DECAY * weights)
        s.master_new[rows_of, :] = weights
        s.copy_new[rows_of, :] = weights.astype(BF16)
        return carry

    targets = [partner[1]] + [device for _, device in near["x"]]
    panel_first = mail.reserve(8 * len(targets))

    def panel_post(index, number):
        rows_of = pl.ds(pl.multiple_of(index * 16, 16), 16)
        place_in = s.turned.at[me, :, rows_of, :]
        sem = panel_first + number * 8 + index
        return pltpu.make_async_remote_copy(
            src_ref=place_in, dst_ref=place_in, send_sem=send_sem.at[sem], recv_sem=recv_sem.at[sem],
            device_id=targets[number], device_id_type=MESH,
        )

    def panel(index, carry):
        block_step(jnp.minimum(index, blocks - 1), 0)
        panel_step(pl.multiple_of(index * 16, 16), s.gram, s.turned.at[me], slots)
        for number in range(len(targets)):
            panel_post(index, number).start()
        return carry

    lax.fori_loop(0, 8, panel, 0)
    vec_hops = vec_step("z", s.vec_z, vec_sum(vec_hops, s.vec_y))
    lax.fori_loop(8, max(blocks, 8), block_step, 0)
    for name in ("first", "second", "master", "copy", "left", "right"):
        store(getattr(s, name + "_new"), getattr(s, name + "_out"))

    def turn(row):
        for n in range(slots):
            t = row * slots + n

            @pl.when(t < 2 * blocks)
            def _():
                s.bases[pl.ds(pl.multiple_of(t * 128, 128), 128), :] = s.turned[row, n].T

    relays = []
    for step in range(nx - 1):
        for index in range(8):
            panel_post(index, 1 + step).wait_recv()
        row = source("x", step) * 2 + at["c"]
        relays.append(mail.put(s.turned.at[row], s.turned.at[row], partner[1]))
    for row in [me] + [source("x", step) * 2 + at["c"] for step in range(nx - 1)]:
        turn(row)
    for post in posts:
        post.recv()
    total = s.branch[...]
    for n in range(3):
        grad_t = jnp.concatenate([s.got[r, n * part : (n + 1) * part, :] for r in range(rows)], 0)
        weight = blocks_of(s.weights, n * square, lines, lines, lines)
        total = total + dot(grad_t, weight, (((0,), (1,)), ((), ())))
    s.input[...] = total
    store(s.input, s.input_out)
    grad = vec_sum(vec_hops, s.vec_z)
    first = BETA_ONE * s.vec_first[...] + (1.0 - BETA_ONE) * grad
    second = BETA_TWO * s.vec_second[...] + (1.0 - BETA_TWO) * grad * grad
    ratio = first / (1.0 - BETA_ONE**STEP) / (jnp.sqrt(second / (1.0 - BETA_TWO**STEP)) + EPSILON)
    s.vec_new[0] = s.vec[...] - LEARN_RATE * ratio
    s.vec_new[1] = first
    s.vec_new[2] = second
    for number, name in enumerate(("vec", "vec_first", "vec_second")):
        store(s.vec_new.at[number], getattr(s, name + "_out"))
    for index in range(8):
        panel_post(index, 0).wait_recv()
    turn(lax.div(me, 2) * 2 + partner[0])
    for step, relay in enumerate(relays):
        relay.recv()
        turn(source("x", step) * 2 + partner[0])
    store(s.bases.at[: z.owned, :], s.lbasis_out)
    store(s.bases.at[z.owned : 2 * z.owned, :], s.rbasis_out)
    for copy in stores:
        copy.wait()
    for index in range(8):
        for number in range(len(targets)):
            panel_post(index, number).wait_send()
    mail.finish(z.posts)


def finish_kernel(count, *refs):
    sems = refs[-1]
    loads = [pltpu.make_async_copy(refs[i], refs[2 * count + i], sems.at[i]) for i in range(count)]
    stores = [pltpu.make_async_copy(refs[2 * count + i], refs[count + i], sems.at[count + i]) for i in range(count)]
    for load in loads:
        load.start()
    for load, copy in zip(loads, stores):
        load.wait()
        copy.start()
    for copy in stores:
        copy.wait()


def shards(
    tokens, cotangent, segment_ids, padding, master, moment_first, moment_second,
    stat_left, stat_right, basis_left, basis_right, vec_params, vec_first, vec_second,
):
    packs, rows = lax.axis_size("pack"), lax.axis_size("row")
    tok, width = tokens.shape
    z = Sizes(packs, rows, tok, width, vec_params.shape[0] - 8 * width, master.shape[0])
    table = jnp.asarray(sine_rows(z.pack_len, width // 2))
    full = jax.ShapeDtypeStruct(master.shape, F32)
    layer = jax.ShapeDtypeStruct(tokens.shape, F32)
    shapes = (layer, layer, full, full, full, jax.ShapeDtypeStruct(master.shape, BF16), full, full, full, full)
    shapes = shapes + (jax.ShapeDtypeStruct((32, 128), F32),) * 3
    scratch = vmem_scratch(z)
    vm, hbm = pl.BlockSpec(memory_space=pltpu.VMEM), pl.BlockSpec(memory_space=pl.ANY)
    outs = pl.pallas_call(
        functools.partial(layer_kernel, z, tuple(scratch)),
        out_shape=shapes,
        in_specs=[vm] * 5 + [hbm] * 10,
        out_specs=(hbm,) * len(shapes),
        scratch_shapes=list(scratch.values())
        + [
            pltpu.SemaphoreType.DMA((z.posts,)),
            pltpu.SemaphoreType.DMA((z.posts,)),
            pltpu.SemaphoreType.DMA((len(LOADS) + len(shapes),)),
            pltpu.SemaphoreType.DMA((packs, rows)),
        ],
        compiler_params=pltpu.CompilerParams(collective_id=1, has_side_effects=True, vmem_limit_bytes=63 << 20),
        name="layer",
    )(
        segment_ids.reshape(-1, 128), padding.reshape(-1, 128), vec_params.reshape(32, 128),
        vec_first.reshape(32, 128), vec_second.reshape(32, 128), tokens, master, table,
        cotangent, moment_first, moment_second, stat_left, stat_right, basis_left, basis_right,
    )
    outs = pl.pallas_call(
        functools.partial(finish_kernel, len(shapes)),
        out_shape=shapes,
        in_specs=[hbm] * len(shapes),
        out_specs=(hbm,) * len(shapes),
        scratch_shapes=[pltpu.VMEM(shape.shape, shape.dtype) for shape in shapes]
        + [pltpu.SemaphoreType.DMA((2 * len(shapes),))],
        compiler_params=pltpu.CompilerParams(vmem_limit_bytes=63 << 20),
        name="finish",
    )(*outs)
    return outs[:-3] + tuple(out.reshape(-1) for out in outs[-3:])


def solution(mesh):
    placed = (
        P(("pack", "row"), None),
        P(("pack", "row"), None),
        P(("pack", "row")),
        P(("pack", "row")),
        P("pack", None),
        P("pack", None),
        P("pack", None),
        P("pack", None),
        P("pack", None),
        P("pack", None),
        P("pack", None),
        P(),
        P(),
        P(),
    )
    return jax.shard_map(
        shards,
        mesh=mesh,
        in_specs=placed,
        out_specs=(
            P(("pack", "row"), None),
            P(("pack", "row"), None),
            P("pack", None),
            P("pack", None),
            P("pack", None),
            P("pack", None),
            P("pack", None),
            P("pack", None),
            P("pack", None),
            P("pack", None),
            P(),
            P(),
            P(),
        ),
        check_vma=False,
    )
```

```python
import functools
import types
import jax
import ml_dtypes
import numpy as np
import jax.numpy as jnp
from jax import lax
from jax.experimental import pallas as pl
from jax.experimental.pallas import tpu as pltpu
from jax.sharding import PartitionSpec as P

HEADS = 8
IMG_W = 32
MASKED_SCORE = -1e30
NORM_EPSILON = 1e-05
STEP = 10
BETA_ONE = 0.9
BETA_TWO = 0.95
LEARN_RATE = 0.25
WEIGHT_DECAY = 0.01
EPSILON = 1e-08
F32 = jnp.float32
BF16 = jnp.bfloat16
NN = (((1,), (0,)), ((), ()))
NT = (((1,), (1,)), ((), ()))
TN = (((0,), (0,)), ((), ()))
MESH = pl.DeviceIdType.MESH


class Place:
    def __init__(self, packs, rows):
        self.packs, self.rows = packs, rows
        self.nx = rows // 2
        self.ny = self.nx if packs % self.nx == 0 else 1
        self.nz = packs // self.ny
        self.size = {"c": 2, "x": self.nx, "y": self.ny, "z": self.nz}

    def locate(self):
        self.p = lax.axis_index("pack")
        self.r = lax.axis_index("row")
        self.at = {
            "c": lax.rem(self.r, 2),
            "x": lax.div(self.r, 2),
            "y": lax.rem(self.p, self.ny),
            "z": lax.div(self.p, self.ny),
        }
        return self

    def device(self, **moved):
        at = {**self.at, **moved}
        return {"pack": at["z"] * self.ny + at["y"], "row": at["x"] * 2 + at["c"]}

    def other(self, dim, step):
        return lax.rem(self.at[dim] + step, self.size[dim])

    def peers(self, dim):
        found = []
        for step in range(1, self.size[dim]):
            there = self.other(dim, step)
            found.append((there, self.device(**{dim: there})))
        return found

    def row_peers(self):
        return [
            {"pack": self.p, "row": lax.rem(self.r + step, self.rows)} for step in range(1, self.rows)
        ]


def dot(left, right, dims=NN):
    return lax.dot_general(left, right, dims, preferred_element_type=F32)


def split2(v):
    high = v.astype(BF16)
    return high, (v - high.astype(F32)).astype(BF16)


def split3(v):
    high = v.astype(BF16)
    rest = v - high.astype(F32)
    mid = rest.astype(BF16)
    return high, mid, (rest - mid.astype(F32)).astype(BF16)


def dot3(left, right, dims=NN):
    la, ra = dims[0][0][0], dims[0][1][0]
    lh, ll = split2(left)
    rh, rl = split2(right)
    return dot(jnp.concatenate([lh, ll, lh], la), jnp.concatenate([rh, rh, rl], ra), dims)


def dot6(left, right, dims=NN):
    la, ra = dims[0][0][0], dims[0][1][0]
    lh, lm, ll = split3(left)
    rh, rm, rl = split3(right)
    return dot(
        jnp.concatenate([lh, lh, lm, lm, lh, ll], la),
        jnp.concatenate([rh, rm, rh, rm, rl, rh], ra),
        dims,
    )


def four_pivots(g, a, first, sub):
    cols = [jnp.broadcast_to(g[:, first + k : first + k + 1], (16, 128)) for k in range(4)]
    lower, inverse, factors, rows_g, rows_a = {}, [], [], [], []
    for k in range(4):
        pivot = cols[k][first + k : first + k + 1, :]
        column, row_g, row_a = cols[k], g[first + k : first + k + 1, :], a[first + k : first + k + 1, :]
        for m in range(k):
            pivot = pivot - lower[k, m] * lower[k, m]
            column = column - factors[m] * lower[k, m]
            row_g = row_g - rows_g[m] * lower[k, m]
            row_a = row_a - rows_a[m] * lower[k, m]
        inverse = lax.rsqrt(pivot)
        for n in range(k + 1, 4):
            entry = cols[k][first + n : first + n + 1, :]
            for m in range(k):
                entry = entry - lower[n, m] * lower[k, m]
            lower[n, k] = entry * inverse
        factors.append(column * inverse)
        rows_g.append(row_g * inverse)
        rows_a.append(row_a * inverse)
    below = sub > first + 3
    for k in range(4):
        factor = jnp.where(below, factors[k], 0.0)
        g = g - factor * rows_g[k]
        a = a - factor * rows_a[k]
    for k in range(4):
        g = jnp.where(sub == first + k, rows_g[k], g)
        a = jnp.where(sub == first + k, rows_a[k], a)
    return g, a


def panel_step(base, m_ref, out_ref, count):
    sub = lax.broadcasted_iota(jnp.int32, (16, 128), 0)
    back = lax.rem(128 - base, 128)
    gram = [pltpu.roll(m_ref[n, pl.ds(base, 16), :128], back, 1) for n in range(count)]
    rest = [m_ref[n, pl.ds(base, 16), 128:] for n in range(count)]
    for first in range(0, 16, 4):
        for n in range(count):
            gram[n], rest[n] = four_pivots(gram[n], rest[n], first, sub)
    for n in range(count):
        out_ref[n, pl.ds(base, 16), :] = rest[n]
    for n in range(count):
        uh, um, ul = split3(pltpu.roll(gram[n], base, 1))
        ah, am, al = split3(rest[n])
        wh, wm, wl = [jnp.concatenate(p, 1) for p in ((uh, ah), (um, am), (ul, al))]
        m_ref[n] -= dot(
            jnp.concatenate([uh, uh, um, um, uh, ul], 0),
            jnp.concatenate([wh, wm, wh, wm, wl, wh], 0),
            TN,
        )


def flat_rows(ref, count):
    return jnp.concatenate([ref[i : i + 1, :] for i in range(count)], 1)


def blocks_of(ref, first, down, across, stride):
    lines = []
    for i in range(down):
        row = [ref[pl.ds((first + i * stride + j) * 128, 128), :] for j in range(across)]
        lines.append(row[0] if across == 1 else jnp.concatenate(row, 1))
    return lines[0] if down == 1 else jnp.concatenate(lines, 0)


TILE = 256
LOG2E = 1.4426950408889634


def sine_rows(pack_len, half):
    column = np.arange(half)
    period = np.float32(10000.0) ** ((2 * (column // 2)).astype(np.float32) / np.float32(half))
    high = pack_len // IMG_W
    angles = np.arange(max(high, IMG_W)).astype(np.float32)[:, None] / period[None, :].astype(np.float32)
    angles = angles.astype(np.float64)
    table = np.where(column[None, :] % 2 == 0, np.sin(angles), np.cos(angles)).astype(np.float32)
    both = np.zeros((high + IMG_W, 2 * half), np.float32)
    both[:high, :half] = table[:high]
    both[high:, half:] = table[:IMG_W]
    pieces, rest = [], both
    for _ in range(3):
        piece = rest.astype(ml_dtypes.bfloat16)
        pieces.append(piece)
        rest = rest - piece.astype(np.float32)
    return np.concatenate(pieces, 0)


def norm_forward(hidden):
    center = hidden - jnp.mean(hidden, axis=-1, keepdims=True)
    scale = lax.rsqrt(jnp.mean(center * center, axis=-1, keepdims=True) + NORM_EPSILON)
    return center * scale, scale


def norm_backward(grad, gain, unit, scale):
    inner = grad * gain
    mean = jnp.mean(inner, axis=-1, keepdims=True)
    along = jnp.mean(inner * unit, axis=-1, keepdims=True)
    return scale * (inner - mean - unit * along)


def column_sum(values):
    return jnp.sum(values, axis=0, keepdims=True)


def when(condition, action):
    if condition is None:
        action()
    else:
        pl.when(condition)(action)


def either(conditions):
    return functools.reduce(jnp.logical_or, conditions)


class Post:
    def __init__(self, copy, send=None, recv=None):
        self.copy, self.send_if, self.recv_if, self.gone = copy, send, recv, False

    def start(self):
        when(self.send_if, lambda: self.copy.start())

    def recv(self):
        when(self.recv_if, lambda: self.copy.wait_recv())

    def sent(self):
        if not self.gone:
            when(self.send_if, lambda: self.copy.wait_send())
        self.gone = True


class Mail:
    def __init__(self, send_sem, recv_sem):
        self.send_sem, self.recv_sem, self.posts = send_sem, recv_sem, []

    def make(self, source, target, device, send=None, recv=None, recv_sem=None):
        index = len(self.posts)
        copy = pltpu.make_async_remote_copy(
            src_ref=source, dst_ref=target,
            send_sem=self.send_sem.at[index],
            recv_sem=self.recv_sem.at[index] if recv_sem is None else recv_sem,
            device_id=device, device_id_type=MESH,
        )
        post = Post(copy, send, recv)
        self.posts.append(post)
        return post

    def reserve(self, count):
        start = len(self.posts)
        self.posts += [None] * count
        return start

    def put(self, *args, **kinds):
        post = self.make(*args, **kinds)
        post.start()
        return post

    def finish(self, count):
        assert len(self.posts) == count
        for post in self.posts:
            if post is not None:
                post.sent()


def greet(devices):
    barrier = pltpu.get_barrier_semaphore()
    for device in devices:
        pl.semaphore_signal(barrier, inc=1, device_id=device, device_id_type=MESH)
    pl.semaphore_wait(barrier, len(devices))


class Sizes:
    def __init__(self, packs, rows, tok, width, hidden, owned):
        self.packs, self.rows, self.tok, self.width, self.hidden, self.owned = packs, rows, tok, width, hidden, owned
        self.pack_len = rows * tok
        self.heads = HEADS // rows
        self.part = width // rows
        self.head = width // HEADS
        self.lines = width // 128
        self.square = self.lines * self.lines
        self.total = packs * owned
        self.blocks = owned // 128
        self.slots = -(-2 * self.blocks // rows)
        place = Place(packs, rows)
        self.nx, self.ny, self.nz = place.nx, place.ny, place.nz
        self.share = self.total // (packs * rows)
        self.chunks = 2 if self.share % 32 == 0 else 1
        self.size = self.share // self.chunks
        self.late = 3 * self.part * self.lines
        self.joint = max(n for n in range(1, packs + 1) if packs % n == 0 and self.late % (16 * n) == 0)
        self.owners = -(-3 * self.square // self.blocks)
        self.givers = [set() for _ in range(self.owners)]
        for b in range(3 * self.square):
            kind, i = b // self.square, b % self.square // self.lines
            start = (i * 3 + kind) * self.part
            size = self.late // self.joint
            self.givers[b // self.blocks] |= set(range(start // size, (start + self.part - 1) // size + 1))
        over_x, over_y, over_z, peers = self.nx - 1, self.ny - 1, self.nz - 1, rows - 1
        gather = peers + 2 * over_x + 1 + 8 * (1 + over_y) + 2 * over_y + (2 * over_z - 1) * (2 + 2 * over_y)
        reduce = self.chunks * (1 + over_x + over_y + over_z + peers)
        vector = 1 + over_x + over_y + over_z
        bases = 8 * (over_x + 1) + over_x
        self.posts = gather + 3 * peers + reduce + packs - 1 + vector + self.owners * rows + bases


def vmem_scratch(z):
    half, most = z.nx * z.ny * z.nz, max(z.nx, z.ny)
    ring = half // min(z.nx, z.ny)
    f = lambda *shape: pltpu.VMEM(shape, F32)
    b = lambda *shape: pltpu.VMEM(shape, BF16)
    return dict(
        tokens_all=f(z.rows, z.tok, z.width),
        codes_all=pltpu.VMEM((z.rows, 2 * z.tok // 128, 128), jnp.int32),
        weights=b(z.total, 128),
        placed=b(z.pack_len, z.width), plain=b(z.pack_len, z.width),
        kf=b(z.heads, z.pack_len, 128), qf=b(z.heads, 128, z.pack_len), vf=b(z.heads, z.pack_len, 128),
        kt=b(z.part, z.pack_len), vt=b(z.part, z.pack_len), q=b(z.pack_len, z.part), ot=f(z.part, z.pack_len),
        att_post=b(z.rows, z.part, z.tok), att=b(z.rows, z.part, z.tok),
        tokens=f(z.tok, z.width), codes=pltpu.VMEM((2 * z.tok // 128, 128), jnp.int32),
        master=f(z.owned, 128), table=b(3 * (z.pack_len // IMG_W + IMG_W), z.width),
        cot=f(z.tok, z.width), layer=f(z.tok, z.width), branch=f(z.tok, z.width),
        dot_post=b(z.rows, z.part, z.tok), dot=b(z.part, z.pack_len),
        grad=f(z.total, 128), vec_part=f(32, 128),
        stage0=b(z.chunks, half, z.size, 128), recv0=b(z.chunks, half, z.size, 128),
        stage1=b(z.chunks, half * (most - 1) // most, z.size, 128),
        recv1=b(z.chunks, half * (most - 1) // most, z.size, 128),
        kept1=f(z.chunks, ring, z.size, 128),
        stage2=b(z.chunks, (most - 1) * z.nz, z.size, 128), recv2=b(z.chunks, (most - 1) * z.nz, z.size, 128),
        kept2=f(z.chunks, z.nz, z.size, 128),
        stage3=b(z.chunks, z.nz, z.size, 128), recv3=b(z.chunks, z.nz, z.size, 128),
        vec_c=f(2, 32, 128), vec_x=f(z.nx, 32, 128), vec_y=f(z.ny, 32, 128), vec_z=f(z.nz, 32, 128),
        post=b(z.rows, 3 * z.part, z.tok), got=b(z.rows, 3 * z.part, z.tok),
        late=f(z.late, 128), late_post=b(z.late, 128), late_recv=b(z.packs, z.late // z.joint, 128),
        late_share=b(z.late // z.joint, 128), late_all=b(z.rows, z.late, 128),
        owned=b(z.owned, 128),
        first=f(z.owned, 128), second=f(z.owned, 128), left=f(z.owned, 128), right=f(z.owned, 128),
        lbasis=f(z.owned, 128), rbasis=f(z.owned, 128),
        gram=f(z.slots, 128, 256), turned=f(z.rows, z.slots, 128, 128), bases=f(2 * z.owned, 128),
        first_new=f(z.owned, 128), second_new=f(z.owned, 128), master_new=f(z.owned, 128), copy_new=b(z.owned, 128),
        left_new=f(z.owned, 128), right_new=f(z.owned, 128), input=f(z.tok, z.width), vec_new=f(3, 32, 128),
    )


LOADS = ("tokens", "master", "table", "cot", "first", "second", "left", "right", "lbasis", "rbasis")


def layer_kernel(z, names, *refs):
    inputs = (
        "ids", "pad", "vec", "vec_first", "vec_second", "tokens_in", "master_in", "table_in",
        "cot_in", "first_in", "second_in", "left_in", "right_in", "lbasis_in", "rbasis_in",
    )
    outputs = (
        "layer_out", "input_out", "first_out", "second_out", "master_out", "copy_out", "left_out", "right_out",
        "lbasis_out", "rbasis_out", "vec_out", "vec_first_out", "vec_second_out",
    )
    s = types.SimpleNamespace(**dict(zip(inputs + outputs + tuple(names), refs)))
    send_sem, recv_sem, load_sem, late_sem = refs[-4:]
    loads = [
        pltpu.make_async_copy(getattr(s, name + "_in"), getattr(s, name), load_sem.at[i]) for i, name in enumerate(LOADS)
    ]
    for load in loads:
        load.start()
    stores = []

    def store(source, target):
        copy = pltpu.make_async_copy(source, target, load_sem.at[len(loads) + len(stores)])
        copy.start()
        stores.append(copy)

    place = Place(z.packs, z.rows).locate()
    mail = Mail(send_sem, recv_sem)
    at, me, pack = place.at, place.r, place.p
    nx, ny, nz, rows, tok, part, head, heads = z.nx, z.ny, z.nz, z.rows, z.tok, z.part, z.head, z.heads
    lines, square, width, hidden = z.lines, z.square, z.width, z.hidden
    partner = place.peers("c")[0]
    near = {dim: place.peers(dim) for dim in ("x", "y", "z")}
    row_peers = place.row_peers()

    def source(dim, step):
        return lax.rem(at[dim] + place.size[dim] - 1 - step, place.size[dim])

    half = z.owned // 2
    quarter = half // 4

    def piece(zz, yy, k=None):
        start = (zz * ny + yy) * z.owned + at["c"] * half
        count = half
        if k is not None:
            start, count = start + k * quarter, quarter
        return s.weights.at[pl.ds(pl.multiple_of(start, 16), count), :]

    def to(dim, index):
        return place.device(**{dim: index})

    up, down = lax.rem(at["z"] + 1, nz), lax.rem(at["z"] + nz - 1, nz)
    inner = at["z"] >= 1
    below_top = at["z"] + 1 < nz
    send_codes = [mail.make(s.codes, s.codes_all.at[me], device) for device in row_peers]
    send_x = [mail.make(s.tokens, s.tokens_all.at[me], device) for _, device in near["x"]]
    send_c = mail.make(s.tokens, s.tokens_all.at[me], partner[1])
    relay_x = []
    for step in range(nx - 1):
        row = source("x", step) * 2 + at["c"]
        relay_x.append(mail.make(s.tokens_all.at[row], s.tokens_all.at[row], partner[1]))
    chain, chain_y, chain_c, chain_yc = [], [], [], []
    for k in range(4):
        part_k = piece(0, at["y"], k)
        chain.append(mail.make(part_k, part_k, to("z", up), send=below_top, recv=inner))
        chain_y.append([mail.make(part_k, part_k, device) for _, device in near["y"]])
        chain_c.append(mail.make(part_k, part_k, partner[1], send=inner, recv=inner))
        chain_yc.append([])
        for step in range(ny - 1):
            part_k = piece(0, source("y", step), k)
            chain_yc[k].append(mail.make(part_k, part_k, partner[1]))

    def spread(zz, condition):
        mine = piece(zz, at["y"])
        over_y = [mail.make(mine, mine, device, condition, condition) for _, device in near["y"]]
        theirs = [piece(zz, source("y", step)) for step in range(ny - 1)]
        over_c = [mail.make(ref, ref, partner[1], condition, condition) for ref in theirs]
        return over_y, over_c

    own_y, own_c = spread(at["z"], inner)
    ups, downs = [], []
    for j in range(nz - 2):
        mine, coming = lax.rem(at["z"] + nz - j, nz), lax.rem(at["z"] + nz - 1 - j, nz)
        there = at["z"] - 1 - j >= 1
        hop = mail.make(piece(mine, at["y"]), piece(mine, at["y"]), to("z", up), (at["z"] - j >= 1) & below_top, there)
        core = mail.make(piece(coming, at["y"]), piece(coming, at["y"]), partner[1], there, there)
        ups.append((hop, core) + spread(coming, there))
    for j in range(nz - 1):
        mine, coming = lax.rem(at["z"] + j, nz), lax.rem(at["z"] + 1 + j, nz)
        there = at["z"] + 1 + j < nz
        hop = mail.make(piece(mine, at["y"]), piece(mine, at["y"]), to("z", down), inner & (at["z"] + j < nz), there)
        core = mail.make(piece(coming, at["y"]), piece(coming, at["y"]), partner[1], there, there)
        downs.append((hop, core) + spread(coming, there))

    own = pl.ds(pl.multiple_of(pack * z.owned, 16), z.owned)
    loads[1].wait()
    s.weights[own, :] = s.master[...].astype(BF16)
    s.codes[: tok // 128, :] = s.ids[...]
    s.codes[tok // 128 :, :] = s.pad[...]
    greet(row_peers + [device for dim in ("y", "z") for _, device in near[dim]])
    loads[0].wait()
    for post in send_codes + send_x + [send_c]:
        post.start()

    def first_hop():
        for k in range(4):
            chain[k].start()
            for post in chain_y[k]:
                post.start()

    pl.when(at["z"] == 0)(first_hop)
    s.tokens_all[me] = s.tokens[...]
    s.codes_all[me] = s.codes[...]
    for post in send_codes:
        post.recv()

    groups = tok // 128
    high = z.pack_len // IMG_W
    ids, pad = s.codes_all[:, :groups, :], s.codes_all[:, groups:, :]
    index = (
        lax.broadcasted_iota(jnp.int32, ids.shape, 0) * tok
        + lax.broadcasted_iota(jnp.int32, ids.shape, 1) * 128
        + lax.broadcasted_iota(jnp.int32, ids.shape, 2)
    )
    starts = jnp.zeros(ids.shape, jnp.int32)
    for image in range(8):
        count = jnp.sum(jnp.where(ids == image, 1.0, 0.0)).astype(jnp.int32)
        starts = starts + jnp.where(ids > image, count, 0)
    places = index - starts
    on_y = lax.div(places, IMG_W)
    on_x = places - on_y * IMG_W

    def line(values, r):
        return jnp.concatenate([values[r, g : g + 1, :] for g in range(groups)], 1)

    def vector(first, count=lines):
        return jnp.concatenate([s.vec[first + i : first + i + 1, :] for i in range(count)], 1)

    loads[2].wait()

    def projections(pos_ref):
        for r in range(rows):
            sub = lax.broadcasted_iota(jnp.int32, (high, tok), 0)
            hot = jnp.concatenate(
                [
                    jnp.where(sub == line(on_y, r), 1.0, 0.0),
                    jnp.where(sub[:IMG_W] == line(on_x, r), 1.0, 0.0),
                ],
                0,
            ).astype(BF16)
            pos_ref[r] = dot(jnp.concatenate([hot] * 3, 0), s.table[...], TN)
        for k in range(4):

            def forward():
                chain[k].copy.wait_recv()
                chain[k].start()
                chain_c[k].copy.start()
                for post in chain_y[k]:
                    post.start()

            pl.when(inner)(forward)
        for post, relay in zip(send_x, relay_x):
            post.recv()
            relay.start()
        for k in range(4):
            for post, relay in zip(chain_y[k], chain_yc[k]):
                post.recv()
                relay.start()
        for post in [send_c] + relay_x + chain_c + [p for found in chain_yc for p in found]:
            post.recv()
        for post in own_y + [ups[0][0], downs[0][0]] if ups else own_y + [downs[0][0]]:
            post.start()
        pick = (
            lax.broadcasted_iota(jnp.int32, (width, part), 0)
            == lax.broadcasted_iota(jnp.int32, (width, part), 1) + me * part
        )
        pick = jnp.where(pick, 1.0, 0.0).astype(BF16)
        wq, wk, wv = [dot(blocks_of(s.weights, n * square, lines, lines, lines), pick).astype(BF16) for n in range(3)]

        def bias(first):
            row = jnp.broadcast_to(vector(first), (8, width))
            return pltpu.roll(row, lax.rem(width - me * part, width), 1)[:1, :part]

        bias_q, bias_v = bias(0), bias(lines)
        scale = LOG2E * head**-0.5
        sub8 = lax.broadcasted_iota(jnp.int32, (8, tok), 0)
        for r in range(rows):
            span = slice(r * tok, (r + 1) * tok)
            rows_in = s.tokens_all[r]
            placed = (rows_in + pos_ref[r]).astype(BF16)
            plain = rows_in.astype(BF16)
            s.placed[span, :] = placed
            s.plain[span, :] = plain
            q = (dot(placed, wq) + bias_q).astype(BF16)
            k = dot(placed, wk).astype(BF16)
            v = (dot(plain, wv) + bias_v).astype(BF16)
            s.q[span, :] = q
            qt, kt, vt = q.astype(F32).T, k.astype(F32).T, v.astype(F32).T
            s.kt[:, span] = kt.astype(BF16)
            s.vt[:, span] = vt.astype(BF16)
            scaled = qt * scale
            q_high = scaled.astype(BF16).astype(F32)
            q_low = scaled - q_high
            same = sub8 == line(ids, r)
            ones = jnp.ones((8, tok), F32)
            free = jnp.zeros((128 - 2 * head - 8, tok), F32)
            barred = jnp.where(same & (line(pad, r) == 0), 0.0, MASKED_SCORE)
            for h in range(heads):
                mine = slice(h * head, (h + 1) * head)
                s.qf[h, :, span] = jnp.concatenate(
                    [q_high[mine], q_low[mine], jnp.where(same, 1.0, 0.0), free], 0
                ).astype(BF16)
                s.kf[h, span, :] = jnp.concatenate([kt[mine], kt[mine], barred, ones, free[8:]], 0).T.astype(BF16)
                s.vf[h, span, :] = jnp.concatenate([vt[mine], vt[mine], ones, free], 0).T.astype(BF16)

    pl.run_scoped(projections, pltpu.VMEM((rows, tok, width), F32))

    att_posts = []
    for step in range(rows - 1):
        device = {"pack": pack, "row": lax.rem(me + 1 + step, rows)}
        att_posts.append(mail.make(s.att_post.at[step], s.att.at[me], device))

    def weight_stage(stage):
        if stage == 0:
            for post, core in zip(own_y, own_c):
                post.recv()
                core.start()
        for moves in (ups, downs):
            if 0 < stage <= len(moves):
                _, _, over_y, over_c = moves[stage - 1]
                for post, core in zip(over_y, over_c):
                    post.recv()
                    core.start()
            if stage < len(moves):
                hop, core, over_y, _ = moves[stage]
                hop.recv()
                if stage + 1 < len(moves):
                    moves[stage + 1][0].start()
                for post in [core] + over_y:
                    post.start()

    stages = nz
    wide_tile = 2 * TILE
    per = tok // wide_tile
    tiles = rows * per

    def attend_step(number, carry):
        step = lax.div(number, per)
        offset = lax.rem(number, per)
        dest = lax.rem(me + 1 + step, rows)
        span = pl.ds(pl.multiple_of(dest * tok + offset * wide_tile, wide_tile), wide_tile)
        for stage in range(stages - 1):
            pl.when(number == (stage + 1) * tiles // stages)(functools.partial(weight_stage, stage))
        pieces = []
        for h in range(heads):
            scores = dot(s.kf[h], s.qf[h, :, span])
            largest = jnp.max(scores, axis=0, keepdims=True)
            weights = jnp.exp2(scores - largest)
            total = jnp.sum(weights, axis=0, keepdims=True)
            out = dot(s.vt[h * head : (h + 1) * head, :], weights.astype(BF16))
            pieces.append(out * (1.0 / total))
            lse = -(largest + jnp.log2(total))
            lh = lse.astype(BF16).astype(F32)
            lm = (lse - lh).astype(BF16).astype(F32)
            tail = s.qf[h, 2 * head : 2 * head + 16, span].astype(F32)
            tail = jnp.concatenate([tail[:8], lh, lm, lse - lh - lm, jnp.zeros((5, wide_tile), F32)], 0)
            s.qf[h, 2 * head : 2 * head + 16, span] = tail.astype(BF16)
        out = pieces[0] if heads == 1 else jnp.concatenate(pieces, 0)
        s.ot[:, span] = out
        s.att_post[step, :, pl.ds(pl.multiple_of(offset * wide_tile, wide_tile), wide_tile)] = out.astype(BF16)
        for there in range(rows - 1):
            pl.when(number == (there + 1) * per - 1)(functools.partial(att_posts[there].start))
        return carry

    lax.fori_loop(0, tiles, attend_step, 0)
    weight_stage(stages - 1)
    s.att[me] = s.att_post[rows - 1]
    for post in att_posts:
        post.recv()
    for post in own_c + [p for moves in (ups, downs) for move in moves for p in [move[1]] + move[3]]:
        post.recv()

    dot_lanes = pl.ds(pl.multiple_of(me * tok, 128), tok)
    dot_posts = [mail.make(s.dot_post.at[d["row"]], s.dot.at[:, dot_lanes], d) for d in row_peers]
    loads[3].wait()

    def middle(act_ref, slope_ref):
        count = 4
        wide = hidden // count // 128

        def put_vector(first, value):
            for i in range(value.shape[1] // 128):
                s.vec_part[first + i : first + i + 1, :] = value[:, i * 128 : (i + 1) * 128]

        bias_out, gain_one, shift_one = vector(2 * lines), vector(3 * lines), vector(4 * lines)
        last = 5 * lines + hidden // 128
        bias_two, gain_two, shift_two = vector(last), vector(last + lines), vector(last + 2 * lines)

        def w_one(n):
            return blocks_of(s.weights, 4 * square + n * wide, lines, wide, hidden // 128)

        def w_two(n):
            first = 4 * square + lines * hidden // 128
            return blocks_of(s.weights, first + n * wide * lines, wide, lines, lines)

        def put_grad(first, stride, value):
            for i in range(value.shape[0] // 128):
                for j in range(value.shape[1] // 128):
                    row = (3 * square + first + i * stride + j) * 128
                    s.grad[row : row + 128, :] = value[i * 128 : (i + 1) * 128, j * 128 : (j + 1) * 128]

        attended_t = jnp.concatenate([s.att[r] for r in range(rows)], 0)
        w_out = blocks_of(s.weights, 3 * square, lines, lines, lines)
        branch = dot(attended_t, w_out, TN) + bias_out
        unit_one, scale_one = norm_forward(s.tokens[...] + branch)
        normed = unit_one * gain_one + shift_one
        normed_low = normed.astype(BF16)
        second = jnp.zeros((tok, width), F32)
        for n in range(count):
            pre = dot(normed_low, w_one(n)) + vector(5 * lines + n * wide, wide)
            square_pre = pre * pre
            curve = jnp.tanh(0.7978845608028654 * pre * (1.0 + 0.044715 * square_pre))
            half_one = 0.5 * (1.0 + curve)
            act = (pre * half_one).astype(BF16)
            slope_ref[n] = half_one + 0.5 * pre * (1.0 - curve * curve) * (
                0.7978845608028654 * (1.0 + 0.134145 * square_pre)
            )
            act_ref[n] = act
            second = second + dot(act, w_two(n))
        unit_two, scale_two = norm_forward(normed + (second + bias_two))
        s.layer[...] = unit_two * gain_two + shift_two
        cot = s.cot[...]
        put_vector(last + lines, column_sum(cot * unit_two))
        put_vector(last + 2 * lines, column_sum(cot))
        sum_grad = norm_backward(cot, gain_two, unit_two, scale_two)
        second_grad = sum_grad.astype(BF16)
        put_vector(last, column_sum(second_grad.astype(F32)))
        normed_grad = sum_grad
        for n in range(count):
            two = w_two(n)
            hidden_grad = (dot(second_grad, two, NT) * slope_ref[n]).astype(BF16)
            put_vector(5 * lines + n * wide, column_sum(hidden_grad.astype(F32)))
            normed_grad = normed_grad + dot(hidden_grad, w_one(n), NT)
            first = lines * hidden // 128 + square + n * wide * lines
            put_grad(first, lines, dot(act_ref[n], second_grad, TN))
            put_grad(square + n * wide, hidden // 128, dot(normed_low, hidden_grad, TN))
        put_vector(3 * lines, column_sum(normed_grad * unit_one))
        put_vector(4 * lines, column_sum(normed_grad))
        branch_grad = norm_backward(normed_grad, gain_one, unit_one, scale_one)
        s.branch[...] = branch_grad
        branch_low = branch_grad.astype(BF16)
        grad_t = dot(w_out, branch_low, NT).astype(BF16)
        for r in range(rows):
            s.dot_post[r] = grad_t[r * part : (r + 1) * part, :]
        for post in dot_posts:
            post.start()
        s.dot[:, dot_lanes] = s.dot_post[me]
        put_vector(2 * lines, column_sum(branch_low.astype(F32)))
        put_grad(0, lines, dot(attended_t, branch_low))

    pl.run_scoped(middle, pltpu.VMEM((4, tok, hidden // 4), BF16), pltpu.VMEM((4, tok, hidden // 4), F32))

    store(s.layer, s.layer_out)

    chunks, size, share = z.chunks, z.size, z.share
    s.grad[: 3 * square * 128, :] = jnp.zeros((3 * square * 128, 128), F32)

    def grad_rows(chunk, x, c, y, z):
        row = (z * ny + y) * (rows * share) + (x * 2 + c) * share + chunk * size
        return s.grad[pl.ds(pl.multiple_of(row, 16), size), :]

    def order(chunk):
        return ("x", "y") if chunk % 2 == 0 else ("y", "x")

    def spot(chunk, one, two, zz):
        return {order(chunk)[0]: one, order(chunk)[1]: two, "z": zz}

    hops0, hops1, hops2, hops3, hops4 = [], [], [], [], []
    for chunk in range(chunks):
        n2 = place.size[order(chunk)[1]]
        hops0.append(mail.make(s.stage0.at[chunk], s.recv0.at[chunk], partner[1]))
        made = []
        for step, (_, device) in enumerate(near[order(chunk)[0]]):
            span = pl.ds(step * n2 * nz, n2 * nz)
            made.append(mail.make(s.stage1.at[chunk, span], s.recv1.at[chunk, span], device))
        hops1.append(made)
        made = []
        for step, (_, device) in enumerate(near[order(chunk)[1]]):
            span = pl.ds(step * nz, nz)
            made.append(mail.make(s.stage2.at[chunk, span], s.recv2.at[chunk, span], device))
        hops2.append(made)
        hops3.append(
            [mail.make(s.stage3.at[chunk, step], s.recv3.at[chunk, step], d) for step, (_, d) in enumerate(near["z"])]
        )
        mine = pl.ds(pl.multiple_of(me * share + chunk * size, 16), size)
        hops4.append([mail.make(s.owned.at[mine], s.owned.at[mine], device) for device in row_peers])

    def reduce_cores():
        for chunk in range(chunks):
            n1, n2 = [place.size[d] for d in order(chunk)]
            for one in range(n1):
                for two in range(n2):
                    for zz in range(nz):
                        rows_of = grad_rows(chunk, c=partner[0], **spot(chunk, one, two, zz))
                        s.stage0[chunk, (one * n2 + two) * nz + zz] = rows_of.astype(BF16)
            hops0[chunk].start()

    def reduce_first():
        for chunk in range(chunks):
            n1, n2 = [place.size[d] for d in order(chunk)]
            hops0[chunk].recv()

            def summed(one, two, zz):
                slot = (one * n2 + two) * nz + zz
                rows_of = grad_rows(chunk, c=at["c"], **spot(chunk, one, two, zz))
                return rows_of + s.recv0[chunk, slot].astype(F32)

            for step, (there, _) in enumerate(near[order(chunk)[0]]):
                for two in range(n2):
                    for zz in range(nz):
                        s.stage1[chunk, step * n2 * nz + two * nz + zz] = summed(there, two, zz).astype(BF16)
                hops1[chunk][step].start()
            for two in range(n2):
                for zz in range(nz):
                    s.kept1[chunk, two * nz + zz] = summed(at[order(chunk)[0]], two, zz)

    def reduce_second():
        for chunk in range(chunks):
            n1, n2 = [place.size[d] for d in order(chunk)]
            for hop in hops1[chunk]:
                hop.recv()

            def summed(two, zz):
                total = s.kept1[chunk, two * nz + zz]
                for step in range(n1 - 1):
                    total = total + s.recv1[chunk, step * n2 * nz + two * nz + zz].astype(F32)
                return total

            for step, (there, _) in enumerate(near[order(chunk)[1]]):
                for zz in range(nz):
                    s.stage2[chunk, step * nz + zz] = summed(there, zz).astype(BF16)
                hops2[chunk][step].start()
            for zz in range(nz):
                s.kept2[chunk, zz] = summed(at[order(chunk)[1]], zz)

    def reduce_third():
        for chunk in range(chunks):
            n2 = place.size[order(chunk)[1]]
            for hop in hops2[chunk]:
                hop.recv()

            def summed(zz):
                total = s.kept2[chunk, zz]
                for step in range(n2 - 1):
                    total = total + s.recv2[chunk, step * nz + zz].astype(F32)
                return total

            for step, (there, _) in enumerate(near["z"]):
                s.stage3[chunk, step] = summed(there).astype(BF16)
                hops3[chunk][step].start()
            s.kept2[chunk, at["z"]] = summed(at["z"])

    def reduce_last():
        for chunk in range(chunks):
            total = s.kept2[chunk, at["z"]]
            for step, hop in enumerate(hops3[chunk]):
                hop.recv()
                total = total + s.recv3[chunk, step].astype(F32)
            mine = pl.ds(pl.multiple_of(me * share + chunk * size, 16), size)
            s.owned[mine, :] = total.astype(BF16)
            for hop in hops4[chunk]:
                hop.start()

    reduce_stages = ((0, reduce_first), (3, reduce_second), (6, reduce_third))
    reduce_cores()
    for post in dot_posts:
        post.recv()

    scale = head**-0.5
    posts = [mail.make(s.post.at[d["row"]], s.got.at[me], d) for d in row_peers]

    def backward(df_ref, mix_ref, both_ref, pair_ref, qt_ref):
        lane = lax.broadcasted_iota(jnp.int32, (tok, part), 1)
        for r in range(rows):
            span = slice(r * tok, (r + 1) * tok)
            grad_t = s.dot[:, span].astype(F32)
            center = grad_t * s.ot[:, span]
            grad_rows_in = grad_t.T
            queries = s.q[span, :].astype(F32)
            scaled = grad_t * scale
            g_high = scaled.astype(BF16).astype(F32)
            g_low = scaled - g_high
            for h in range(heads):
                own_lines = slice(h * head, (h + 1) * head)
                shift = -scale * column_sum(center[own_lines])
                sh = shift.astype(BF16).astype(F32)
                sm = (shift - sh).astype(BF16).astype(F32)
                rest = jnp.zeros((128 - 2 * head - 3, tok), F32)
                df_ref[h, :, span] = jnp.concatenate(
                    [g_high[own_lines], g_low[own_lines], sh, sm, shift - sh - sm, rest], 0
                ).astype(BF16)
                mine = (lane >= h * head) & (lane < (h + 1) * head)
                none = jnp.zeros((tok, part), F32)
                free = [jnp.zeros((tok, 128 - 2 * part), F32)] if part < 64 else []
                mix_ref[2 * h, span, :] = jnp.concatenate(
                    [jnp.where(mine, grad_rows_in, 0.0), none] + free, 1
                ).astype(BF16)
                mix_ref[2 * h + 1, span, :] = jnp.concatenate(
                    [none, jnp.where(mine, queries, 0.0)] + free, 1
                ).astype(BF16)
        pair_ref[...] = jnp.zeros_like(pair_ref)
        turns = z.pack_len // TILE

        def tile_step(number, carry):
            span = pl.ds(pl.multiple_of(number * TILE, TILE), TILE)
            for eighth, action in reduce_stages:
                pl.when(number == eighth * turns // 8)(action)
            pieces, mix = [], []
            for h in range(heads):
                probs = jnp.exp2(dot(s.kf[h], s.qf[h, :, span]))
                along = dot(s.vf[h], df_ref[h, :, span])
                both_ref[:, 2 * h * TILE : (2 * h + 1) * TILE] = probs.astype(BF16)
                score_grad = (probs * along).astype(BF16)
                both_ref[:, (2 * h + 1) * TILE : (2 * h + 2) * TILE] = score_grad
                pieces.append(dot(s.kt[h * head : (h + 1) * head, :], score_grad))
                mix += [mix_ref[2 * h, span, :], mix_ref[2 * h + 1, span, :]]
            qt_ref[:, span] = pieces[0] if heads == 1 else jnp.concatenate(pieces, 0)
            pair_ref[...] += dot(both_ref[...], jnp.concatenate(mix, 0))
            return carry

        lax.fori_loop(0, turns, tile_step, 0)
        for r in range(rows):
            span = slice(r * tok, (r + 1) * tok)
            pair = pair_ref[span, :].T
            s.post[r] = jnp.concatenate([qt_ref[:, span], pair[part : 2 * part], pair[:part]], 0).astype(BF16)

    pl.run_scoped(
        backward,
        pltpu.VMEM((heads, 128, z.pack_len), BF16),
        pltpu.VMEM((2 * heads, z.pack_len, 128), BF16),
        pltpu.VMEM((z.pack_len, 2 * heads * TILE), BF16),
        pltpu.VMEM((z.pack_len, 128), F32),
        pltpu.VMEM((part, z.pack_len), F32),
    )

    joint, owners = z.joint, z.owners
    size_l = z.late // joint
    for kind, first, last in (("placed", 0, 2 * part), ("plain", 2 * part, 3 * part)):
        base = getattr(s, kind)
        total = jnp.zeros((last - first, width), F32)
        for r in range(rows):
            total = total + dot(s.post[r, first:last, :], base[r * tok : (r + 1) * tok, :])
        for i in range(lines):
            row = i * 3 * part + first
            s.late[row : row + last - first, :] = total[:, i * 128 : (i + 1) * 128]
    s.late_post[...] = s.late[...].astype(BF16)
    spread_posts = []
    joined = None if joint == z.packs else pack < joint
    for step in range(1, z.packs):
        there = lax.rem(pack + step, z.packs)
        lands = None if joint == z.packs else there < joint
        rows_of = pl.ds(pl.multiple_of(lax.rem(there, joint) * size_l, 16), size_l)
        spread_posts.append(
            mail.put(
                s.late_post.at[rows_of, :], s.late_recv.at[step - 1], {"pack": there, "row": me}, lands, joined
            )
        )

    ones = jnp.ones((16, tok), BF16)
    sums = jnp.zeros((16, 3 * part), F32)
    for r in range(rows):
        sums = sums + dot(ones, s.post[r], NT)
    for n in (0, 2):
        row = jnp.concatenate([sums[:8, n * part : (n + 1) * part], jnp.zeros((8, width - part), F32)], 1)
        row = pltpu.roll(row, me * part, 1)
        for i in range(lines):
            line_of = (n // 2) * lines + i
            s.vec_part[line_of : line_of + 1, :] = row[:1, i * 128 : (i + 1) * 128]

    def vec_step(dim, buffer, value):
        buffer[at[dim]] = value
        return [mail.put(buffer.at[at[dim]], buffer.at[at[dim]], device) for _, device in place.peers(dim)]

    def vec_sum(hops, buffer):
        for hop in hops:
            hop.recv()
        total = buffer[0]
        for number in range(1, buffer.shape[0]):
            total = total + buffer[number]
        return total

    vec_hops = vec_step("c", s.vec_c, s.vec_part[...])
    reduce_last()
    own_late = pl.ds(pl.multiple_of(lax.rem(pack, joint) * size_l, 16), size_l)
    for post in spread_posts:
        post.recv()
    total = s.late[own_late, :]
    for step in range(z.packs - 1):
        total = total + s.late_recv[step].astype(F32)
    s.late_share[...] = total.astype(BF16)
    s.late_all[me, own_late, :] = total.astype(BF16)
    for owner in range(owners):
        for step in range(rows):
            leaves = either([pack == giver for giver in sorted(z.givers[owner]) if step or giver != owner])
            mail.put(
                s.late_share, s.late_all.at[me, own_late, :],
                {"pack": pack * 0 + owner, "row": lax.rem(me + step, rows)}, leaves, None,
                late_sem.at[lax.rem(pack, joint), step],
            )
    vec_hops = vec_step("x", s.vec_x, vec_sum(vec_hops, s.vec_c))
    for post in posts:
        post.start()
    s.got[me] = s.post[me]
    for load in loads[4:]:
        load.wait()
    for chunk in range(chunks):
        for hop in hops4[chunk]:
            hop.recv()
            hop.sent()

    def late_wait():
        for giver in range(joint):
            for step in range(rows):

                def wait():
                    pltpu.make_async_remote_copy(
                        src_ref=s.late_share, dst_ref=s.late_all.at[0, :size_l, :],
                        send_sem=send_sem.at[0], recv_sem=late_sem.at[giver, step],
                        device_id={"pack": pack, "row": lax.rem(me + 1, rows)}, device_id_type=MESH,
                    ).wait_recv()

                takers = [n for n in range(owners) if giver in z.givers[n] and (step or n != giver)]
                if takers:
                    pl.when(either([pack == n for n in takers]))(wait)
        for b in range(3 * square):
            kind, i, j = b // square, b % square // lines, b % lines

            def place_block():
                start = (i * 3 + kind) * part
                found = [s.late_all[r, start : start + part, :] for r in range(j * 128 // part, (j + 1) * 128 // part)]
                block = jnp.concatenate(found, 0).astype(F32).T
                row = b % z.blocks * 128
                s.owned[row : row + 128, :] = block.astype(BF16)

            pl.when(pack == b // z.blocks)(place_block)

    pl.when(pack < owners)(late_wait)
    vec_hops = vec_step("y", s.vec_y, vec_sum(vec_hops, s.vec_x))
    blocks, slots = z.blocks, z.slots
    for n in range(slots):
        t = jnp.minimum(me * slots + n, 2 * blocks - 1)
        is_right = t >= blocks
        rows_of = pl.ds(pl.multiple_of(jnp.where(is_right, t - blocks, t) * 128, 128), 128)
        g = s.owned[rows_of, :].astype(F32)
        g = jnp.where(is_right, g.T, g).astype(BF16)
        stat = jnp.where(is_right, s.right[rows_of, :], s.left[rows_of, :])
        basis = jnp.where(is_right, s.rbasis[rows_of, :], s.lbasis[rows_of, :])
        new = BETA_TWO * stat + (1.0 - BETA_TWO) * dot(g, g, NT)
        a = dot6(new, basis)
        a_t = a.T
        s.gram[n, :, :128] = dot6(a_t, a)
        s.gram[n, :, 128:] = a_t
    def block_step(number, carry):
        rows_of = pl.ds(pl.multiple_of(number * 128, 128), 128)
        g = s.owned[rows_of, :]
        s.left_new[rows_of, :] = BETA_TWO * s.left[rows_of, :] + (1.0 - BETA_TWO) * dot(g, g, NT)
        s.right_new[rows_of, :] = BETA_TWO * s.right[rows_of, :] + (1.0 - BETA_TWO) * dot(g, g, TN)
        lb, rb = s.lbasis[rows_of, :], s.rbasis[rows_of, :]
        lh, ll = split2(lb)
        turned = dot(jnp.concatenate([lh, ll], 0), jnp.concatenate([g, g], 0), TN)
        rotated = dot3(turned, rb)
        first = BETA_ONE * s.first[rows_of, :] + (1.0 - BETA_ONE) * rotated
        second = BETA_TWO * s.second[rows_of, :] + (1.0 - BETA_TWO) * rotated * rotated
        s.first_new[rows_of, :] = first
        s.second_new[rows_of, :] = second
        ratio = first / (1.0 - BETA_ONE**STEP) / (jnp.sqrt(second / (1.0 - BETA_TWO**STEP)) + EPSILON)
        stepped = dot3(dot3(lb, ratio), rb, NT)
        weights = s.master[rows_of, :]
        weights = weights - LEARN_RATE * (stepped + WEIGHT_DECAY * weights)
        s.master_new[rows_of, :] = weights
        s.copy_new[rows_of, :] = weights.astype(BF16)
        return carry

    targets = [partner[1]] + [device for _, device in near["x"]]
    panel_first = mail.reserve(8 * len(targets))

    def panel_post(index, number):
        rows_of = pl.ds(pl.multiple_of(index * 16, 16), 16)
        place_in = s.turned.at[me, :, rows_of, :]
        sem = panel_first + number * 8 + index
        return pltpu.make_async_remote_copy(
            src_ref=place_in, dst_ref=place_in, send_sem=send_sem.at[sem], recv_sem=recv_sem.at[sem],
            device_id=targets[number], device_id_type=MESH,
        )

    def panel(index, carry):
        block_step(jnp.minimum(index, blocks - 1), 0)
        panel_step(pl.multiple_of(index * 16, 16), s.gram, s.turned.at[me], slots)
        for number in range(len(targets)):
            panel_post(index, number).start()
        return carry

    lax.fori_loop(0, 8, panel, 0)
    vec_hops = vec_step("z", s.vec_z, vec_sum(vec_hops, s.vec_y))
    lax.fori_loop(8, max(blocks, 8), block_step, 0)
    for name in ("first", "second", "master", "copy", "left", "right"):
        store(getattr(s, name + "_new"), getattr(s, name + "_out"))

    def turn(row):
        for n in range(slots):
            t = row * slots + n

            @pl.when(t < 2 * blocks)
            def _():
                s.bases[pl.ds(pl.multiple_of(t * 128, 128), 128), :] = s.turned[row, n].T

    turn(me)
    relays = []
    for step in range(nx - 1):
        for index in range(8):
            panel_post(index, 1 + step).wait_recv()
        row = source("x", step) * 2 + at["c"]
        relays.append(mail.put(s.turned.at[row], s.turned.at[row], partner[1]))
    for index in range(8):
        panel_post(index, 0).wait_recv()
    turn(lax.div(me, 2) * 2 + partner[0])
    for step in range(nx - 1):
        turn(source("x", step) * 2 + at["c"])
    for post in posts:
        post.recv()
    total = s.branch[...]
    for n in range(3):
        grad_t = jnp.concatenate([s.got[r, n * part : (n + 1) * part, :] for r in range(rows)], 0)
        weight = blocks_of(s.weights, n * square, lines, lines, lines)
        total = total + dot(grad_t, weight, (((0,), (1,)), ((), ())))
    s.input[...] = total
    store(s.input, s.input_out)
    grad = vec_sum(vec_hops, s.vec_z)
    first = BETA_ONE * s.vec_first[...] + (1.0 - BETA_ONE) * grad
    second = BETA_TWO * s.vec_second[...] + (1.0 - BETA_TWO) * grad * grad
    ratio = first / (1.0 - BETA_ONE**STEP) / (jnp.sqrt(second / (1.0 - BETA_TWO**STEP)) + EPSILON)
    s.vec_new[0] = s.vec[...] - LEARN_RATE * ratio
    s.vec_new[1] = first
    s.vec_new[2] = second
    for number, name in enumerate(("vec", "vec_first", "vec_second")):
        store(s.vec_new.at[number], getattr(s, name + "_out"))
    for step, relay in enumerate(relays):
        relay.recv()
        turn(source("x", step) * 2 + partner[0])
    store(s.bases.at[: z.owned, :], s.lbasis_out)
    store(s.bases.at[z.owned : 2 * z.owned, :], s.rbasis_out)
    for copy in stores:
        copy.wait()
    for index in range(8):
        for number in range(len(targets)):
            panel_post(index, number).wait_send()
    mail.finish(z.posts)


def finish_kernel(count, *refs):
    sems = refs[-1]
    loads = [pltpu.make_async_copy(refs[i], refs[2 * count + i], sems.at[i]) for i in range(count)]
    stores = [pltpu.make_async_copy(refs[2 * count + i], refs[count + i], sems.at[count + i]) for i in range(count)]
    for load in loads:
        load.start()
    for load, copy in zip(loads, stores):
        load.wait()
        copy.start()
    for copy in stores:
        copy.wait()


def shards(
    tokens, cotangent, segment_ids, padding, master, moment_first, moment_second,
    stat_left, stat_right, basis_left, basis_right, vec_params, vec_first, vec_second,
):
    packs, rows = lax.axis_size("pack"), lax.axis_size("row")
    tok, width = tokens.shape
    z = Sizes(packs, rows, tok, width, vec_params.shape[0] - 8 * width, master.shape[0])
    table = jnp.asarray(sine_rows(z.pack_len, width // 2))
    full = jax.ShapeDtypeStruct(master.shape, F32)
    layer = jax.ShapeDtypeStruct(tokens.shape, F32)
    shapes = (layer, layer, full, full, full, jax.ShapeDtypeStruct(master.shape, BF16), full, full, full, full)
    shapes = shapes + (jax.ShapeDtypeStruct((32, 128), F32),) * 3
    scratch = vmem_scratch(z)
    vm, hbm = pl.BlockSpec(memory_space=pltpu.VMEM), pl.BlockSpec(memory_space=pl.ANY)
    outs = pl.pallas_call(
        functools.partial(layer_kernel, z, tuple(scratch)),
        out_shape=shapes,
        in_specs=[vm] * 5 + [hbm] * 10,
        out_specs=(hbm,) * len(shapes),
        scratch_shapes=list(scratch.values())
        + [
            pltpu.SemaphoreType.DMA((z.posts,)),
            pltpu.SemaphoreType.DMA((z.posts,)),
            pltpu.SemaphoreType.DMA((len(LOADS) + len(shapes),)),
            pltpu.SemaphoreType.DMA((packs, rows)),
        ],
        compiler_params=pltpu.CompilerParams(collective_id=1, has_side_effects=True, vmem_limit_bytes=63 << 20),
        name="layer",
    )(
        segment_ids.reshape(-1, 128), padding.reshape(-1, 128), vec_params.reshape(32, 128),
        vec_first.reshape(32, 128), vec_second.reshape(32, 128), tokens, master, table,
        cotangent, moment_first, moment_second, stat_left, stat_right, basis_left, basis_right,
    )
    outs = pl.pallas_call(
        functools.partial(finish_kernel, len(shapes)),
        out_shape=shapes,
        in_specs=[hbm] * len(shapes),
        out_specs=(hbm,) * len(shapes),
        scratch_shapes=[pltpu.VMEM(shape.shape, shape.dtype) for shape in shapes]
        + [pltpu.SemaphoreType.DMA((2 * len(shapes),))],
        compiler_params=pltpu.CompilerParams(vmem_limit_bytes=63 << 20),
        name="finish",
    )(*outs)
    return outs[:-3] + tuple(out.reshape(-1) for out in outs[-3:])


def solution(mesh):
    placed = (
        P(("pack", "row"), None),
        P(("pack", "row"), None),
        P(("pack", "row")),
        P(("pack", "row")),
        P("pack", None),
        P("pack", None),
        P("pack", None),
        P("pack", None),
        P("pack", None),
        P("pack", None),
        P("pack", None),
        P(),
        P(),
        P(),
    )
    return jax.shard_map(
        shards,
        mesh=mesh,
        in_specs=placed,
        out_specs=(
            P(("pack", "row"), None),
            P(("pack", "row"), None),
            P("pack", None),
            P("pack", None),
            P("pack", None),
            P("pack", None),
            P("pack", None),
            P("pack", None),
            P("pack", None),
            P("pack", None),
            P(),
            P(),
            P(),
        ),
        check_vma=False,
    )
```
